128 devices in a mesh: span: 64 (over z, x, y_hi, core), head: 2 (over y_lo).
Axes of the slice: x: 4, y: 4 (y_hi: 2, y_lo: 2; y = y_hi * 2 + y_lo), z: 4, core: 2. Of those that a mesh axis runs over, the one named last changes fastest.
Arguments:
- tokens: bfloat16 [16384, 1536], P(('span', 'head')), may hold values from -6 to 6
- doc_starts: int32 [8], replicated, may hold values from 0 to 16383, as said below
- norm_gain: bfloat16 [2, 1536], P(None, ('span', 'head')), may hold values from 0.5 to 1.5
- in_weight: bfloat16 [2, 1536, 6448], P(None, ('span', 'head')), may hold values from -0.15625 to 0.15625
- conv_weight: bfloat16 [2, 4, 3328], P(None, None, ('span', 'head')), may hold values from -3 to 3
- conv_bias: bfloat16 [2, 3328], P(None, ('span', 'head')), may hold values from -1.5 to 1.5
- step_bias: float32 [2, 48], P(None, 'head')
- decay_log: float32 [2, 48], P(None, 'head')
- skip_gain: float32 [2, 48], P(None, 'head'), may hold values from 0.5 to 1.5
- gate_gain: bfloat16 [2, 3072], P(None, ('span', 'head')), may hold values from 0.5 to 1.5
- out_weight: bfloat16 [2, 3072, 1536], P(None, ('span', 'head')), may hold values from -0.109375 to 0.109375
- cotangent: bfloat16 [16384, 1536], P(('span', 'head')), may hold values from -6 to 6
Outputs:
- output: bfloat16 [16384, 1536], P(('span', 'head'))
- tokens_grad: float32 [16384, 1536], P(('span', 'head'))
- norm_gain_grad: float32 [2, 1536], P(None, ('span', 'head'))
- in_weight_grad: float32 [2, 1536, 6448], P(None, ('span', 'head'))
- conv_weight_grad: float32 [2, 4, 3328], P(None, None, ('span', 'head'))
- conv_bias_grad: float32 [2, 3328], P(None, ('span', 'head'))
- step_bias_grad: float32 [2, 48], P(None, 'head')
- decay_log_grad: float32 [2, 48], P(None, 'head')
- skip_gain_grad: float32 [2, 48], P(None, 'head')
- gate_gain_grad: float32 [2, 3072], P(None, ('span', 'head'))
- out_weight_grad: float32 [2, 3072, 1536], P(None, ('span', 'head'))
The draws below stay inside these ranges and needn't reach their ends.
Inputs may be any that keep to these rules, and one draw needn't show every extreme that they name: `doc_starts`: strictly increasing; the first is 0.
All inputs are finite; a program needn't handle non-finite values.
Results may differ from the reference program's by a relative error of at most 0.03.
Values may be sent and summed in bfloat16 or wider, within the bound.
No kernel may reach another device: no remote copies, remote signals or barrier semaphores. Data moves between devices by JAX's collectives and lax.ppermute only.
A program may use at most 896 MiB of HBM per device.

```python
import math
from functools import partial
import jax
import jax.numpy as jnp
from jax import lax

D = 1536
DI = 3072
H = 48
HP = 64
N = 128
CONV = 4
LAYERS = 2
DOCS = 8
TOK_DEV = 128
SPAN_TOK = 256
TOKENS = 16384
CH = 3328
PROJ = 6448
N_SPAN = 64


def head_kind(key):
    return jax.random.uniform(key, (LAYERS, H), jnp.float32)


def draw_step_bias(key, part):
    head_kinds = head_kind(key)
    key = jax.random.fold_in(key, 21)
    fast_share = 0.5
    fast_bias = jax.random.uniform(key, (LAYERS, H), jnp.float32, -4.0, -3.0)
    slow_bias = jax.random.uniform(jax.random.fold_in(key, 1), (LAYERS, H), jnp.float32, -10.0, -9.0)
    return jnp.where(head_kinds < fast_share, fast_bias, slow_bias)


def draw_decay_log(key, part):
    head_kinds = head_kind(key)
    key = jax.random.fold_in(key, 22)
    fast_share = 0.5
    fast_log = jax.random.uniform(key, (LAYERS, H), jnp.float32, -0.5, 0.5)
    slow_rate = jax.random.uniform(jax.random.fold_in(key, 1), (LAYERS, H), jnp.float32, 0.5, 1.5)
    slow_log = jnp.log(slow_rate) - math.log(TOKENS * 0.00012)
    return jnp.where(head_kinds < fast_share, fast_log, slow_log)


def draw_doc_starts(key, part):
    key = jax.random.fold_in(key, 23)
    first_key = jax.random.fold_in(key, 1)
    last_key = jax.random.fold_in(key, 2)
    early_starts = jnp.sort(jax.random.permutation(first_key, TOK_DEV - 1)[:3]) + 1
    late_starts = jnp.sort(jax.random.permutation(last_key, TOK_DEV - 1)[:DOCS - 4]) + (TOKENS - TOK_DEV + 1)
    return jnp.concatenate([jnp.zeros((1,), jnp.int32), early_starts.astype(jnp.int32), late_starts.astype(jnp.int32)])


def shard_levels(own_key, extent, cuts, least, largest):
    loudness = 1.0
    for dim, shards_of in cuts:
        steps = jax.random.uniform(jax.random.fold_in(jax.random.fold_in(own_key, 6), dim), (shards_of,), jnp.float32, least / len(cuts), largest / len(cuts))
        loudness = loudness * jnp.repeat(jnp.exp(steps), extent[dim] // shards_of).reshape((-1,) + (1,) * (len(extent) - 1 - dim))
    return loudness


def centred(stream_key, extent, scale, bound, split=(), kind=jnp.bfloat16):
    loudness = shard_levels(stream_key, extent, split, -0.22, 0.18) if split else 1.0
    values = jax.random.normal(stream_key, extent, jnp.float32) * scale * loudness
    return jnp.minimum(jnp.maximum(values, -bound), bound).astype(kind)


def setup_inputs(seed: int = 0) -> dict:
    key_list = jax.random.split(jax.random.key(seed), 13)
    tokens = centred(key_list[0], (TOKENS, D), 1.0, 6.0, ((0, 128),))
    doc_starts = draw_doc_starts(jax.random.fold_in(key_list[12], 71), 0)
    norm_gain = jnp.clip(1.0 + 0.1 * jax.random.normal(key_list[2], (LAYERS, D), jnp.float32), 0.5, 1.5).astype(jnp.bfloat16)
    in_weight = centred(key_list[3], (LAYERS, D, PROJ), D ** -0.5, 0.15625, ((1, 128),))
    conv_weight = centred(key_list[4], (LAYERS, CONV, CH), CONV ** -0.5, 3.0, ((2, 128),))
    conv_bias = centred(key_list[5], (LAYERS, CH), 0.3, 1.5, ((1, 128),))
    step_bias = draw_step_bias(jax.random.fold_in(key_list[12], 71), 0)
    decay_log = draw_decay_log(jax.random.fold_in(key_list[12], 71), 0)
    skip_gain = jnp.clip(0.5 + 1.0 * jax.random.uniform(key_list[8], (LAYERS, H), jnp.float32) ** shard_levels(key_list[8], (LAYERS, H), ((1, 2),), -0.2, 0.2), 0.5, 1.5)
    gate_gain = jnp.clip(1.0 + 0.1 * jax.random.normal(key_list[9], (LAYERS, DI), jnp.float32), 0.5, 1.5).astype(jnp.bfloat16)
    out_weight = centred(key_list[10], (LAYERS, DI, D), DI ** -0.5, 0.109375, ((1, 128),))
    cotangent = centred(key_list[11], (TOKENS, D), 1.0, 6.0, ((0, 128),))
    return {"tokens": tokens, "doc_starts": doc_starts, "norm_gain": norm_gain, "in_weight": in_weight, "conv_weight": conv_weight, "conv_bias": conv_bias, "step_bias": step_bias, "decay_log": decay_log, "skip_gain": skip_gain, "gate_gain": gate_gain, "out_weight": out_weight, "cotangent": cotangent}


highest = lax.Precision.HIGHEST
epsilon = 1e-05

@jax.custom_vjp
def low(v):
    return lax.optimization_barrier(v.astype(jnp.bfloat16)).astype(jnp.float32)

@jax.custom_vjp
def low_back(v):
    return v

def low_keep(v):
    return (low(v), None)

def low_pass(kept, grad):
    return (grad,)

def back_keep(v):
    return (v, None)

def back_low(kept, grad):
    return (low(grad),)
low.defvjp(low_keep, low_pass)
low_back.defvjp(back_keep, back_low)

def rms_gain(hidden, gain):
    mean_square = lax.optimization_barrier(jnp.mean(hidden * hidden, axis=-1, keepdims=True))
    return hidden * lax.rsqrt(mean_square + epsilon) * gain

def segment_ids(doc_starts, positions):
    return lax.optimization_barrier(jnp.sum((doc_starts[None, :] <= positions[:, None]).astype(jnp.int32), axis=1)) - 1

def causal_conv(inputs, segment, conv_weight, conv_bias):
    length = inputs.shape[0]
    summed = jnp.zeros_like(inputs) + conv_bias[None, :]
    for offset in range(CONV):
        shifted = jnp.concatenate([jnp.zeros((offset, inputs.shape[1]), inputs.dtype), inputs[:length - offset]], axis=0)
        shifted_seg = jnp.concatenate([jnp.full((offset,), -1, jnp.int32), segment[:length - offset]]).astype(jnp.int32)
        same_doc = (shifted_seg == segment).astype(inputs.dtype)
        summed = summed + conv_weight[offset][None, :] * shifted * same_doc[:, None]
    return jax.nn.silu(summed)

def span_factors(step_raw, step_bias, decay_log, segment, seg_before):
    step_size = jax.nn.softplus(step_raw + step_bias[None, :])
    running = jnp.cumsum(-jnp.exp(decay_log)[None, :] * step_size, axis=0)
    run_heads = running.T
    length = segment.shape[0]
    order = jnp.arange(length)
    intra_mask = (order[None, :] <= order[:, None]) & (segment[None, :] == segment[:, None])
    mask_float = intra_mask.astype(running.dtype)
    spread = run_heads[:, :, None] - run_heads[:, None, :]
    decay_matrix = jnp.exp(jnp.where(intra_mask[None], spread, 0.0)) * mask_float[None] * step_size.T[:, None, :]
    inflow = jnp.exp(running) * (segment == seg_before).astype(running.dtype)[:, None]
    weights = jnp.exp(running[-1][None, :] - running) * step_size * (segment == segment[-1]).astype(running.dtype)[:, None]
    span_decay = jnp.exp(running[-1]) * (segment[-1] == seg_before).astype(running.dtype)
    return (decay_matrix, inflow, weights, span_decay)

def span_mix(head_params, carried_in, pieces):
    step_bias, decay_log, skip_gain = head_params
    x_full, x_low, b_low, c_low, step_raw, segment, seg_before = pieces
    decay_matrix, inflow, weights, span_decay = span_factors(step_raw, step_bias, decay_log, segment, seg_before)
    gram_matrix = low_back(jnp.dot(c_low, b_low.T, precision=highest))
    mixing = low(gram_matrix[None] * decay_matrix)
    within = jnp.einsum('hts,shp->thp', mixing, x_low, precision=highest)
    reading = jnp.einsum('hpn,tn->thp', carried_in, c_low, precision=highest)
    mixed_out = within + inflow[:, :, None] * reading + skip_gain[None, :, None] * x_full
    weighted = low(weights[:, :, None] * x_full)
    own_state = jnp.einsum('shp,sn->hpn', weighted, b_low, precision=highest)
    return (span_decay[:, None, None] * carried_in + own_state, mixed_out)

def by_span(array):
    return array.reshape((N_SPAN, SPAN_TOK) + array.shape[1:])

def layer_forward(hidden, params, segment, seg_before):
    norm_gain, in_weight, conv_weight, conv_bias, step_bias, decay_log, skip_gain, gate_gain, out_weight = params
    normed = low(rms_gain(hidden, norm_gain))
    project = low_back(jnp.dot(normed, in_weight, precision=highest))
    gate_part = project[:, :DI]
    x_in = low(project[:, DI:2 * DI])
    bc_in = low(project[:, 2 * DI:2 * DI + 2 * N])
    step_raw = low(project[:, 2 * DI + 2 * N:])
    conv_out = causal_conv(jnp.concatenate([x_in, bc_in], axis=1), segment, conv_weight, conv_bias)
    x_full = conv_out[:, :DI]
    x_low = low(x_full)
    b_low = low(conv_out[:, DI:DI + N])
    c_low = low(conv_out[:, DI + N:])
    pieces = (by_span(x_full.reshape(TOKENS, H, HP)), by_span(x_low.reshape(TOKENS, H, HP)), by_span(b_low), by_span(c_low), by_span(step_raw), by_span(segment), seg_before)
    start_state = jnp.zeros((H, HP, N), hidden.dtype)
    last_state, mixed_out = lax.scan(jax.checkpoint(partial(span_mix, (step_bias, decay_log, skip_gain))), start_state, pieces)
    mixed_out = low(low_back(mixed_out.reshape(TOKENS, DI)))
    gated = mixed_out * jax.nn.silu(gate_part)
    gate_normed = low(rms_gain(gated, gate_gain))
    branch = low_back(jnp.dot(gate_normed, out_weight, precision=highest))
    return hidden + branch

def reference(tokens, doc_starts, norm_gain, in_weight, conv_weight, conv_bias, step_bias, decay_log, skip_gain, gate_gain, out_weight, cotangent):
    positions = jnp.arange(TOKENS, dtype=jnp.int32)
    segment = segment_ids(doc_starts, positions).astype(jnp.int32)
    before = jnp.concatenate([jnp.full((1,), -1, jnp.int32), segment[:-1]]).astype(jnp.int32)
    seg_before = before.reshape(N_SPAN, SPAN_TOK)[:, 0]

    def network(hidden, gain_all, in_all, conv_all, bias_all, step_all, decay_all, skip_all, gate_all, out_all):
        for layer_index in range(LAYERS):
            params = (gain_all[layer_index], in_all[layer_index], conv_all[layer_index], bias_all[layer_index], step_all[layer_index], decay_all[layer_index], skip_all[layer_index], gate_all[layer_index], out_all[layer_index])
            hidden = layer_forward(hidden, params, segment, seg_before)
        return hidden
    floats = [member.astype(jnp.float32) for member in (tokens, norm_gain, in_weight, conv_weight, conv_bias, step_bias, decay_log, skip_gain, gate_gain, out_weight)]
    result, pullback = jax.vjp(network, *floats)
    gradients = pullback(cotangent.astype(jnp.float32))
    return (result.astype(jnp.bfloat16), gradients[0], gradients[1], gradients[2], gradients[3], gradients[4], gradients[5], gradients[6], gradients[7], gradients[8], gradients[9])
```

```python
import functools

import jax
import jax.numpy as jnp
from jax import lax
from jax.experimental import pallas as pl
from jax.experimental.pallas import tpu as pltpu
from jax.sharding import Mesh, PartitionSpec as P

D = 1536
DI = 3072
H = 48
HP = 64
N = 128
CONV = 4
LAYERS = 2
CH = DI + 2 * N
EPS = 1e-05

AX = ("z", "x", "yh", "c", "yl")
ZX = ("z", "x")
LINE = ("yh", "c", "yl")
Y = ("yh", "yl")
NQ = 16
NG = 8
TOK = 128
GT = TOK * NG
SPAN = 256
NS = GT // SPAN
HL = H // NG
W = HL * HP
CA = W + 2 * N + 128

bf = jnp.bfloat16
f32 = jnp.float32
HI = lax.Precision.HIGHEST


def mm(a, b, ca=1, cb=0):
    return lax.dot_general(a, b, (((ca,), (cb,)), ((), ())), preferred_element_type=f32)


def mm_hi(a, b):
    return jnp.dot(a, b, precision=HI, preferred_element_type=f32)


def a2a(a, axes):
    return lax.all_to_all(a, axes, 0, 0, tiled=True)


def core_swap(a):
    return lax.ppermute(a, "c", [(0, 1), (1, 0)])


def line_gather(own):
    n = own.shape[1]
    line = a2a(jnp.broadcast_to(own[None], (4,) + own.shape), Y)
    both = lax.all_gather(line, "c", axis=0)
    both = both.reshape(2, 2, 2, TOK, n)
    return both.transpose(1, 0, 2, 3, 4).reshape(GT, n)


def line_reduce(part):
    n = part.shape[1]
    core = lax.axis_index("c")
    blocks = part.reshape(2, 2, 2, TOK, n)
    mine = lax.dynamic_index_in_dim(blocks, core, 1, keepdims=False)
    other = lax.dynamic_index_in_dim(blocks, 1 - core, 1, keepdims=False)
    got = core_swap(other.astype(bf))
    chip = (mine + got.astype(f32)).astype(bf).reshape(4, TOK, n)
    return jnp.sum(a2a(chip, Y).astype(f32), axis=0)


def small_reduce(parts):
    m = parts.shape[0]
    sent = parts.reshape(m, NG, TOK).transpose(1, 0, 2)
    return jnp.sum(a2a(sent, LINE), axis=0)


def small_gather(own):
    m = own.shape[0]
    got = a2a(jnp.broadcast_to(own[None], (NG,) + own.shape), LINE)
    return got.transpose(1, 0, 2).reshape(m, GT)


def group_gather(block):
    return lax.all_gather(block, ZX, axis=0, tiled=True)


def group_gather_now(block):
    r, n = block.shape
    return a2a(jnp.broadcast_to(block[None], (NQ, r, n)), ZX).reshape(NQ * r, n)


def group_reduce(full):
    r = full.shape[0] // NQ
    return jnp.sum(a2a(full.reshape(NQ, r, full.shape[1]), ZX).astype(f32), axis=0)


def heads_out(cols, width):
    r = cols.shape[0]
    return cols.reshape(r, 2, 2, 2, width).transpose(2, 3, 1, 0, 4).reshape(NG, r, width)


def heads_in(blocks):
    _, r, width = blocks.shape
    return blocks.reshape(2, 2, 2, r, width).transpose(3, 2, 0, 1, 4).reshape(r, NG * width)


def line_of(group):
    yl, yh, c = group // 4, (group // 2) % 2, group % 2
    return yh * 4 + c * 2 + yl


TO_HEADS = [(s, (s % NQ) * NG + line_of(s // NQ)) for s in range(NQ * NG)]
TO_OWNER = [(b, a) for a, b in TO_HEADS]


def in_blocks(weight, gain, extra):
    folded = (weight.astype(f32) * gain.astype(f32)[:, None]).astype(bf)
    z = heads_out(folded[:, :DI], W)
    x = heads_out(folded[:, DI : 2 * DI], W)
    bc = jnp.broadcast_to(folded[None, :, 2 * DI : 2 * DI + 2 * N], (NG, 12, 2 * N))
    step = heads_out(folded[:, 2 * DI + 2 * N :], HL)
    extra = jnp.broadcast_to(extra[None], (NG,) + extra.shape)
    step = jnp.concatenate([step, extra], axis=2)
    step = jnp.pad(step, ((0, 0), (0, 0), (0, 128 - step.shape[2])))
    return jnp.concatenate([x, bc, step, z], axis=2)


SCAN_ROWS = HL * HP // NQ


def scan_kernel(reverse, q_ref, got_ref, out_ref):
    row = q_ref[0] * SCAN_ROWS + lax.broadcasted_iota(jnp.int32, (SCAN_ROWS, N), 0)
    lane = lax.broadcasted_iota(jnp.int32, (SCAN_ROWS, N), 1)
    head = jnp.zeros((SCAN_ROWS, N), jnp.int32)
    for k in range(1, HL):
        head = head + (row >= k * HP).astype(jnp.int32)
    chosen = (lane == head) | (lane == head + HL) | (lane == head + 2 * HL)
    carry = jnp.zeros((SCAN_ROWS, N), f32)
    pad = jnp.zeros((32 - SCAN_ROWS, N), f32)
    for j in range(NQ - 1, -1, -1) if reverse else range(NQ):
        out_ref[j] = jnp.concatenate([carry, pad], axis=0).astype(bf)
        block = got_ref[j].astype(f32)
        decay = jnp.sum(
            jnp.where(chosen, block[SCAN_ROWS : SCAN_ROWS + 1], 0.0), axis=1, keepdims=True
        )
        carry = decay * carry + block[:SCAN_ROWS]


def exclusive_scan(total_decay, total_state, reverse):
    q = lax.axis_index(ZX)
    rows = SCAN_ROWS
    hi = total_decay.astype(bf)
    rest = total_decay - hi.astype(f32)
    mid = rest.astype(bf)
    low = (rest - mid.astype(f32)).astype(bf)
    tail = jnp.pad(jnp.concatenate([hi, mid, low])[None], ((0, 7), (0, N - 3 * HL)))
    sent = jnp.concatenate(
        [total_state.astype(bf).reshape(NQ, rows, N), jnp.broadcast_to(tail[None], (NQ, 8, N))],
        axis=1,
    )
    got = a2a(sent, ZX)
    outs = pl.pallas_call(
        functools.partial(scan_kernel, reverse),
        out_shape=jax.ShapeDtypeStruct((NQ, 32, N), bf),
        in_specs=[
            pl.BlockSpec(memory_space=pltpu.SMEM),
            pl.BlockSpec(memory_space=pltpu.VMEM),
        ],
        out_specs=pl.BlockSpec(memory_space=pltpu.VMEM),
        name="group_scan",
    )(q.reshape(1).astype(jnp.int32), got)
    back = a2a(outs, ZX)[:, :rows]
    return back.reshape(HL * HP, N).astype(f32)


def silu_parts(v):
    s = jax.nn.sigmoid(v)
    return v * s, s * (1.0 + v * (1.0 - s))


def per_device(
    tokens,
    doc_starts,
    norm_gain,
    in_weight,
    conv_weight,
    conv_bias,
    step_bias,
    decay_log,
    skip_gain,
    gate_gain,
    out_weight,
    cotangent,
):
    q = lax.axis_index(ZX)
    yh, core, yl = lax.axis_index("yh"), lax.axis_index("c"), lax.axis_index("yl")
    sub = yh * 2 + core
    group = yl * 4 + sub

    a_blocks, z_blocks = [], []
    own_ch = CH // (NQ * NG)
    conv_own = jnp.concatenate([conv_weight, conv_bias[:, None]], axis=1).reshape(-1, own_ch)
    conv_own = jnp.pad(conv_own, ((0, 12 - conv_own.shape[0]), (0, 0)))
    sent = [in_blocks(in_weight[l], norm_gain[l], conv_own if l == 0 else conv_own[:, :0]) for l in range(LAYERS)]
    got = a2a(jnp.stack(sent, axis=1), LINE)
    for l in range(LAYERS):
        block = got[:, l].reshape(NG * 12, CA + W)
        a_blocks.append(block[:, :CA])
        z_blocks.append(block[:, CA:])
    folded_out = (out_weight.astype(f32) * gate_gain.astype(f32)[:, :, None]).astype(bf)
    out_blocks = lax.ppermute(folded_out, AX, TO_HEADS)
    w_a, w_z, w_o = [None] * 2, [None] * 2, [None] * 2
    w_a[0] = group_gather_now(a_blocks[0])
    conv_all = w_a[0][:, W + 2 * N + HL : W + 2 * N + HL + own_ch].reshape(NQ * NG, 12, own_ch)
    conv_all = conv_all[:, : LAYERS * (CONV + 1)].transpose(1, 0, 2)
    conv_all = conv_all.reshape(LAYERS, CONV + 1, CH).astype(f32)
    conv_x = lax.dynamic_slice_in_dim(conv_all, group * W, W, 2)
    conv_here = jnp.concatenate([conv_x, conv_all[:, :, DI:]], axis=2)
    w_z[0] = group_gather(z_blocks[0])
    w_o[0] = group_gather(out_blocks[0])
    w_a[1] = group_gather(a_blocks[1])
    w_z[1] = group_gather(z_blocks[1])
    w_o[1] = group_gather(out_blocks[1])

    pos = q * GT + jnp.arange(-(CONV - 1), GT + CONV - 1, dtype=jnp.int32)
    seg_ext = jnp.sum((doc_starts[None, :] <= pos[:, None]).astype(jnp.int32), axis=1) - 1
    seg = seg_ext[CONV - 1 : CONV - 1 + GT]
    seg_spans = seg.reshape(NS, SPAN)
    seg_before = seg_ext[CONV - 2 : CONV - 2 + GT : SPAN]
    same_back = [
        (seg_ext[CONV - 1 - k : CONV - 1 - k + GT] == seg).astype(f32)[:, None] for k in range(CONV)
    ]
    same_fwd = [
        (seg_ext[CONV - 1 + k : CONV - 1 + k + GT] == seg).astype(f32)[:, None] for k in range(CONV)
    ]
    order = jnp.arange(SPAN)
    tri = (order[None, :] <= order[:, None]).astype(f32)
    mask = (order[None, :] <= order[:, None])[None] & (
        seg_spans[:, None, :] == seg_spans[:, :, None]
    )
    in_mask = (seg_spans == seg_before[:, None]).astype(f32)[:, :, None]
    end_mask = (seg_spans == seg_spans[:, -1:]).astype(f32)[:, :, None]
    span_mask = in_mask[:, -1]
    head_of = (jnp.arange(W)[:, None] // HP == jnp.arange(HL)[None]).astype(f32)

    def expand(a):
        return mm_hi(a.reshape(-1, HL), head_of.T)

    def by_head(a):
        return mm_hi(a, head_of).reshape(NS, SPAN, HL)

    def heads(a):
        return a.reshape(NS, SPAN, HL, HP)

    def pick_heads(a):
        return lax.dynamic_slice_in_dim(a, sub * HL, HL, 0)

    h = tokens.astype(f32)
    saved = []
    grad_full = line_gather(cotangent)

    for l in range(LAYERS):
        bias_h, log_h, skip_h = (pick_heads(p[l]) for p in (step_bias, decay_log, skip_gain))
        r_in = lax.rsqrt(jnp.mean(h * h, axis=-1, keepdims=True) + EPS)
        normed = line_gather((h * r_in).astype(bf))
        proj = mm(normed, w_a[l])
        u = proj[:, : W + 2 * N].astype(bf)
        step_in = proj[:, W + 2 * N : W + 2 * N + HL].astype(bf).astype(f32)
        step_in = step_in.reshape(NS, SPAN, HL) + bias_h
        edge = lax.ppermute(u[GT - (CONV - 1) :], ZX, [(i, i + 1) for i in range(NQ - 1)])
        z = mm(normed, w_z[l])
        ext = jnp.concatenate([edge, u], axis=0).astype(f32)
        cw = conv_here[l]
        pre = jnp.broadcast_to(cw[CONV][None], (GT, W + 2 * N))
        for k in range(CONV):
            pre = pre + cw[k][None] * ext[CONV - 1 - k : CONV - 1 - k + GT] * same_back[k]
        v = pre * jax.nn.sigmoid(pre)
        xc = v[:, :W]
        b_low = v[:, W : W + N].astype(bf).reshape(NS, SPAN, N)
        c_low = v[:, W + N :].astype(bf).reshape(NS, SPAN, N)
        step = jax.nn.softplus(step_in)
        rate = -jnp.exp(log_h)
        run = jnp.einsum("ts,ksh->kth", tri, rate * step, precision=HI)
        run_t = run.transpose(0, 2, 1)
        spread = run_t[:, :, :, None] - run_t[:, :, None, :]
        decay = jnp.where(mask[:, None], jnp.exp(jnp.where(mask[:, None], spread, 0.0)), 0.0)
        inflow = jnp.exp(run) * in_mask
        w_end = jnp.exp(run[:, -1:] - run) * end_mask
        span_decay = jnp.exp(run[:, -1]) * span_mask
        gram = jnp.einsum("ktn,ksn->kts", c_low, b_low, preferred_element_type=f32)
        mixing = (gram[:, None] * decay).astype(bf)
        step_x = expand(step)
        xs = (step_x * xc).astype(bf)
        weights_x = expand(w_end * step)
        weighted = (weights_x * xc).astype(bf)
        own = jnp.einsum("kshp,ksn->khpn", heads(weighted), b_low, preferred_element_type=f32)
        total = own[0]
        total_decay = span_decay[0]
        for k in range(1, NS):
            total = span_decay[k][:, None, None] * total + own[k]
            total_decay = total_decay * span_decay[k]
        carried = exclusive_scan(total_decay, total.reshape(HL * HP, N), False)
        within = jnp.einsum("khts,kshp->kthp", mixing, heads(xs), preferred_element_type=f32)
        carry = carried.reshape(HL, HP, N)
        carries = []
        for k in range(NS):
            carries.append(carry)
            carry = span_decay[k][:, None, None] * carry + own[k]
        carried_in = jnp.stack(carries)
        carried_low = carried_in.astype(bf)
        reading = jnp.einsum("khpn,ktn->kthp", carried_low, c_low, preferred_element_type=f32)
        inflow_x = expand(inflow)
        y0 = within.reshape(GT, W) + inflow_x * reading.reshape(GT, W)
        skip_x = jnp.repeat(skip_h, HP)[None]
        mixed = (y0 + skip_x * xc).astype(bf).astype(f32)
        silu_z, dsilu_z = silu_parts(z)
        gated = mixed * silu_z
        gated_low = gated.astype(bf)
        square = jnp.sum(gated * gated, axis=1)
        part = mm(gated_low, w_o[l])
        if l == LAYERS - 1:
            d_q = mm(grad_full, w_o[l], 1, 1)
            sums = small_reduce(jnp.stack([square, jnp.sum(d_q * gated, axis=1)]))
            r_gate = lax.rsqrt(sums[0] / DI + EPS)
            kappa = r_gate * r_gate * r_gate * sums[1] / DI
            gate_scales = small_gather(jnp.stack([r_gate, kappa]))
        else:
            d_q = None
            gate_scales = None
            r_gate = lax.rsqrt(small_reduce(square[None])[0] / DI + EPS)
        branch = line_reduce(part) * r_gate[:, None]
        saved.append(
            dict(
                h=h, r_in=r_in, normed=normed, ext=ext, pre=pre, v=v, b_low=b_low, c_low=c_low,
                step_in=step_in, step=step, rate=rate, decay=decay, inflow_x=inflow_x, w_end=w_end,
                span_decay=span_decay, gram=gram, mixing=mixing, step_x=step_x, xs=xs,
                weights_x=weights_x, weighted=weighted, carried_in=carried_in,
                carried_low=carried_low, y0=y0, skip_x=skip_x, mixed=mixed, silu_z=silu_z,
                dsilu_z=dsilu_z, gated=gated, r_gate=r_gate, branch=branch, d_q=d_q,
                gate_scales=gate_scales,
            )
        )
        h = h + branch
    output = h.astype(bf)

    grad = cotangent.astype(f32)
    in_grads, gain_grads, out_grads, gate_grads = ([None] * LAYERS for _ in range(4))
    conv_grads, head_grads = [None] * LAYERS, [None] * LAYERS
    for l in reversed(range(LAYERS)):
        s = saved[l]
        if l == LAYERS - 1:
            d_q, gate_scales = s["d_q"], s["gate_scales"]
        else:
            grad_low = grad.astype(bf)
            dot = jnp.sum(grad_low.astype(f32) * s["branch"], axis=1)
            kappa = s["r_gate"] * s["r_gate"] * dot / DI
            gate_scales = small_gather(jnp.stack([s["r_gate"], kappa]))
            grad_full = line_gather(grad_low)
            d_q = mm(grad_full, w_o[l], 1, 1)
        r_full, k_full = gate_scales[0][:, None], gate_scales[1][:, None]
        gated = s["gated"]
        out_part = mm((gated * r_full).astype(bf), grad_full, 0, 0)
        out_sum = group_reduce(out_part.astype(bf))
        d_gated = r_full * d_q - gated * k_full
        dy = (d_gated * s["silu_z"]).astype(bf)
        dz = (d_gated * s["mixed"] * s["dsilu_z"]).astype(bf)
        z_part = mm(s["normed"], dz, 0, 0)
        z_sum = group_reduce(z_part.astype(bf))
        dyf = dy.astype(f32)
        xc = s["v"][:, :W]
        b_low, c_low = s["b_low"], s["c_low"]
        dyh = heads(dy)
        scaled = (s["inflow_x"] * dyf).astype(bf)
        dcarr = jnp.einsum("kthp,ktn->khpn", heads(scaled), c_low, preferred_element_type=f32)
        sd = s["span_decay"]
        total = dcarr[NS - 1]
        total_decay = sd[NS - 1]
        for k in range(NS - 2, -1, -1):
            total = dcarr[k] + sd[k][:, None, None] * total
            total_decay = total_decay * sd[k]
        later = exclusive_scan(total_decay, total.reshape(HL * HP, N), True)
        d_mix = jnp.einsum("kthp,kshp->khts", dyh, heads(s["xs"]), preferred_element_type=f32)
        d_gram = jnp.sum(d_mix * s["decay"], axis=1).astype(bf)
        d_xs = jnp.einsum(
            "khts,kthp->kshp", s["mixing"], dyh, preferred_element_type=f32
        ).reshape(GT, W)
        d_c = jnp.einsum("kts,ksn->ktn", d_gram, b_low, preferred_element_type=f32)
        d_c = d_c + jnp.einsum(
            "kthp,khpn->ktn", heads(scaled), s["carried_low"], preferred_element_type=f32
        )
        d_b = jnp.einsum("kts,ktn->ksn", d_gram, c_low, preferred_element_type=f32)
        end = later.reshape(HL, HP, N)
        ends = [None] * NS
        for k in range(NS - 1, -1, -1):
            ends[k] = end
            end = dcarr[k] + sd[k][:, None, None] * end
        d_end = jnp.stack(ends)
        d_end_low = d_end.astype(bf)
        d_span = jnp.sum(d_end * s["carried_in"], axis=(2, 3))
        d_weighted = jnp.einsum(
            "khpn,ksn->kshp", d_end_low, b_low, preferred_element_type=f32
        ).reshape(GT, W)
        d_b = d_b + jnp.einsum(
            "khpn,kshp->ksn", d_end_low, heads(s["weighted"]), preferred_element_type=f32
        )
        d_xc = s["skip_x"] * dyf + s["step_x"] * d_xs + s["weights_x"] * d_weighted
        skip_sum = by_head(dyf * xc)
        skip_grad = jnp.sum(skip_sum, axis=(0, 1))
        row_sum = by_head(dyf * s["y0"])
        col_sum = by_head(s["xs"].astype(f32) * d_xs)
        d_step = by_head(xc * d_xs)
        d_w = by_head(d_weighted * xc)
        step, w_end, rate = s["step"], s["w_end"], s["rate"]
        d_step = d_step + d_w * w_end
        d_ww = d_w * w_end * step
        d_run = row_sum - col_sum - d_ww
        d_last = jnp.sum(d_ww, axis=1) + d_span * sd
        d_a = jnp.einsum("ts,kth->ksh", tri, d_run, precision=HI) + d_last[:, None, :]
        d_step = d_step + rate * d_a
        log_grad = rate * jnp.sum(step * d_a, axis=(0, 1))
        d_raw = d_step * jax.nn.sigmoid(s["step_in"])
        bias_grad = jnp.sum(d_raw, axis=(0, 1))
        dv = jnp.concatenate([d_xc, d_b.reshape(GT, N), d_c.reshape(GT, N)], axis=1)
        pre = s["pre"]
        sig = jax.nn.sigmoid(pre)
        d_pre = dv * (sig * (1.0 + pre * (1.0 - sig)))
        edge = lax.ppermute(d_pre[: CONV - 1], ZX, [(i + 1, i) for i in range(NQ - 1)])
        d_ext = jnp.concatenate([d_pre, edge], axis=0)
        cw = conv_here[l]
        du = jnp.zeros_like(d_pre)
        taps = []
        for k in range(CONV):
            du = du + cw[k][None] * d_ext[k : k + GT] * same_fwd[k]
            past = s["ext"][CONV - 1 - k : CONV - 1 - k + GT]
            taps.append(jnp.sum(d_pre * past * same_back[k], axis=0))
        taps.append(jnp.sum(d_pre, axis=0))
        taps = jnp.stack(taps)
        conv_full = jnp.zeros((CONV + 1, CH), f32)
        conv_full = lax.dynamic_update_slice_in_dim(conv_full, taps[:, :W], group * W, 1)
        conv_grads[l] = conv_full.at[:, DI:].set(taps[:, W:])
        head_full = jnp.zeros((3, H), f32)
        head_grads[l] = lax.dynamic_update_slice_in_dim(
            head_full, jnp.stack([bias_grad, log_grad, skip_grad]), group * HL, 1
        )
        da = jnp.concatenate(
            [du.astype(bf), jnp.pad(d_raw.reshape(GT, HL), ((0, 0), (0, 128 - HL))).astype(bf)],
            axis=1,
        )
        d_norm = line_reduce(mm(da, w_a[l], 1, 1) + mm(dz, w_z[l], 1, 1))
        a_part = mm(s["normed"], da, 0, 0)
        a_sum = group_reduce(a_part.astype(bf))
        hidden, r_in = s["h"], s["r_in"]
        inner = jnp.mean(hidden * d_norm, axis=1, keepdims=True)
        grad = grad + r_in * d_norm - hidden * (r_in * r_in * r_in) * inner
        both = jnp.concatenate([a_sum, z_sum], axis=1).reshape(NG, 12, CA + W)
        both = a2a(both, LINE)
        g_in = jnp.concatenate(
            [
                heads_in(both[:, :, CA:]),
                heads_in(both[:, :, :W]),
                jnp.sum(both[:, :, W : W + 2 * N], axis=0),
                heads_in(both[:, :, W + 2 * N : W + 2 * N + HL]),
            ],
            axis=1,
        )
        in_grads[l] = g_in * norm_gain[l].astype(f32)[:, None]
        gain_grads[l] = jnp.sum(g_in * in_weight[l].astype(f32), axis=1)
        g_out = lax.ppermute(out_sum, AX, TO_OWNER)
        out_grads[l] = g_out * gate_gain[l].astype(f32)[:, None]
        gate_grads[l] = jnp.sum(g_out * out_weight[l].astype(f32), axis=1)

    conv_sent = jnp.stack(conv_grads).reshape(LAYERS, CONV + 1, NQ * NG, CH // (NQ * NG))
    conv_sent = conv_sent.transpose(2, 0, 1, 3).reshape(NQ * NG, -1)
    head_sent = jnp.stack(head_grads).reshape(LAYERS, 3, 2, H // 2).transpose(2, 0, 1, 3)
    head_sent = jnp.tile(head_sent.reshape(2, -1), (NQ * NG // 2, 1))
    small = jnp.concatenate([conv_sent, head_sent], axis=1)
    small = jnp.sum(a2a(small, AX), axis=0)
    n_conv = conv_sent.shape[1]
    conv_grad = small[:n_conv].reshape(LAYERS, CONV + 1, -1)
    head_grad = small[n_conv:].reshape(LAYERS, 3, -1)
    return (
        output,
        grad,
        jnp.stack(gain_grads),
        jnp.stack(in_grads),
        conv_grad[:, :CONV],
        conv_grad[:, CONV],
        head_grad[:, 0],
        head_grad[:, 1],
        head_grad[:, 2],
        jnp.stack(gate_grads),
        jnp.stack(out_grads),
    )


def solution(mesh):
    fine = Mesh(mesh.devices.reshape(4, 4, 2, 2, 2), AX)
    tok, last, mid, heads = P(AX, None), P(None, AX), P(None, AX, None), P(None, "yl")
    conv = P(None, None, AX)
    return jax.shard_map(
        per_device,
        mesh=fine,
        in_specs=(tok, P(), last, mid, conv, last, heads, heads, heads, last, mid, tok),
        out_specs=(tok, tok, last, mid, conv, last, heads, heads, heads, last, mid),
        check_vma=False,
    )
```

```python
import functools

import jax
import jax.numpy as jnp
from jax import lax
from jax.experimental import pallas as pl
from jax.experimental.pallas import tpu as pltpu
from jax.sharding import Mesh, PartitionSpec as P

D = 1536
DI = 3072
H = 48
HP = 64
N = 128
CONV = 4
LAYERS = 2
CH = DI + 2 * N
EPS = 1e-05

AX = ("z", "x", "yh", "c", "yl")
ZX = ("z", "x")
LINE = ("yh", "c", "yl")
Y = ("yh", "yl")
NQ = 16
NG = 8
TOK = 128
GT = TOK * NG
SPAN = 256
NS = GT // SPAN
HL = H // NG
W = HL * HP
CC = W + 2 * N
CA = CC + 128

bf = jnp.bfloat16
f32 = jnp.float32
HI = lax.Precision.HIGHEST


SMEM = pl.BlockSpec(memory_space=pltpu.SMEM)


def struct(shape, dtype=f32):
    return jax.ShapeDtypeStruct(shape, dtype)


def mm(a, b, ca=1, cb=0):
    return lax.dot_general(a, b, (((ca,), (cb,)), ((), ())), preferred_element_type=f32)


def a2a(a, axes):
    return lax.all_to_all(a, axes, 0, 0, tiled=True)


def core_swap(a):
    return lax.ppermute(a, "c", [(0, 1), (1, 0)])


def line_index():
    return lax.axis_index("yh") * 2 + lax.axis_index("yl")


def along_line(a, distance):
    return lax.ppermute(a, Y, [(i, (i + distance) % 4) for i in range(4)])


def place_kernel(extra, pos_ref, *refs):
    blocks, outs = refs[:NG], refs[NG:]
    step = pl.program_id(0)
    for i, block in enumerate(blocks):

        @pl.when(step == i)
        def _(block=block):
            outs[0][...] = block[:TOK]
            if extra:
                outs[1][...] = block[TOK:]


def line_gather(own):
    rows, n = own.shape
    extra = rows - TOK
    y, core = line_index(), lax.axis_index("c")
    blocks, places = [], []

    def place(distance, c):
        at = (y - distance) % 4
        return (at // 2) * 4 + c * 2 + at % 2

    for d in (0, 1, 3, 2):
        got = along_line(own, d) if d else own
        blocks += [got, core_swap(got)]
        places += [place(d, core), place(d, 1 - core)]
    shapes = [struct((GT, n), own.dtype)]
    if extra:
        shapes.append(struct((NG * extra, n), own.dtype))
    outs = pl.pallas_call(
        functools.partial(place_kernel, extra),
        out_shape=shapes,
        grid_spec=pltpu.PrefetchScalarGridSpec(
            num_scalar_prefetch=1,
            grid=(NG,),
            in_specs=[pl.BlockSpec((rows, n), lambda i, pos: (0, 0))] * NG,
            out_specs=[pl.BlockSpec((TOK, n), lambda i, pos: (pos[i], 0))]
            + [pl.BlockSpec((extra, n), lambda i, pos: (pos[i], 0))] * (extra > 0),
        ),
        compiler_params=pltpu.CompilerParams(vmem_limit_bytes=60 * 1024 * 1024),
        name="place_tokens",
    )(jnp.stack(places).astype(jnp.int32), *blocks)
    return outs if extra else outs[0]


def line_reduce(part):
    n = part.shape[1]
    core, y = lax.axis_index("c"), line_index()
    blocks = part.reshape(2, 2, 2, TOK, n)
    mine = lax.dynamic_index_in_dim(blocks, core, 1, keepdims=False)
    other = lax.dynamic_index_in_dim(blocks, 1 - core, 1, keepdims=False)
    got = core_swap(other.astype(bf))
    chip = (mine.astype(f32) + got.astype(f32)).reshape(4, TOK, n)
    total = lax.dynamic_index_in_dim(chip, y, 0, keepdims=False)
    chip = chip.astype(bf)
    for d in (1, 3, 2):
        sent = lax.dynamic_index_in_dim(chip, (y + d) % 4, 0, keepdims=False)
        total = total + along_line(sent, d).astype(f32)
    return total


def small_reduce(parts):
    m = parts.shape[0]
    sent = parts.reshape(m, NG, TOK).transpose(1, 0, 2)
    return jnp.sum(a2a(sent, LINE), axis=0)


def small_sum(parts):
    return jnp.sum(a2a(jnp.broadcast_to(parts[None], (NG,) + parts.shape), LINE), axis=0)


def rounded(a):
    return lax.reduce_precision(a, exponent_bits=8, mantissa_bits=7)


def three_parts(a):
    hi = rounded(a)
    mid = rounded(a - hi)
    return [hi.astype(bf), mid.astype(bf), (a - hi - mid).astype(bf)]


def group_gather(block):
    return lax.all_gather(block, ZX, axis=0, tiled=True)


def group_gather_now(block):
    r, n = block.shape
    return a2a(jnp.broadcast_to(block[None], (NQ, r, n)), ZX).reshape(NQ * r, n)


def tie(*arrays):
    return lax.optimization_barrier(arrays)


def group_reduce(full):
    r = full.shape[0] // NQ
    return jnp.sum(a2a(full.reshape(NQ, r, full.shape[1]), ZX).astype(f32), axis=0)


def heads_out(cols, width):
    r = cols.shape[0]
    return cols.reshape(r, 2, 2, 2, width).transpose(2, 3, 1, 0, 4).reshape(NG, r, width)


def heads_in(blocks):
    _, r, width = blocks.shape
    return blocks.reshape(2, 2, 2, r, width).transpose(3, 2, 0, 1, 4).reshape(r, NG * width)


def line_of(group):
    yl, yh, c = group // 4, (group // 2) % 2, group % 2
    return yh * 4 + c * 2 + yl


TO_HEADS = [(s, (s % NQ) * NG + line_of(s // NQ)) for s in range(NQ * NG)]
TO_OWNER = [(b, a) for a, b in TO_HEADS]


def in_blocks(weight, gain, extra):
    folded = (weight.astype(f32) * gain.astype(f32)[:, None]).astype(bf)
    z = heads_out(folded[:, :DI], W)
    x = heads_out(folded[:, DI : 2 * DI], W)
    bc = jnp.broadcast_to(folded[None, :, 2 * DI : 2 * DI + 2 * N], (NG, 12, 2 * N))
    step = heads_out(folded[:, 2 * DI + 2 * N :], HL)
    extra = jnp.broadcast_to(extra[None], (NG,) + extra.shape)
    step = jnp.concatenate([step, extra], axis=2)
    step = jnp.pad(step, ((0, 0), (0, 0), (0, 128 - step.shape[2])))
    return jnp.concatenate([x, bc, step, z], axis=2)


SCAN_ROWS = HL * HP // NQ


def scan_kernel(reverse, q_ref, got_ref, out_ref):
    row = q_ref[0] * SCAN_ROWS + lax.broadcasted_iota(jnp.int32, (SCAN_ROWS, N), 0)
    lane = lax.broadcasted_iota(jnp.int32, (SCAN_ROWS, N), 1)
    head = jnp.zeros((SCAN_ROWS, N), jnp.int32)
    for k in range(1, HL):
        head = head + (row >= k * HP).astype(jnp.int32)
    chosen = (lane == head) | (lane == head + HL) | (lane == head + 2 * HL)
    carry = jnp.zeros((SCAN_ROWS, N), f32)
    pad = jnp.zeros((32 - SCAN_ROWS, N), f32)
    for j in range(NQ - 1, -1, -1) if reverse else range(NQ):
        out_ref[j] = jnp.concatenate([carry, pad], axis=0).astype(bf)
        block = got_ref[j].astype(f32)
        decay = jnp.sum(
            jnp.where(chosen, block[SCAN_ROWS : SCAN_ROWS + 1], 0.0), axis=1, keepdims=True
        )
        carry = decay * carry + block[:SCAN_ROWS]


def exclusive_scan(sent, reverse):
    q = lax.axis_index(ZX)
    got = a2a(sent, ZX)
    outs = pl.pallas_call(
        functools.partial(scan_kernel, reverse),
        out_shape=jax.ShapeDtypeStruct((NQ, 32, N), bf),
        in_specs=[
            pl.BlockSpec(memory_space=pltpu.SMEM),
            pl.BlockSpec(memory_space=pltpu.VMEM),
        ],
        out_specs=pl.BlockSpec(memory_space=pltpu.VMEM),
        name="group_scan",
    )(q.reshape(1).astype(jnp.int32), got)
    return a2a(outs, ZX)


PAIRS = HL // 2
LAST = NS - 1


def dot(a, b, ca, cb, precision=None):
    return lax.dot_general(
        a, b, (((ca,), (cb,)), ((), ())), preferred_element_type=f32, precision=precision
    )


def by_lanes(cols):
    lane = lax.broadcasted_iota(jnp.int32, (cols.shape[0], 128), 1)
    return jnp.concatenate(
        [
            jnp.where(lane < HP, cols[:, 2 * p : 2 * p + 1], cols[:, 2 * p + 1 : 2 * p + 2])
            for p in range(PAIRS)
        ],
        axis=1,
    )


def by_rows(row, states):
    return jnp.concatenate(
        [row[:, h : h + 1] * states[h * HP : (h + 1) * HP] for h in range(HL)], axis=0
    )


def head_sums(wide):
    column = lax.broadcasted_iota(jnp.int32, (W, 128), 0)
    lane = lax.broadcasted_iota(jnp.int32, (W, 128), 1)
    chosen = ((column >= lane * HP) & (column < lane * HP + HP)).astype(f32)
    return dot(wide, chosen, 1, 0, HI)


def token_sums(wide):
    return dot(jnp.ones((8, wide.shape[1]), f32), wide, 1, 1, HI)


def write_states(sent_ref, states, decay):
    lane = lax.broadcasted_iota(jnp.int32, (8, 128), 1)
    decay = jnp.where(lane < HL, jnp.broadcast_to(decay, (8, 128)), 0.0)
    hi = decay.astype(bf).astype(f32)
    mid = (decay - hi).astype(bf).astype(f32)
    low = decay - hi - mid
    tail = hi + pltpu.roll(mid, HL, 1) + pltpu.roll(low, 2 * HL, 1)
    for j in range(NQ):
        block = states[j * SCAN_ROWS : (j + 1) * SCAN_ROWS]
        sent_ref[j] = jnp.concatenate([block, tail], axis=0).astype(bf)


def read_states(back_ref):
    return jnp.concatenate([back_ref[j].astype(f32)[:SCAN_ROWS] for j in range(NQ)], axis=0)


def span_masks(segc_ref, segr_ref):
    row = lax.broadcasted_iota(jnp.int32, (SPAN, SPAN), 0)
    col = lax.broadcasted_iota(jnp.int32, (SPAN, SPAN), 1)
    return (col <= row) & (segc_ref[...] == segr_ref[0])


def head_decay(mask, run, run_t, h):
    return jnp.exp(jnp.where(mask, run[:, h : h + 1] - run_t[h : h + 1], -1e30))


def end_weights(run, segc_ref, seg_end):
    return jnp.exp(run[SPAN - 1 :] - run) * (segc_ref[...] == seg_end).astype(f32)


def inflow_of(run, segc_ref, seg_before):
    return jnp.exp(run) * (segc_ref[...] == seg_before).astype(f32)


def mix_kernel(
    seg_ref, v_ref, raw_ref, bias_ref, rate_ref, segc_ref, segr_ref,
    within_ref, local_ref, step_ref, run_ref, before_ref, decay_ref, sent_ref, acc_ref, dec_ref,
):
    k = pl.program_id(0)

    @pl.when(k == 0)
    def _():
        acc_ref[...] = jnp.zeros_like(acc_ref)
        dec_ref[...] = jnp.ones_like(dec_ref)

    lane = lax.broadcasted_iota(jnp.int32, (SPAN, 128), 1)
    raw = raw_ref[...].astype(f32) + bias_ref[...]
    step = jnp.where(lane < HL, jax.nn.softplus(raw), 0.0)
    row = lax.broadcasted_iota(jnp.int32, (SPAN, SPAN), 0)
    col = lax.broadcasted_iota(jnp.int32, (SPAN, SPAN), 1)
    run = dot((col <= row).astype(f32), rate_ref[...] * step, 1, 0, HI)
    step_ref[...] = step
    run_ref[...] = run
    run_t = run.T
    mask = span_masks(segc_ref, segr_ref)
    xc = v_ref[:, :W]
    b_low = v_ref[:, W : W + N].astype(bf)
    c_low = v_ref[:, W + N :].astype(bf)
    gram = dot(c_low, b_low, 1, 1)
    xs = (by_lanes(step) * xc).astype(bf)
    half = lane < HP
    for p in range(PAIRS):
        cols = slice(p * 128, (p + 1) * 128)
        out = [
            dot((gram * head_decay(mask, run, run_t, h)).astype(bf), xs[:, cols], 1, 0)
            for h in (2 * p, 2 * p + 1)
        ]
        within_ref[:, cols] = jnp.where(half, out[0], out[1])
    w_end = end_weights(run, segc_ref, seg_ref[1, k])
    weighted = (by_lanes(w_end * step) * xc).astype(bf)
    own = dot(weighted, b_low, 0, 0)
    local_ref[0] = acc_ref[...]
    before_ref[0] = dec_ref[...]
    inside = (seg_ref[1, k] == seg_ref[0, k]).astype(f32)
    decay = jnp.exp(run[SPAN - 1 :]) * inside
    decay_ref[0] = decay
    acc = by_rows(decay, acc_ref[...]) + own
    acc_ref[...] = acc
    dec = dec_ref[...] * decay
    dec_ref[...] = dec

    @pl.when(k == LAST)
    def _():
        write_states(sent_ref, acc, dec)


def silu_both(v):
    s = 1.0 / (1.0 + jnp.exp(-v))
    return v * s, s * (1.0 + v * (1.0 - s))


def gate_kernel(
    last, seg_ref, back_ref, local_ref, before_ref, run_ref, v_ref, within_ref, z_ref, segc_ref,
    skip_ref, wo_ref, *rest,
):
    if last:
        grad_ref, y0_ref, part_ref, sums_ref, carry_ref = rest
    else:
        y0_ref, part_ref, sums_ref, carry_ref = rest
    k = pl.program_id(0)

    @pl.when(k == 0)
    def _():
        carry_ref[...] = read_states(back_ref)

    carried = (by_rows(before_ref[0], carry_ref[...]) + local_ref[0]).astype(bf)
    xc = v_ref[:, :W]
    c_low = v_ref[:, W + N :].astype(bf)
    reading = dot(c_low, carried, 1, 1)
    y0 = within_ref[...] + by_lanes(inflow_of(run_ref[...], segc_ref, seg_ref[0, k])) * reading
    y0_ref[...] = y0
    mixed = (y0 + skip_ref[...] * xc).astype(bf).astype(f32)
    gated = mixed * silu_both(z_ref[...])[0]
    part_ref[...] = dot(gated.astype(bf), wo_ref[...], 1, 0).astype(bf)
    sums = token_sums(gated * gated)
    if last:
        d_q = dot(grad_ref[...], wo_ref[...], 1, 1)
        row = lax.broadcasted_iota(jnp.int32, (8, SPAN), 0)
        sums = jnp.where(row < 1, sums, token_sums(gated * d_q))
    sums_ref[...] = sums


def gate_back_kernel(
    seg_ref, grad_ref, wo_ref, scale_ref, v_ref, y0_ref, z_ref, run_ref, segc_ref, skip_ref,
    decay_ref, dy_ref, dz_ref, gr_ref, local_ref, after_ref, sent_ref, acc_ref, dec_ref,
):
    i = pl.program_id(0)
    k = LAST - i

    @pl.when(i == 0)
    def _():
        acc_ref[...] = jnp.zeros_like(acc_ref)
        dec_ref[...] = jnp.ones_like(dec_ref)

    scales = scale_ref[...].T
    r, kappa = scales[:, 0:1], scales[:, 1:2]
    d_q = dot(grad_ref[...], wo_ref[...], 1, 1)
    mixed = (y0_ref[...] + skip_ref[...] * v_ref[:, :W]).astype(bf).astype(f32)
    silu, d_silu = silu_both(z_ref[...])
    gated = mixed * silu
    gr_ref[...] = (r * gated).astype(bf)
    d_gated = r * d_q - kappa * gated
    dy = (d_gated * silu).astype(bf)
    dy_ref[...] = dy
    dz_ref[...] = (d_gated * mixed * d_silu).astype(bf)
    inflow = by_lanes(inflow_of(run_ref[...], segc_ref, seg_ref[0, k]))
    scaled = (inflow * dy.astype(f32)).astype(bf)
    d_carried = dot(scaled, v_ref[:, W + N :].astype(bf), 0, 0)
    local_ref[0] = acc_ref[...]
    after_ref[0] = dec_ref[...]
    decay = decay_ref[0]
    acc = by_rows(decay, acc_ref[...]) + d_carried
    acc_ref[...] = acc
    dec = dec_ref[...] * decay
    dec_ref[...] = dec

    @pl.when(i == LAST)
    def _():
        write_states(sent_ref, acc, dec)


def mix_back_kernel(v_ref, step_ref, run_ref, segc_ref, segr_ref, dy_ref, dxs_ref, dbc_ref):
    lane = lax.broadcasted_iota(jnp.int32, (SPAN, 128), 1)
    half = lane < HP
    run = run_ref[...]
    run_t = run.T
    mask = span_masks(segc_ref, segr_ref)
    xs = (by_lanes(step_ref[...]) * v_ref[:, :W]).astype(bf)
    b_low = v_ref[:, W : W + N].astype(bf)
    c_low = v_ref[:, W + N :].astype(bf)
    gram = dot(c_low, b_low, 1, 1)
    d_gram = jnp.zeros((SPAN, SPAN), f32)
    zero = jnp.zeros((SPAN, 128), bf)
    for p in range(PAIRS):
        cols = slice(p * 128, (p + 1) * 128)
        dy = dy_ref[:, cols]
        out = []
        for i, h in enumerate((2 * p, 2 * p + 1)):
            decay = head_decay(mask, run, run_t, h)
            mixing = (gram * decay).astype(bf)
            dy_one = jnp.where(half, dy, zero) if i == 0 else jnp.where(half, zero, dy)
            d_gram = d_gram + dot(dy_one, xs[:, cols], 1, 1) * decay
            out.append(dot(mixing, dy, 0, 0))
        dxs_ref[:, cols] = jnp.where(half, out[0], out[1])
    d_gram = d_gram.astype(bf)
    dbc_ref[:, :N] = dot(d_gram, c_low, 0, 0)
    dbc_ref[:, N:] = dot(d_gram, b_low, 1, 0)


def end_kernel(
    seg_ref, later_ref, back_ref, local_ref, before_ref, dlocal_ref, after_ref, decay_ref, v_ref,
    pre_ref, raw_ref, bias_ref, rate_ref, step_ref, run_ref, segc_ref, skip_ref, dy_ref, dxs_ref,
    dbc_ref, y0_ref, dpre_ref, draw_ref, sums_ref, later_s, carry_s,
):
    k = pl.program_id(0)

    @pl.when(k == 0)
    def _():
        later_s[...] = read_states(later_ref)
        carry_s[...] = read_states(back_ref)
        sums_ref[...] = jnp.zeros_like(sums_ref)

    d_end = by_rows(after_ref[0], later_s[...]) + dlocal_ref[0]
    carried = by_rows(before_ref[0], carry_s[...]) + local_ref[0]
    d_end_low = d_end.astype(bf)
    run, step, rate = run_ref[...], step_ref[...], rate_ref[...]
    xc = v_ref[:, :W]
    b_low = v_ref[:, W : W + N].astype(bf)
    dy = dy_ref[...].astype(f32)
    dxs = dxs_ref[...]
    step_x = by_lanes(step)
    xs = (step_x * xc).astype(bf).astype(f32)
    w_end = end_weights(run, segc_ref, seg_ref[1, k])
    weights_x = by_lanes(w_end * step)
    weighted = (weights_x * xc).astype(bf)
    scaled = (by_lanes(inflow_of(run, segc_ref, seg_ref[0, k])) * dy).astype(bf)
    d_weighted = dot(b_low, d_end_low, 1, 1)
    d_b = dbc_ref[:, :N] + dot(weighted, d_end_low, 1, 0)
    d_c = dbc_ref[:, N:] + dot(scaled, carried.astype(bf), 1, 0)
    d_xc = skip_ref[...] * dy + step_x * dxs + weights_x * d_weighted
    dv = jnp.concatenate([d_xc, d_b, d_c], axis=1)
    dpre_ref[...] = dv * silu_both(pre_ref[...])[1]
    skip_sum = head_sums(dy * xc)
    d_run = head_sums(dy * y0_ref[...] - xs * dxs)
    d_step = head_sums(xc * dxs)
    d_w = head_sums(d_weighted * xc)
    product = d_end * carried
    ones = jnp.ones((8, N), f32)
    lane8 = lax.broadcasted_iota(jnp.int32, (8, 128), 1)
    d_span = jnp.zeros((8, 128), f32)
    for h in range(HL):
        rows = dot(ones, product[h * HP : (h + 1) * HP], 1, 1, HI)
        d_span = d_span + jnp.where(lane8 == h, jnp.sum(rows, axis=1, keepdims=True), 0.0)
    d_step = d_step + d_w * w_end
    d_ww = d_w * w_end * step
    d_run = d_run - d_ww
    d_last = jnp.sum(d_ww, axis=0, keepdims=True) + d_span[:1] * decay_ref[0]
    row = lax.broadcasted_iota(jnp.int32, (SPAN, SPAN), 0)
    col = lax.broadcasted_iota(jnp.int32, (SPAN, SPAN), 1)
    d_a = dot((col >= row).astype(f32), d_run, 1, 0, HI) + d_last
    d_step = d_step + rate * d_a
    raw = raw_ref[...].astype(f32) + bias_ref[...]
    lane = lax.broadcasted_iota(jnp.int32, (SPAN, 128), 1)
    d_raw = jnp.where(lane < HL, d_step / (1.0 + jnp.exp(-raw)), 0.0)
    draw_ref[...] = d_raw.astype(bf)
    sums = jnp.concatenate(
        [
            jnp.sum(d_raw, axis=0, keepdims=True),
            rate * jnp.sum(step * d_a, axis=0, keepdims=True),
            jnp.sum(skip_sum, axis=0, keepdims=True),
            jnp.zeros((5, 128), f32),
        ],
        axis=0,
    )
    sums_ref[...] = sums_ref[...] + sums


def tok_block(n, reverse=False):
    return pl.BlockSpec((SPAN, n), lambda k: (LAST - k if reverse else k, 0))


def span_block(rows, n, reverse=False):
    return pl.BlockSpec((1, rows, n), lambda k: (LAST - k if reverse else k, 0, 0))


def whole(*shape):
    return pl.BlockSpec(shape, lambda k: (0,) * len(shape))


STATE = struct((NS, W, N))
ROW = struct((NS, 1, 128))
SENT = struct((NQ, 32, N), bf)
STATE_SCRATCH = pltpu.VMEM((W, N), f32)


def call(kernel, name, ins, outs, shapes, scratch, args, us):
    return pl.pallas_call(
        kernel,
        grid=(NS,),
        in_specs=ins,
        out_specs=outs,
        out_shape=shapes,
        scratch_shapes=scratch,
        compiler_params=pltpu.CompilerParams(
            dimension_semantics=("arbitrary",), vmem_limit_bytes=60 * 1024 * 1024
        ),
        cost_estimate=pl.CostEstimate(
            flops=int(us * 8e8), bytes_accessed=int(us * 3e6), transcendentals=0
        ),
        name=name,
    )(*args)


def span_mix(seg, v, raw, bias, rate, segc, segr):
    return call(
        mix_kernel,
        "span_mix",
        [SMEM, tok_block(CC), tok_block(128), whole(1, 128), whole(1, 128), tok_block(1),
         span_block(1, SPAN)],
        [tok_block(W), span_block(W, N), tok_block(128), tok_block(128), span_block(1, 128),
         span_block(1, 128), whole(NQ, 32, N)],
        [struct((GT, W)), STATE, struct((GT, 128)), struct((GT, 128)), ROW, ROW, SENT],
        [STATE_SCRATCH, pltpu.VMEM((1, 128), f32)],
        (seg, v, raw, bias, rate, segc, segr),
        12,
    )


def span_gate(seg, back, local, before, run, v, within, z, segc, skip, wo, grad):
    last = grad is not None
    ins = [SMEM, whole(NQ, 32, N), span_block(W, N), span_block(1, 128), tok_block(128),
           tok_block(CC), tok_block(W), tok_block(W), tok_block(1), whole(1, W), whole(W, D)]
    args = (seg, back, local, before, run, v, within, z, segc, skip, wo)
    return call(
        functools.partial(gate_kernel, last),
        "span_gate",
        ins + [tok_block(D)] if last else ins,
        [tok_block(W), tok_block(D), pl.BlockSpec((8, SPAN), lambda k: (0, k))],
        [struct((GT, W)), struct((GT, D), bf), struct((8, GT))],
        [STATE_SCRATCH],
        args + (grad,) if last else args,
        10,
    )


def span_gate_back(seg, grad, wo, scales, v, y0, z, run, segc, skip, decay):
    return call(
        gate_back_kernel,
        "span_gate_back",
        [SMEM, tok_block(D, True), whole(W, D), pl.BlockSpec((8, SPAN), lambda k: (0, LAST - k)),
         tok_block(CC, True), tok_block(W, True), tok_block(W, True), tok_block(128, True),
         tok_block(1, True), whole(1, W), span_block(1, 128, True)],
        [tok_block(W, True), tok_block(W, True), tok_block(W, True), span_block(W, N, True),
         span_block(1, 128, True), whole(NQ, 32, N)],
        [struct((GT, W), bf), struct((GT, W), bf), struct((GT, W), bf), STATE, ROW, SENT],
        [STATE_SCRATCH, pltpu.VMEM((1, 128), f32)],
        (seg, grad, wo, scales, v, y0, z, run, segc, skip, decay),
        12,
    )


def span_mix_back(v, step, run, segc, segr, dy):
    return call(
        mix_back_kernel,
        "span_mix_back",
        [tok_block(CC), tok_block(128), tok_block(128), tok_block(1), span_block(1, SPAN),
         tok_block(W)],
        [tok_block(W), tok_block(2 * N)],
        [struct((GT, W)), struct((GT, 2 * N))],
        [],
        (v, step, run, segc, segr, dy),
        14,
    )


def span_end(seg, later, back, local, before, dlocal, after, decay, v, pre, raw, bias, rate, step,
             run, segc, skip, dy, dxs, dbc, y0):
    return call(
        end_kernel,
        "span_end",
        [SMEM, whole(NQ, 32, N), whole(NQ, 32, N), span_block(W, N), span_block(1, 128),
         span_block(W, N), span_block(1, 128), span_block(1, 128), tok_block(CC), tok_block(CC),
         tok_block(128), whole(1, 128), whole(1, 128), tok_block(128), tok_block(128),
         tok_block(1), whole(1, W), tok_block(W), tok_block(W), tok_block(2 * N), tok_block(W)],
        [tok_block(CC), tok_block(128), whole(8, 128)],
        [struct((GT, CC)), struct((GT, 128), bf), struct((8, 128))],
        [STATE_SCRATCH, STATE_SCRATCH],
        (seg, later, back, local, before, dlocal, after, decay, v, pre, raw, bias, rate, step, run,
         segc, skip, dy, dxs, dbc, y0),
        16,
    )


SMALL = CC + HL


def small_block(conv_grads, head_grads):
    own_ch = CH // (NQ * NG)
    conv = jnp.stack(conv_grads).reshape(LAYERS * (CONV + 1), NQ * NG, own_ch)
    conv = jnp.pad(conv.transpose(1, 0, 2), ((0, 0), (0, 12 - LAYERS * (CONV + 1)), (0, 0)))
    head = jnp.stack(head_grads, axis=1)
    high = rounded(head)
    head = jnp.concatenate([high, head - high], axis=1)
    head = jnp.tile(head, (NQ * NG // 2, 1, 1))
    head = jnp.pad(head, ((0, 0), (0, 12 - 2 * LAYERS), (0, 0)))
    block = jnp.concatenate([conv, head], axis=2).reshape(D, own_ch + 3 * H // 2)
    return jnp.pad(block.astype(bf), ((0, 0), (SMALL, CA - SMALL - block.shape[1])))


def per_device(
    tokens,
    doc_starts,
    norm_gain,
    in_weight,
    conv_weight,
    conv_bias,
    step_bias,
    decay_log,
    skip_gain,
    gate_gain,
    out_weight,
    cotangent,
):
    q = lax.axis_index(ZX)
    yh, core, yl = lax.axis_index("yh"), lax.axis_index("c"), lax.axis_index("yl")
    sub = yh * 2 + core
    group = yl * 4 + sub

    own_ch = CH // (NQ * NG)
    conv_own = jnp.concatenate([conv_weight, conv_bias[:, None]], axis=1).reshape(-1, own_ch)
    conv_own = jnp.pad(conv_own, ((0, 12 - conv_own.shape[0]), (0, 0)))
    sent = [in_blocks(in_weight[l], norm_gain[l], conv_own if l == 0 else conv_own[:, :0]) for l in range(LAYERS)]
    got = a2a(jnp.stack(sent, axis=1), LINE)
    got, tokens, out_weight = tie(got, tokens, out_weight)
    in_0 = got[:, 0].reshape(NG * 12, CA + W)
    in_1 = got[:, 1].reshape(NG * 12, CA + W)
    folded_out = (out_weight.astype(f32) * gate_gain.astype(f32)[:, :, None]).astype(bf)
    out_blocks = lax.ppermute(folded_out, AX, TO_HEADS)
    w_a0 = group_gather_now(in_0[:, :CA])
    conv_all = w_a0[:, W + 2 * N + HL : W + 2 * N + HL + own_ch].reshape(NQ * NG, 12, own_ch)
    conv_all = conv_all[:, : LAYERS * (CONV + 1)].transpose(1, 0, 2)
    conv_all = conv_all.reshape(LAYERS, CONV + 1, CH).astype(f32)
    conv_x = lax.dynamic_slice_in_dim(conv_all, group * W, W, 2)
    conv_here = jnp.concatenate([conv_x, conv_all[:, :, DI:]], axis=2)
    w_z0 = group_gather_now(in_0[:, CA:])
    w_o = [group_gather(out_blocks[l]) for l in range(LAYERS)]
    w_in1 = group_gather(in_1)

    pos = q * GT + jnp.arange(-(CONV - 1), GT + CONV - 1, dtype=jnp.int32)
    seg_ext = jnp.sum((doc_starts[None, :] <= pos[:, None]).astype(jnp.int32), axis=1) - 1
    seg = seg_ext[CONV - 1 : CONV - 1 + GT]
    seg_spans = seg.reshape(NS, SPAN)
    seg_before = seg_ext[CONV - 2 : CONV - 2 + GT : SPAN]
    seg_ends = jnp.stack([seg_before, seg_spans[:, -1]])
    seg_col, seg_row = seg[:, None], seg_spans[:, None, :]
    same_back = [
        (seg_ext[CONV - 1 - k : CONV - 1 - k + GT] == seg).astype(f32)[:, None] for k in range(CONV)
    ]
    same_fwd = [
        (seg_ext[CONV - 1 + k : CONV - 1 + k + GT] == seg).astype(f32)[:, None] for k in range(CONV)
    ]

    def pick_heads(a):
        own = lax.dynamic_slice_in_dim(a, sub * HL, HL, 0)
        return jnp.pad(own, (0, 128 - HL))[None]

    h = tokens.astype(f32)
    saved = []
    cot_late, w_a0 = tie(cotangent, w_a0)
    grad_full = line_gather(cot_late)

    for l in range(LAYERS):
        bias_h = pick_heads(step_bias[l])
        rate = jnp.where(jnp.arange(128)[None] < HL, -jnp.exp(pick_heads(decay_log[l])), 0.0)
        skip_x = jnp.repeat(lax.dynamic_slice_in_dim(skip_gain[l], sub * HL, HL, 0), HP)[None]
        r_in = lax.rsqrt(jnp.mean(h * h, axis=-1, keepdims=True) + EPS)
        normed = line_gather((h * r_in).astype(bf))
        proj = mm(normed, w_a0 if l == 0 else w_in1)
        u = proj[:, :CC].astype(bf)
        raw = proj[:, CC:CA].astype(bf)
        edge = lax.ppermute(u[GT - (CONV - 1) :], ZX, [(i, i + 1) for i in range(NQ - 1)])
        z = mm(normed, w_z0) if l == 0 else proj[:, CA:]
        ext = jnp.concatenate([edge, u], axis=0).astype(f32)
        cw = conv_here[l]
        pre = jnp.broadcast_to(cw[CONV][None], (GT, W + 2 * N))
        for k in range(CONV):
            pre = pre + cw[k][None] * ext[CONV - 1 - k : CONV - 1 - k + GT] * same_back[k]
        v = pre * jax.nn.sigmoid(pre)
        within, local, step, run, before, decay, sent = span_mix(
            seg_ends, v, raw, bias_h, rate, seg_col, seg_row
        )
        if l == 0:
            sent, w_z0 = tie(sent, w_z0)
        back = exclusive_scan(sent, False)
        if l == 0:
            back, grad_full, w_o[0] = tie(back, grad_full, w_o[0])
        y0, part, sums = span_gate(
            seg_ends, back, local, before, run, v, within, z, seg_col, skip_x, w_o[l],
            grad_full if l == LAYERS - 1 else None,
        )
        total = line_reduce(part)
        if l == LAYERS - 1:
            sums = small_sum(sums[:2])
            r_all = lax.rsqrt(sums[0] / DI + EPS)
            gate_scales = jnp.stack([r_all, r_all * r_all * r_all * sums[1] / DI])
            r_gate = lax.dynamic_slice_in_dim(r_all, (line_index() // 2 * 4 + core * 2 + yl) * TOK, TOK, 0)
        else:
            gate_scales = None
            total, square, w_in1, w_o[1] = tie(total, small_reduce(sums[:1])[0], w_in1, w_o[1])
            r_gate = lax.rsqrt(square / DI + EPS)
        branch = total * r_gate[:, None]
        saved.append(
            dict(
                h=h, r_in=r_in, normed=normed, ext=ext, pre=pre, v=v, z=z, raw=raw, bias_h=bias_h,
                rate=rate, skip_x=skip_x, step=step, run=run, before=before, decay=decay,
                local=local, back=back, y0=y0, r_gate=r_gate, branch=branch,
                gate_scales=gate_scales,
            )
        )
        h = h + branch
    output = h.astype(bf)

    grad = cotangent.astype(f32)
    in_grads, gain_grads, out_grads, gate_grads = ([None] * LAYERS for _ in range(4))
    conv_grads, head_grads = [None] * LAYERS, [None] * LAYERS
    in_sums, out_sums = [None] * LAYERS, [None] * LAYERS
    for l in reversed(range(LAYERS)):
        s = saved[l]
        if l == LAYERS - 1:
            gate_scales = s["gate_scales"]
        else:
            grad_low = grad.astype(bf)
            inner = jnp.sum(grad_low.astype(f32) * s["branch"], axis=1)
            kappa = s["r_gate"] * s["r_gate"] * inner / DI
            extra = jnp.concatenate(three_parts(s["r_gate"]) + three_parts(kappa))
            extra = jnp.pad(extra[None], ((0, 15), (0, D - 6 * TOK)))
            grad_full, extra = line_gather(jnp.concatenate([grad_low, extra], axis=0))
            extra = extra.reshape(NG, 16, D)[:, 0, : 6 * TOK].reshape(NG, 2, 3, TOK).astype(f32)
            gate_scales = jnp.sum(extra, axis=2).transpose(1, 0, 2).reshape(2, GT)
            grad_full, in_sums[1] = tie(grad_full, in_sums[1])
        scales = jnp.pad(gate_scales, ((0, 6), (0, 0)))
        dy, dz, gr, dlocal, after, sent = span_gate_back(
            seg_ends, grad_full, w_o[l], scales, s["v"], s["y0"], s["z"], s["run"], seg_col,
            s["skip_x"], s["decay"],
        )
        later = exclusive_scan(sent, True)
        later, dz, gr = tie(later, dz, gr)
        if l == LAYERS - 1:
            later, output = tie(later, output)
        else:
            z_sum = group_reduce(mm(s["normed"], dz, 0, 0).astype(bf))
        out_sum = group_reduce(mm(gr, grad_full, 0, 0).astype(bf))
        dxs, dbc = span_mix_back(s["v"], s["step"], s["run"], seg_col, seg_row, dy)
        d_pre, d_raw, head_sum = span_end(
            seg_ends, later, s["back"], s["local"], s["before"], dlocal, after, s["decay"], s["v"],
            s["pre"], s["raw"], s["bias_h"], s["rate"], s["step"], s["run"], seg_col, s["skip_x"],
            dy, dxs, dbc, s["y0"],
        )
        if l == LAYERS - 1:
            d_pre, out_sum = tie(d_pre, out_sum)
        edge = lax.ppermute(d_pre[: CONV - 1], ZX, [(i + 1, i) for i in range(NQ - 1)])
        d_ext = jnp.concatenate([d_pre, edge], axis=0)
        cw = conv_here[l]
        du = jnp.zeros_like(d_pre)
        taps = []
        for k in range(CONV):
            du = du + cw[k][None] * d_ext[k : k + GT] * same_fwd[k]
            past = s["ext"][CONV - 1 - k : CONV - 1 - k + GT]
            taps.append(jnp.sum(d_pre * past * same_back[k], axis=0))
        taps.append(jnp.sum(d_pre, axis=0))
        taps = jnp.stack(taps)
        conv_full = jnp.zeros((CONV + 1, CH), f32)
        conv_full = lax.dynamic_update_slice_in_dim(conv_full, taps[:, :W], group * W, 1)
        conv_grads[l] = conv_full.at[:, DI:].set(taps[:, W:])
        head_full = lax.dynamic_update_slice_in_dim(
            jnp.zeros((3, H), f32), head_sum[:3, :HL], group * HL, 1
        )
        head_grads[l] = head_full.reshape(3, 2, H // 2).transpose(1, 0, 2).reshape(2, 3 * H // 2)
        da = jnp.concatenate([du.astype(bf), d_raw], axis=1)
        if l == 0:
            small = small_block(conv_grads, head_grads)
            a_part = mm(s["normed"], da, 0, 0) + small.astype(f32)
            in_sum = jnp.concatenate([group_reduce(a_part.astype(bf)), z_sum], axis=1)
            d_norm = line_reduce(mm(da, w_a0, 1, 1) + mm(dz, w_z0, 1, 1))
        else:
            da = jnp.concatenate([da, dz], axis=1)
            d_norm = line_reduce(mm(da, w_in1, 1, 1))
            in_sum = group_reduce(mm(s["normed"], da, 0, 0).astype(bf))
        hidden, r_in = s["h"], s["r_in"]
        inner = jnp.mean(hidden * d_norm, axis=1, keepdims=True)
        grad = grad + r_in * d_norm - hidden * (r_in * r_in * r_in) * inner
        in_sums[l], out_sums[l] = in_sum, out_sum

    for l in reversed(range(LAYERS)):
        both = in_sums[l].reshape(NG, 12, CA + W)
        both = a2a(both, LINE)
        if l == 0:
            small = jnp.sum(both[:, :, SMALL:CA], axis=0)
        g_in = jnp.concatenate(
            [
                heads_in(both[:, :, CA:]),
                heads_in(both[:, :, :W]),
                jnp.sum(both[:, :, W : W + 2 * N], axis=0),
                heads_in(both[:, :, W + 2 * N : W + 2 * N + HL]),
            ],
            axis=1,
        )
        in_grads[l] = g_in * norm_gain[l].astype(f32)[:, None]
        gain_grads[l] = jnp.sum(g_in * in_weight[l].astype(f32), axis=1)
        g_out = lax.ppermute(out_sums[l], AX, TO_OWNER)
        out_grads[l] = g_out * gate_gain[l].astype(f32)[:, None]
        gate_grads[l] = jnp.sum(g_out * out_weight[l].astype(f32), axis=1)

    conv_grad = small[: LAYERS * (CONV + 1), :own_ch].reshape(LAYERS, CONV + 1, own_ch)
    head_grad = small[:LAYERS] + small[LAYERS : 2 * LAYERS]
    head_grad = head_grad[:, own_ch : own_ch + 3 * H // 2].reshape(LAYERS, 3, H // 2)
    return (
        output,
        grad,
        jnp.stack(gain_grads),
        jnp.stack(in_grads),
        conv_grad[:, :CONV],
        conv_grad[:, CONV],
        head_grad[:, 0],
        head_grad[:, 1],
        head_grad[:, 2],
        jnp.stack(gate_grads),
        jnp.stack(out_grads),
    )


def solution(mesh):
    fine = Mesh(mesh.devices.reshape(4, 4, 2, 2, 2), AX)
    tok, last, mid, heads = P(AX, None), P(None, AX), P(None, AX, None), P(None, "yl")
    conv = P(None, None, AX)
    return jax.shard_map(
        per_device,
        mesh=fine,
        in_specs=(tok, P(), last, mid, conv, last, heads, heads, heads, last, mid, tok),
        out_specs=(tok, tok, last, mid, conv, last, heads, heads, heads, last, mid),
        check_vma=False,
    )
```

```python
import functools

import jax
import jax.numpy as jnp
from jax import lax
from jax.experimental import pallas as pl
from jax.experimental.pallas import tpu as pltpu
from jax.sharding import Mesh, PartitionSpec as P

D = 1536
DI = 3072
H = 48
HP = 64
N = 128
CONV = 4
LAYERS = 2
CH = DI + 2 * N
EPS = 1e-05

AX = ("z", "x", "yh", "c", "yl")
ZX = ("z", "x")
LINE = ("yh", "c", "yl")
Y = ("yh", "yl")
NQ = 16
NG = 8
TOK = 128
GT = TOK * NG
SPAN = 256
NS = GT // SPAN
HL = H // NG
W = HL * HP
CC = W + 2 * N
CA = CC + 128

bf = jnp.bfloat16
f32 = jnp.float32
HI = lax.Precision.HIGHEST


SMEM = pl.BlockSpec(memory_space=pltpu.SMEM)


def struct(shape, dtype=f32):
    return jax.ShapeDtypeStruct(shape, dtype)


def mm(a, b, ca=1, cb=0):
    return lax.dot_general(a, b, (((ca,), (cb,)), ((), ())), preferred_element_type=f32)


def a2a(a, axes):
    return lax.all_to_all(a, axes, 0, 0, tiled=True)


def core_swap(a):
    return lax.ppermute(a, "c", [(0, 1), (1, 0)])


def line_index():
    return lax.axis_index("yh") * 2 + lax.axis_index("yl")


def along_line(a, distance):
    return lax.ppermute(a, Y, [(i, (i + distance) % 4) for i in range(4)])


def fill_places(pos_ref, blocks, x_ref):
    for i, block in enumerate(blocks):
        at = pl.multiple_of(pos_ref[i] * TOK, TOK)
        x_ref[pl.ds(at, TOK)] = block[:TOK]


def place_kernel(pos_ref, *refs):
    blocks, (out_ref, extra_ref, x_ref) = refs[:NG], refs[NG:]
    k = pl.program_id(0)

    @pl.when(k == 0)
    def _():
        fill_places(pos_ref, blocks, x_ref)
        for i, block in enumerate(blocks):
            extra_ref[pl.ds(pl.multiple_of(pos_ref[i] * 16, 16), 16)] = block[TOK:]

    out_ref[...] = x_ref[pl.ds(pl.multiple_of(k * SPAN, SPAN), SPAN)]


def place_plain_kernel(pos_ref, *refs):
    blocks, (out_ref, x_ref) = refs[:NG], refs[NG:]
    k = pl.program_id(0)

    @pl.when(k == 0)
    def _():
        fill_places(pos_ref, blocks, x_ref)

    out_ref[...] = x_ref[pl.ds(pl.multiple_of(k * SPAN, SPAN), SPAN)]


def place_project_kernel(pos_ref, *refs):
    blocks, (w_ref, out_ref, u_ref, raw_ref, x_ref) = refs[:NG], refs[NG:]
    k = pl.program_id(0)

    @pl.when(k == 0)
    def _():
        fill_places(pos_ref, blocks, x_ref)

    x = x_ref[pl.ds(pl.multiple_of(k * SPAN, SPAN), SPAN)]
    out_ref[...] = x
    project = jnp.dot(x, w_ref[...], preferred_element_type=f32).astype(bf)
    u_ref[...] = project[:, :CC]
    raw_ref[...] = project[:, CC:]


def line_blocks(own, first=None):
    y, core = line_index(), lax.axis_index("c")
    blocks, places = [], []

    def place(distance, c):
        at = (y - distance) % 4
        return (at // 2) * 4 + c * 2 + at % 2

    for d in (0, 1, 3, 2):
        got = along_line(own, d) if d else own
        if d and first is not None:
            got = wait_for(got, first)
        blocks += [got, core_swap(got)]
        places += [place(d, core), place(d, 1 - core)]
    return jnp.stack(places).astype(jnp.int32), blocks


X_SCRATCH = pltpu.VMEM((GT, D), bf)


def place_tokens(places, blocks):
    return call(
        place_plain_kernel,
        "place_tokens",
        [SMEM] + [whole(TOK, D)] * NG,
        tok_block(D),
        struct((GT, D), bf),
        [X_SCRATCH],
        (places, *blocks),
        4,
    )


def line_gather_more(own, first):
    places, blocks = line_blocks(own, first)
    return call(
        place_kernel,
        "place_gradient",
        [SMEM] + [whole(TOK + 16, D)] * NG,
        [tok_block(D), whole(NG * 16, D)],
        [struct((GT, D), bf), struct((NG * 16, D), bf)],
        [X_SCRATCH],
        (places, *blocks),
        4,
    )


def line_project(own, weight):
    return place_project(*line_blocks(own), weight)


def place_project(places, blocks, weight):
    return call(
        place_project_kernel,
        "place_project",
        [SMEM] + [whole(TOK, D)] * NG + [whole(D, CA)],
        [tok_block(D), tok_block(CC), tok_block(128)],
        [struct((GT, D), bf), struct((GT, CC), bf), struct((GT, 128), bf)],
        [X_SCRATCH],
        (places, *blocks, weight),
        9,
    )


def chip_kernel(y_ref, mine_ref, got_ref, own_ref, *sent_refs):
    def rows(distance):
        at = pl.multiple_of((y_ref[0] + distance) % 4 * TOK, TOK)
        return mine_ref[pl.ds(at, TOK)].astype(f32) + got_ref[pl.ds(at, TOK)].astype(f32)

    own_ref[...] = rows(0)
    for distance, ref in zip((1, 3, 2), sent_refs):
        ref[...] = rows(distance).astype(bf)


def line_parts(other, mine, first=None):
    got = core_swap(other)
    if first is not None:
        got = wait_for(got, first)
    own, *sent = pl.pallas_call(
        chip_kernel,
        out_shape=[struct((TOK, D))] + [struct((TOK, D), bf)] * 3,
        in_specs=[SMEM] + [pl.BlockSpec(memory_space=pltpu.VMEM)] * 2,
        out_specs=[pl.BlockSpec(memory_space=pltpu.VMEM)] * 4,
        compiler_params=pltpu.CompilerParams(vmem_limit_bytes=60 * 1024 * 1024),
        name="chip_sum",
    )(line_index().reshape(1).astype(jnp.int32), mine, got)
    return [own] + [along_line(block, d) for block, d in zip(sent, (1, 3, 2))]


def span_order():
    core = lax.axis_index("c")
    return jnp.stack([1 - core, 3 - core, core, 2 + core]).astype(jnp.int32)


def write_half(other_ref, mine_ref, value):
    i = pl.program_id(0)

    @pl.when(i < 2)
    def _():
        other_ref[...] = value

    @pl.when(i >= 2)
    def _():
        mine_ref[...] = value


def parts_sum(refs):
    total = refs[0][...]
    for ref in refs[1:]:
        total = total + ref[...].astype(f32)
    return total


def inverse_rms(a):
    return lax.rsqrt(jnp.mean(a * a, axis=1, keepdims=True) + EPS)


def advance_kernel(p0, p1, p2, p3, square_ref, h_ref, out_ref, branch_ref, normed_ref, scale_ref):
    square = jnp.sum(square_ref[...], axis=0, keepdims=True)
    r_gate = jnp.broadcast_to(lax.rsqrt(square / DI + EPS), (8, TOK))
    scale_ref[...] = r_gate
    branch = parts_sum((p0, p1, p2, p3)) * r_gate.T[:, 0:1]
    h = h_ref[...] + branch
    out_ref[...] = h
    branch_ref[...] = branch
    normed_ref[...] = (h * inverse_rms(h)).astype(bf)


def in_parts(row):
    hi = row.astype(bf).astype(f32)
    mid = (row - hi).astype(bf).astype(f32)
    return [hi, mid, row - hi - mid]


def retreat_kernel(extra, p0, p1, p2, p3, h_ref, grad_ref, *refs):
    h = h_ref[...]
    r_in = inverse_rms(h)
    d_norm = parts_sum((p0, p1, p2, p3))
    inner = jnp.mean(h * d_norm, axis=1, keepdims=True)
    grad = grad_ref[...].astype(f32) + r_in * d_norm - h * (r_in * r_in * r_in * inner)
    if not extra:
        refs[0][...] = grad
        return
    branch_ref, scale_ref, out_ref, sent_ref = refs
    out_ref[...] = grad
    low = grad.astype(bf)
    r_gate = scale_ref[...]
    column = jnp.sum(low.astype(f32) * branch_ref[...], axis=1, keepdims=True)
    row = jnp.broadcast_to(column, (TOK, 128)).T[:8]
    kappa = r_gate * r_gate * row / DI
    rows = in_parts(r_gate) + in_parts(kappa)
    rows = jnp.concatenate(rows + [jnp.zeros((8, D - 6 * TOK), f32)], axis=1)
    sent_ref[:TOK] = low
    sent_ref[TOK:] = jnp.concatenate([rows, jnp.zeros((8, D), f32)], axis=0).astype(bf)


def plain_call(kernel, name, shapes, args):
    return pl.pallas_call(
        kernel,
        out_shape=shapes,
        compiler_params=pltpu.CompilerParams(vmem_limit_bytes=60 * 1024 * 1024),
        cost_estimate=pl.CostEstimate(
            flops=int(2e8), bytes_accessed=int(1e6), transcendentals=0
        ),
        name=name,
    )(*args)


def to_owners(row):
    return a2a(row.reshape(NG, TOK), LINE)


def to_line(rows):
    m = rows.shape[0]
    return a2a(jnp.broadcast_to(rows[None], (NG,) + rows.shape), LINE).reshape(NG * m, GT)


def rounded(a):
    return lax.reduce_precision(a, exponent_bits=8, mantissa_bits=7)


def group_gather(block):
    return lax.all_gather(block, ZX, axis=0, tiled=True)


def group_gather_now(block):
    r, n = block.shape
    return a2a(jnp.broadcast_to(block[None], (NQ, r, n)), ZX).reshape(NQ * r, n)


def wait_for(value, *others):
    return lax.optimization_barrier((value, others))[0]


def group_reduce(full):
    r = full.shape[0] // NQ
    return jnp.sum(a2a(full.reshape(NQ, r, full.shape[1]), ZX).astype(f32), axis=0)


def heads_out(cols, width):
    r = cols.shape[0]
    return cols.reshape(r, 2, 2, 2, width).transpose(2, 3, 1, 0, 4).reshape(NG, r, width)


def heads_in(blocks):
    _, r, width = blocks.shape
    return blocks.reshape(2, 2, 2, r, width).transpose(3, 2, 0, 1, 4).reshape(r, NG * width)


def line_of(group):
    yl, yh, c = group // 4, (group // 2) % 2, group % 2
    return yh * 4 + c * 2 + yl


TO_HEADS = [(s, (s % NQ) * NG + line_of(s // NQ)) for s in range(NQ * NG)]
TO_OWNER = [(b, a) for a, b in TO_HEADS]


def in_blocks(weight, gain, extra):
    folded = (weight.astype(f32) * gain.astype(f32)[:, None]).astype(bf)
    z = heads_out(folded[:, :DI], W)
    x = heads_out(folded[:, DI : 2 * DI], W)
    bc = jnp.broadcast_to(folded[None, :, 2 * DI : 2 * DI + 2 * N], (NG, 12, 2 * N))
    step = heads_out(folded[:, 2 * DI + 2 * N :], HL)
    extra = jnp.broadcast_to(extra[None], (NG,) + extra.shape)
    step = jnp.concatenate([step, extra], axis=2)
    step = jnp.pad(step, ((0, 0), (0, 0), (0, 128 - step.shape[2])))
    return jnp.concatenate([x, bc, step, z], axis=2)


SCAN_ROWS = HL * HP // NQ


def scan_kernel(reverse, q_ref, got_ref, out_ref):
    row = q_ref[0] * SCAN_ROWS + lax.broadcasted_iota(jnp.int32, (SCAN_ROWS, N), 0)
    lane = lax.broadcasted_iota(jnp.int32, (SCAN_ROWS, N), 1)
    head = jnp.zeros((SCAN_ROWS, N), jnp.int32)
    for k in range(1, HL):
        head = head + (row >= k * HP).astype(jnp.int32)
    chosen = (lane == head) | (lane == head + HL) | (lane == head + 2 * HL)
    carry = jnp.zeros((SCAN_ROWS, N), f32)
    pad = jnp.zeros((32 - SCAN_ROWS, N), f32)
    for j in range(NQ - 1, -1, -1) if reverse else range(NQ):
        out_ref[j] = jnp.concatenate([carry, pad], axis=0).astype(bf)
        block = got_ref[j].astype(f32)
        decay = jnp.sum(
            jnp.where(chosen, block[SCAN_ROWS : SCAN_ROWS + 1], 0.0), axis=1, keepdims=True
        )
        carry = decay * carry + block[:SCAN_ROWS]


def exclusive_scan(sent, reverse, first, second):
    q = lax.axis_index(ZX)
    got = a2a(sent, ZX)
    if first is not None:
        got = wait_for(got, first)
    outs = pl.pallas_call(
        functools.partial(scan_kernel, reverse),
        out_shape=jax.ShapeDtypeStruct((NQ, 32, N), bf),
        in_specs=[
            pl.BlockSpec(memory_space=pltpu.SMEM),
            pl.BlockSpec(memory_space=pltpu.VMEM),
        ],
        out_specs=pl.BlockSpec(memory_space=pltpu.VMEM),
        name="group_scan",
    )(q.reshape(1).astype(jnp.int32), got)
    return wait_for(a2a(outs, ZX), second)


PAIRS = HL // 2
LAST = NS - 1


def dot(a, b, ca, cb, precision=None):
    return lax.dot_general(
        a, b, (((ca,), (cb,)), ((), ())), preferred_element_type=f32, precision=precision
    )


def by_lanes(cols):
    lane = lax.broadcasted_iota(jnp.int32, (cols.shape[0], 128), 1)
    return jnp.concatenate(
        [
            jnp.where(lane < HP, cols[:, 2 * p : 2 * p + 1], cols[:, 2 * p + 1 : 2 * p + 2])
            for p in range(PAIRS)
        ],
        axis=1,
    )


def by_rows(row, states):
    return jnp.concatenate(
        [row[:, h : h + 1] * states[h * HP : (h + 1) * HP] for h in range(HL)], axis=0
    )


def two_parts(a):
    hi = a.astype(bf)
    return hi, (a - hi.astype(f32)).astype(bf)


def head_sums(wide):
    column = lax.broadcasted_iota(jnp.int32, (W, 128), 0)
    lane = lax.broadcasted_iota(jnp.int32, (W, 128), 1)
    chosen = ((column >= lane * HP) & (column < lane * HP + HP)).astype(f32).astype(bf)
    hi, low = two_parts(wide)
    return dot(hi, chosen, 1, 0) + dot(low, chosen, 1, 0)


def token_sums(wide):
    ones = jnp.ones((8, wide.shape[1]), bf)
    hi, low = two_parts(wide)
    return dot(ones, hi, 1, 1) + dot(ones, low, 1, 1)


def running_sums(chosen, a):
    hi = a.astype(bf).astype(f32)
    mid = (a - hi).astype(bf).astype(f32)
    packed = hi + pltpu.roll(mid, 8, 1) + pltpu.roll(a - hi - mid, 16, 1)
    out = dot(chosen.astype(f32).astype(bf), packed.astype(bf), 1, 0)
    total = out + pltpu.roll(out, 128 - 8, 1) + pltpu.roll(out, 128 - 16, 1)
    lane = lax.broadcasted_iota(jnp.int32, (SPAN, 128), 1)
    return jnp.where(lane < HL, total, 0.0)


def write_states(sent_ref, states, decay):
    lane = lax.broadcasted_iota(jnp.int32, (8, 128), 1)
    decay = jnp.where(lane < HL, jnp.broadcast_to(decay, (8, 128)), 0.0)
    hi = decay.astype(bf).astype(f32)
    mid = (decay - hi).astype(bf).astype(f32)
    low = decay - hi - mid
    tail = hi + pltpu.roll(mid, HL, 1) + pltpu.roll(low, 2 * HL, 1)
    for j in range(NQ):
        block = states[j * SCAN_ROWS : (j + 1) * SCAN_ROWS]
        sent_ref[j] = jnp.concatenate([block, tail], axis=0).astype(bf)


def read_states(back_ref):
    return jnp.concatenate([back_ref[j].astype(f32)[:SCAN_ROWS] for j in range(NQ)], axis=0)


def span_masks(segc_ref, segr_ref):
    row = lax.broadcasted_iota(jnp.int32, (SPAN, SPAN), 0)
    col = lax.broadcasted_iota(jnp.int32, (SPAN, SPAN), 1)
    return (col <= row) & (segc_ref[...] == segr_ref[0])


def head_decay(mask, run, run_t, h):
    return jnp.exp(jnp.where(mask, run[:, h : h + 1] - run_t[h : h + 1], -1e30))


def end_weights(run, segc_ref, seg_end):
    return jnp.exp(run[SPAN - 1 :] - run) * (segc_ref[...] == seg_end).astype(f32)


def inflow_of(run, segc_ref, seg_before):
    return jnp.exp(run) * (segc_ref[...] == seg_before).astype(f32)


def past_rows(k, u_ref, past_ref, edge_ref):
    past = jnp.where(k == 0, edge_ref[...].astype(f32), past_ref[...].astype(f32))
    return jnp.concatenate([past, u_ref[...].astype(f32)], axis=0)


def back_by(rows, distance):
    return (pltpu.roll(rows, distance, 0) if distance else rows)[16:]


def mix_kernel(
    seg_ref, u_ref, past_ref, edge_ref, same_ref, conv_ref, raw_ref, bias_ref, rate_ref, segc_ref,
    segr_ref, v_ref, pre_ref, within_ref, local_ref, step_ref, run_ref, before_ref, decay_ref, sent_ref, acc_ref, dec_ref,
):
    k = pl.program_id(0)

    @pl.when(k == 0)
    def _():
        acc_ref[...] = jnp.zeros_like(acc_ref)
        dec_ref[...] = jnp.ones_like(dec_ref)

    rows = past_rows(k, u_ref, past_ref, edge_ref)
    pre = jnp.broadcast_to(conv_ref[CONV : CONV + 1], (SPAN, CC))
    for i in range(CONV):
        pre = pre + conv_ref[i : i + 1] * back_by(rows, i) * same_ref[:, i : i + 1]
    pre_ref[...] = pre
    v = silu_both(pre)[0]
    v_ref[...] = v
    lane = lax.broadcasted_iota(jnp.int32, (SPAN, 128), 1)
    raw = raw_ref[...].astype(f32) + bias_ref[...]
    step = jnp.where(lane < HL, jax.nn.softplus(raw), 0.0)
    row = lax.broadcasted_iota(jnp.int32, (SPAN, SPAN), 0)
    col = lax.broadcasted_iota(jnp.int32, (SPAN, SPAN), 1)
    run = running_sums(col <= row, rate_ref[...] * step)
    step_ref[...] = step
    run_ref[...] = run
    run_t = run.T
    mask = span_masks(segc_ref, segr_ref)
    xc = v[:, :W]
    b_low = v[:, W : W + N].astype(bf)
    c_low = v[:, W + N :].astype(bf)
    gram = dot(c_low, b_low, 1, 1)
    xs = (by_lanes(step) * xc).astype(bf)
    half = lane < HP
    for p in range(PAIRS):
        cols = slice(p * 128, (p + 1) * 128)
        out = [
            dot((gram * head_decay(mask, run, run_t, h)).astype(bf), xs[:, cols], 1, 0)
            for h in (2 * p, 2 * p + 1)
        ]
        within_ref[:, cols] = jnp.where(half, out[0], out[1])
    w_end = end_weights(run, segc_ref, seg_ref[1, k])
    weighted = (by_lanes(w_end * step) * xc).astype(bf)
    own = dot(weighted, b_low, 0, 0)
    local_ref[0] = acc_ref[...]
    before_ref[0] = dec_ref[...]
    inside = (seg_ref[1, k] == seg_ref[0, k]).astype(f32)
    decay = jnp.exp(run[SPAN - 1 :]) * inside
    decay_ref[0] = decay
    acc = by_rows(decay, acc_ref[...]) + own
    acc_ref[...] = acc
    dec = dec_ref[...] * decay
    dec_ref[...] = dec

    @pl.when(k == LAST)
    def _():
        write_states(sent_ref, acc, dec)


def silu_both(v):
    s = 1.0 / (1.0 + jnp.exp(-v))
    return v * s, s * (1.0 + v * (1.0 - s))


def gate_kernel(
    last, order_ref, seg_ref, back_ref, local_ref, before_ref, run_ref, v_ref, within_ref, z_ref, segc_ref,
    skip_ref, wo_ref, *rest,
):
    if last:
        dq_ref, y0_ref, other_ref, mine_ref, sums_ref, carry_ref = rest
    else:
        y0_ref, other_ref, mine_ref, sums_ref, carry_ref = rest
    i = pl.program_id(0)
    k = order_ref[i]

    @pl.when(i == 0)
    def _():
        carry_ref[...] = read_states(back_ref)

    carried = (by_rows(before_ref[0], carry_ref[...]) + local_ref[0]).astype(bf)
    xc = v_ref[:, :W]
    c_low = v_ref[:, W + N :].astype(bf)
    reading = dot(c_low, carried, 1, 1)
    y0 = within_ref[...] + by_lanes(inflow_of(run_ref[...], segc_ref, seg_ref[0, k])) * reading
    y0_ref[...] = y0
    mixed = (y0 + skip_ref[...] * xc).astype(bf).astype(f32)
    gated = mixed * silu_both(z_ref[...])[0]
    write_half(other_ref, mine_ref, dot(gated.astype(bf), wo_ref[...], 1, 0).astype(bf))
    sums = token_sums(gated * gated)
    if last:
        row = lax.broadcasted_iota(jnp.int32, (8, SPAN), 0)
        sums = jnp.where(row < 1, sums, token_sums(gated * dq_ref[...]))
    sums_ref[...] = sums


def gate_back_kernel(
    last, seg_ref, grad_ref, wo_ref, scale_ref, v_ref, y0_ref, z_ref, run_ref, segc_ref, skip_ref,
    decay_ref, dy_ref, dz_ref, gr_ref, local_ref, after_ref, sent_ref, acc_ref, dec_ref,
):
    i = pl.program_id(0)
    k = LAST - i

    @pl.when(i == 0)
    def _():
        acc_ref[...] = jnp.zeros_like(acc_ref)
        dec_ref[...] = jnp.ones_like(dec_ref)

    if last:
        sums = scale_ref[...]
        odd = lax.broadcasted_iota(jnp.int32, (2 * NG, SPAN), 0) % 2 == 1
        square = jnp.sum(jnp.where(odd, 0.0, sums), axis=0, keepdims=True)
        inner = jnp.sum(jnp.where(odd, sums, 0.0), axis=0, keepdims=True)
        r_row = lax.rsqrt(square / DI + EPS)
        k_row = r_row * r_row * r_row * inner / DI
    else:
        rows = scale_ref[...].astype(f32)
        pieces = [rows[:, i * TOK : (i + 1) * TOK] for i in range(6)]
        r_two = pieces[0] + pieces[1] + pieces[2]
        k_two = pieces[3] + pieces[4] + pieces[5]
        r_row = jnp.concatenate([r_two[0:1], r_two[16:17]], axis=1)
        k_row = jnp.concatenate([k_two[0:1], k_two[16:17]], axis=1)
    r = jnp.broadcast_to(r_row, (8, SPAN)).T[:, 0:1]
    kappa = jnp.broadcast_to(k_row, (8, SPAN)).T[:, 0:1]
    d_q = grad_ref[...] if last else dot(grad_ref[...], wo_ref[...], 1, 1)
    mixed = (y0_ref[...] + skip_ref[...] * v_ref[:, :W]).astype(bf).astype(f32)
    silu, d_silu = silu_both(z_ref[...])
    gated = mixed * silu
    gr_ref[...] = (r * gated).astype(bf)
    d_gated = r * d_q - kappa * gated
    dy = (d_gated * silu).astype(bf)
    dy_ref[...] = dy
    dz_ref[...] = (d_gated * mixed * d_silu).astype(bf)
    inflow = by_lanes(inflow_of(run_ref[...], segc_ref, seg_ref[0, k]))
    scaled = (inflow * dy.astype(f32)).astype(bf)
    d_carried = dot(scaled, v_ref[:, W + N :].astype(bf), 0, 0)
    local_ref[0] = acc_ref[...]
    after_ref[0] = dec_ref[...]
    decay = decay_ref[0]
    acc = by_rows(decay, acc_ref[...]) + d_carried
    acc_ref[...] = acc
    dec = dec_ref[...] * decay
    dec_ref[...] = dec

    @pl.when(i == LAST)
    def _():
        write_states(sent_ref, acc, dec)


def mix_back_kernel(v_ref, step_ref, run_ref, segc_ref, segr_ref, dy_ref, dxs_ref, dbc_ref):
    lane = lax.broadcasted_iota(jnp.int32, (SPAN, 128), 1)
    half = lane < HP
    run = run_ref[...]
    run_t = run.T
    mask = span_masks(segc_ref, segr_ref)
    xs = (by_lanes(step_ref[...]) * v_ref[:, :W]).astype(bf)
    b_low = v_ref[:, W : W + N].astype(bf)
    c_low = v_ref[:, W + N :].astype(bf)
    gram = dot(c_low, b_low, 1, 1)
    d_gram = jnp.zeros((SPAN, SPAN), f32)
    zero = jnp.zeros((SPAN, 128), bf)
    for p in range(PAIRS):
        cols = slice(p * 128, (p + 1) * 128)
        dy = dy_ref[:, cols]
        out = []
        for i, h in enumerate((2 * p, 2 * p + 1)):
            decay = head_decay(mask, run, run_t, h)
            mixing = (gram * decay).astype(bf)
            dy_one = jnp.where(half, dy, zero) if i == 0 else jnp.where(half, zero, dy)
            d_gram = d_gram + dot(dy_one, xs[:, cols], 1, 1) * decay
            out.append(dot(mixing, dy, 0, 0))
        dxs_ref[:, cols] = jnp.where(half, out[0], out[1])
    d_gram = d_gram.astype(bf)
    dbc_ref[:, :N] = dot(d_gram, c_low, 0, 0)
    dbc_ref[:, N:] = dot(d_gram, b_low, 1, 0)


def end_kernel(
    seg_ref, later_ref, back_ref, local_ref, before_ref, dlocal_ref, after_ref, decay_ref, v_ref,
    pre_ref, raw_ref, bias_ref, rate_ref, step_ref, run_ref, segc_ref, skip_ref, dy_ref, dxs_ref,
    dbc_ref, y0_ref, dpre_ref, draw_ref, sums_ref, later_s, carry_s,
):
    k = pl.program_id(0)

    @pl.when(k == 0)
    def _():
        later_s[...] = read_states(later_ref)
        carry_s[...] = read_states(back_ref)
        sums_ref[...] = jnp.zeros_like(sums_ref)

    d_end = by_rows(after_ref[0], later_s[...]) + dlocal_ref[0]
    carried = by_rows(before_ref[0], carry_s[...]) + local_ref[0]
    d_end_low = d_end.astype(bf)
    run, step, rate = run_ref[...], step_ref[...], rate_ref[...]
    xc = v_ref[:, :W]
    b_low = v_ref[:, W : W + N].astype(bf)
    dy = dy_ref[...].astype(f32)
    dxs = dxs_ref[...]
    step_x = by_lanes(step)
    xs = (step_x * xc).astype(bf).astype(f32)
    w_end = end_weights(run, segc_ref, seg_ref[1, k])
    weights_x = by_lanes(w_end * step)
    weighted = (weights_x * xc).astype(bf)
    scaled = (by_lanes(inflow_of(run, segc_ref, seg_ref[0, k])) * dy).astype(bf)
    d_weighted = dot(b_low, d_end_low, 1, 1)
    d_b = dbc_ref[:, :N] + dot(weighted, d_end_low, 1, 0)
    d_c = dbc_ref[:, N:] + dot(scaled, carried.astype(bf), 1, 0)
    d_xc = skip_ref[...] * dy + step_x * dxs + weights_x * d_weighted
    dv = jnp.concatenate([d_xc, d_b, d_c], axis=1)
    dpre_ref[...] = dv * silu_both(pre_ref[...])[1]
    skip_sum = head_sums(dy * xc)
    d_run = head_sums(dy * y0_ref[...] - xs * dxs)
    d_step = head_sums(xc * dxs)
    d_w = head_sums(d_weighted * xc)
    product = d_end * carried
    lane1 = lax.broadcasted_iota(jnp.int32, (1, 128), 1)
    d_span = jnp.zeros((1, 128), f32)
    for h in range(HL):
        rows = jnp.sum(product[h * HP : (h + 1) * HP], axis=0, keepdims=True)
        d_span = d_span + jnp.where(lane1 == h, jnp.sum(rows, axis=1, keepdims=True), 0.0)
    d_step = d_step + d_w * w_end
    d_ww = d_w * w_end * step
    d_run = d_run - d_ww
    d_last = jnp.sum(d_ww, axis=0, keepdims=True) + d_span * decay_ref[0]
    row = lax.broadcasted_iota(jnp.int32, (SPAN, SPAN), 0)
    col = lax.broadcasted_iota(jnp.int32, (SPAN, SPAN), 1)
    d_a = running_sums(col >= row, d_run) + d_last
    d_step = d_step + rate * d_a
    raw = raw_ref[...].astype(f32) + bias_ref[...]
    lane = lax.broadcasted_iota(jnp.int32, (SPAN, 128), 1)
    d_raw = jnp.where(lane < HL, d_step / (1.0 + jnp.exp(-raw)), 0.0)
    draw_ref[...] = d_raw.astype(bf)
    sums = jnp.concatenate(
        [
            jnp.sum(d_raw, axis=0, keepdims=True),
            rate * jnp.sum(step * d_a, axis=0, keepdims=True),
            jnp.sum(skip_sum, axis=0, keepdims=True),
            jnp.zeros((5, 128), f32),
        ],
        axis=0,
    )
    sums_ref[...] = sums_ref[...] + sums


def conv_back_kernel(
    order_ref, dpre_ref, next_ref, after_ref, u_ref, past_ref, edge_ref, same_ref, conv_ref, draw_ref, dz_ref,
    wa_ref, wz_ref, da_ref, other_ref, mine_ref, taps_ref,
):
    i = pl.program_id(0)
    k = order_ref[i]

    @pl.when(i == 0)
    def _():
        taps_ref[...] = jnp.zeros_like(taps_ref)

    d_pre = dpre_ref[...]
    later = jnp.where(k == LAST, after_ref[...], next_ref[...])
    d_rows = jnp.concatenate([d_pre, later], axis=0)
    rows = past_rows(k, u_ref, past_ref, edge_ref)
    du = jnp.zeros((SPAN, CC), f32)
    taps = []
    for tap in range(CONV):
        ahead = pltpu.roll(d_rows, SPAN + 8 - tap, 0) if tap else d_rows
        same = same_ref[:, CONV + tap : CONV + tap + 1]
        du = du + conv_ref[tap : tap + 1] * ahead[:SPAN] * same
        product = d_pre * back_by(rows, tap) * same_ref[:, tap : tap + 1]
        taps.append(jnp.sum(product, axis=0, keepdims=True))
    taps.append(jnp.sum(d_pre, axis=0, keepdims=True))
    taps.append(jnp.zeros((3, CC), f32))
    taps_ref[...] = taps_ref[...] + jnp.concatenate(taps, axis=0)
    da = jnp.concatenate([du.astype(bf), draw_ref[...]], axis=1)
    da_ref[...] = da
    part = dot(da, wa_ref[...], 1, 1) + dot(dz_ref[...], wz_ref[...], 1, 1)
    write_half(other_ref, mine_ref, part.astype(bf))


def tok_block(n, reverse=False):
    return pl.BlockSpec((SPAN, n), lambda k: (LAST - k if reverse else k, 0))


def span_block(rows, n, reverse=False):
    return pl.BlockSpec((1, rows, n), lambda k: (LAST - k if reverse else k, 0, 0))


def whole(*shape):
    return pl.BlockSpec(shape, lambda k: (0,) * len(shape))


STATE = struct((NS, W, N))
ROW = struct((NS, 1, 128))
SENT = struct((NQ, 32, N), bf)
STATE_SCRATCH = pltpu.VMEM((W, N), f32)


def call(kernel, name, ins, outs, shapes, scratch, args, us):
    return pl.pallas_call(
        kernel,
        grid=(NS,),
        in_specs=ins,
        out_specs=outs,
        out_shape=shapes,
        scratch_shapes=scratch,
        compiler_params=pltpu.CompilerParams(
            dimension_semantics=("arbitrary",), vmem_limit_bytes=60 * 1024 * 1024
        ),
        cost_estimate=pl.CostEstimate(
            flops=int(us * 4e7), bytes_accessed=int(us * 2e5), transcendentals=0
        ),
        name=name,
    )(*args)


def ordered_call(kernel, name, ins, outs, shapes, scratch, args, us):
    return pl.pallas_call(
        kernel,
        grid_spec=pltpu.PrefetchScalarGridSpec(
            num_scalar_prefetch=1, grid=(NS,), in_specs=ins, out_specs=outs, scratch_shapes=scratch
        ),
        out_shape=shapes,
        compiler_params=pltpu.CompilerParams(
            dimension_semantics=("arbitrary",), vmem_limit_bytes=60 * 1024 * 1024
        ),
        cost_estimate=pl.CostEstimate(
            flops=int(us * 4e7), bytes_accessed=int(us * 2e5), transcendentals=0
        ),
        name=name,
    )(span_order(), *args)


def tok_at(n):
    return pl.BlockSpec((SPAN, n), lambda i, order: (order[i], 0))


def span_at(rows, n):
    return pl.BlockSpec((1, rows, n), lambda i, order: (order[i], 0, 0))


def whole_at(*shape):
    return pl.BlockSpec(shape, lambda i, order: (0,) * len(shape))


HALVES = [
    pl.BlockSpec((SPAN, D), lambda i, order: (jnp.minimum(i, 1), 0)),
    pl.BlockSpec((SPAN, D), lambda i, order: (jnp.maximum(i - 2, 0), 0)),
]
HALF_SHAPES = [struct((GT // 2, D), bf)] * 2


def past_block(n):
    return pl.BlockSpec((16, n), lambda k: (jnp.maximum(k * (SPAN // 16) - 1, 0), 0))


def span_mix(seg, u, edge, same, conv, raw, bias, rate, segc, segr):
    return call(
        mix_kernel,
        "span_mix",
        [SMEM, tok_block(CC), past_block(CC), whole(16, CC), tok_block(8), whole(8, CC),
         tok_block(128), whole(1, 128), whole(1, 128), tok_block(1), span_block(1, SPAN)],
        [tok_block(CC), tok_block(CC), tok_block(W), span_block(W, N), tok_block(128),
         tok_block(128), span_block(1, 128), span_block(1, 128), whole(NQ, 32, N)],
        [struct((GT, CC)), struct((GT, CC)), struct((GT, W)), STATE, struct((GT, 128)),
         struct((GT, 128)), ROW, ROW, SENT],
        [STATE_SCRATCH, pltpu.VMEM((1, 128), f32)],
        (seg, u, u, edge, same, conv, raw, bias, rate, segc, segr),
        10,
    )


def conv_back(d_pre, after, u, edge, same, conv, d_raw, dz, wa, wz, at):
    following = pl.BlockSpec(
        (8, CC), lambda i, order: (jnp.minimum((order[i] + 1) * (SPAN // 8), GT // 8 - 1), 0)
    )
    past = pl.BlockSpec(
        (16, CC), lambda i, order: (jnp.maximum(order[i] * (SPAN // 16) - 1, 0), 0)
    )
    return ordered_call(
        conv_back_kernel,
        "conv_back",
        [tok_at(CC), following, whole_at(8, CC), tok_at(CC), past, whole_at(16, CC), tok_at(8),
         whole_at(8, CC), tok_at(128), tok_at(W), whole_at(D, CA),
         pl.BlockSpec((D, W), lambda i, order: (0, at))],
        [tok_at(CA)] + HALVES + [whole_at(8, CC)],
        [struct((GT, CA), bf)] + HALF_SHAPES + [struct((8, CC))],
        [],
        (d_pre, d_pre, after, u, u, edge, same, conv, d_raw, dz, wa, wz),
        10,
    )


def span_gate(seg, back, local, before, run, v, within, z, segc, skip, wo, d_q):
    last = d_q is not None
    ins = [SMEM, whole_at(NQ, 32, N), span_at(W, N), span_at(1, 128), tok_at(128), tok_at(CC),
           tok_at(W), tok_at(W), tok_at(1), whole_at(1, W), whole_at(W, D)]
    args = (seg, back, local, before, run, v, within, z, segc, skip, wo)
    return ordered_call(
        functools.partial(gate_kernel, last),
        "span_gate",
        ins + [tok_at(W)] if last else ins,
        [tok_at(W)] + HALVES + [pl.BlockSpec((8, SPAN), lambda i, order: (0, order[i]))],
        [struct((GT, W))] + HALF_SHAPES + [struct((8, GT))],
        [STATE_SCRATCH],
        args + (d_q,) if last else args,
        10,
    )


def span_gate_back(last, seg, grad, wo, scales, v, y0, z, run, segc, skip, decay):
    if last:
        scale_block = pl.BlockSpec((2 * NG, SPAN), lambda k: (0, LAST - k))
    else:
        scale_block = pl.BlockSpec((32, D), lambda k: (LAST - k, 0))
    return call(
        functools.partial(gate_back_kernel, last),
        "span_gate_back",
        [SMEM, tok_block(W if last else D, True), whole(W, D), scale_block,
         tok_block(CC, True), tok_block(W, True), tok_block(W, True), tok_block(128, True),
         tok_block(1, True), whole(1, W), span_block(1, 128, True)],
        [tok_block(W, True), tok_block(W, True), tok_block(W, True), span_block(W, N, True),
         span_block(1, 128, True), whole(NQ, 32, N)],
        [struct((GT, W), bf), struct((GT, W), bf), struct((GT, W), bf), STATE, ROW, SENT],
        [STATE_SCRATCH, pltpu.VMEM((1, 128), f32)],
        (seg, grad, wo, scales, v, y0, z, run, segc, skip, decay),
        12,
    )


def span_mix_back(v, step, run, segc, segr, dy):
    return call(
        mix_back_kernel,
        "span_mix_back",
        [tok_block(CC), tok_block(128), tok_block(128), tok_block(1), span_block(1, SPAN),
         tok_block(W)],
        [tok_block(W), tok_block(2 * N)],
        [struct((GT, W)), struct((GT, 2 * N))],
        [],
        (v, step, run, segc, segr, dy),
        14,
    )


def span_end(seg, later, back, local, before, dlocal, after, decay, v, pre, raw, bias, rate, step,
             run, segc, skip, dy, dxs, dbc, y0):
    return call(
        end_kernel,
        "span_end",
        [SMEM, whole(NQ, 32, N), whole(NQ, 32, N), span_block(W, N), span_block(1, 128),
         span_block(W, N), span_block(1, 128), span_block(1, 128), tok_block(CC), tok_block(CC),
         tok_block(128), whole(1, 128), whole(1, 128), tok_block(128), tok_block(128),
         tok_block(1), whole(1, W), tok_block(W), tok_block(W), tok_block(2 * N), tok_block(W)],
        [tok_block(CC), tok_block(128), whole(8, 128)],
        [struct((GT, CC)), struct((GT, 128), bf), struct((8, 128))],
        [STATE_SCRATCH, STATE_SCRATCH],
        (seg, later, back, local, before, dlocal, after, decay, v, pre, raw, bias, rate, step, run,
         segc, skip, dy, dxs, dbc, y0),
        16,
    )


def z_out_sums(normed, dz, out_part):
    z_part = mm(normed, dz, 0, 0).astype(bf).reshape(NQ, 96, W)
    out_part = out_part.reshape(NQ, 24, 4, W).transpose(0, 2, 1, 3).reshape(NQ, 96, W)
    sent = jnp.concatenate([z_part, out_part], axis=1)
    return jnp.sum(a2a(sent, ZX).astype(f32), axis=0), sent


SMALL = CC + HL


def small_block(conv_grads, head_grads):
    own_ch = CH // (NQ * NG)
    conv = jnp.stack(conv_grads).reshape(LAYERS * (CONV + 1), NQ * NG, own_ch)
    conv = jnp.pad(conv.transpose(1, 0, 2), ((0, 0), (0, 12 - LAYERS * (CONV + 1)), (0, 0)))
    head = jnp.stack(head_grads, axis=1)
    high = rounded(head)
    head = jnp.concatenate([high, head - high], axis=1)
    head = jnp.tile(head, (NQ * NG // 2, 1, 1))
    head = jnp.pad(head, ((0, 0), (0, 12 - 2 * LAYERS), (0, 0)))
    block = jnp.concatenate([conv, head], axis=2).reshape(D, own_ch + 3 * H // 2)
    return jnp.pad(block.astype(bf), ((0, 0), (SMALL, CA - SMALL - block.shape[1])))


def per_device(
    tokens,
    doc_starts,
    norm_gain,
    in_weight,
    conv_weight,
    conv_bias,
    step_bias,
    decay_log,
    skip_gain,
    gate_gain,
    out_weight,
    cotangent,
):
    q = lax.axis_index(ZX)
    yh, core, yl = lax.axis_index("yh"), lax.axis_index("c"), lax.axis_index("yl")
    sub = yh * 2 + core
    group = yl * 4 + sub

    own_ch = CH // (NQ * NG)
    conv_own = jnp.concatenate([conv_weight, conv_bias[:, None]], axis=1).reshape(-1, own_ch)
    conv_own = jnp.pad(conv_own, ((0, 12 - conv_own.shape[0]), (0, 0)))
    sent = [in_blocks(in_weight[l], norm_gain[l], conv_own if l == 0 else conv_own[:, :0]) for l in range(LAYERS)]
    sent = jnp.stack(sent, axis=1)
    got = a2a(sent, LINE)
    in_0 = got[:, 0].reshape(NG * 12, CA + W)
    in_1 = got[:, 1].reshape(NG * 12, CA + W)
    own_0 = jnp.broadcast_to(in_0[None, :, :CA], (NQ, NG * 12, CA))
    w_a0 = a2a(own_0, ZX).reshape(D, CA)
    h = tokens.astype(f32)
    normed = (h * lax.rsqrt(jnp.mean(h * h, axis=-1, keepdims=True) + EPS)).astype(bf)
    pos = q * GT + jnp.arange(-(CONV - 1), GT + CONV - 1, dtype=jnp.int32)
    seg_ext = jnp.sum((doc_starts[None, :] <= pos[:, None]).astype(jnp.int32), axis=1) - 1
    seg = seg_ext[CONV - 1 : CONV - 1 + GT]
    seg_spans = seg.reshape(NS, SPAN)
    seg_before = seg_ext[CONV - 2 : CONV - 2 + GT : SPAN]
    seg_ends = jnp.stack([seg_before, seg_spans[:, -1]])
    seg_col, seg_row = seg[:, None], seg_spans[:, None, :]
    same = jnp.stack(
        [seg_ext[CONV - 1 - k : CONV - 1 - k + GT] == seg for k in range(CONV)]
        + [seg_ext[CONV - 1 + k : CONV - 1 + k + GT] == seg for k in range(CONV)],
        axis=1,
    ).astype(f32)

    def pick_heads(a):
        own = lax.dynamic_slice_in_dim(a, sub * HL, HL, 0)
        return jnp.pad(own, (0, 128 - HL))[None]

    onward = [(i, i + 1) for i in range(NQ - 1)]
    consts = []
    for l in range(LAYERS):
        rate = jnp.where(jnp.arange(128)[None] < HL, -jnp.exp(pick_heads(decay_log[l])), 0.0)
        skip_x = jnp.repeat(lax.dynamic_slice_in_dim(skip_gain[l], sub * HL, HL, 0), HP)[None]
        consts.append((pick_heads(step_bias[l]), rate, skip_x))
    prepared = own_0, consts, same, seg_ends, seg_col, seg_row, span_order()
    places, blocks = line_blocks(wait_for(normed, got), prepared)
    cot_places, cot_blocks = line_blocks(wait_for(cotangent, blocks[6]))
    grad_full = place_tokens(cot_places, cot_blocks)
    folded_out = (out_weight.astype(f32) * gate_gain.astype(f32)[:, :, None]).astype(bf)
    out_blocks = lax.ppermute(folded_out, AX, TO_HEADS)

    w_a0 = wait_for(w_a0, cot_blocks)
    normed, u, raw = place_project(places, blocks, w_a0)
    tail = u[GT - 16 :]
    conv_all = wait_for(w_a0, tail)[:, SMALL : SMALL + own_ch].reshape(NQ * NG, 12, own_ch)
    conv_all = conv_all[:, : LAYERS * (CONV + 1)].transpose(1, 0, 2)
    conv_all = conv_all.reshape(LAYERS, CONV + 1, CH).astype(f32)
    conv_x = lax.dynamic_slice_in_dim(conv_all, group * W, W, 2)
    conv_here = jnp.concatenate([conv_x, conv_all[:, :, DI:]], axis=2)
    conv_here = jnp.pad(conv_here, ((0, 0), (0, 7 - CONV), (0, 0)))
    zo = jnp.concatenate([in_0[:, CA:], out_blocks[0].reshape(96, W)], axis=0)
    zo = group_gather(wait_for(zo, tail)).reshape(NQ, 192, W)
    w_z0 = zo[:, :96].reshape(D, W)
    w_o = [zo[:, 96:].reshape(W, D), None]
    w_in1 = group_gather(wait_for(in_1, tail))
    saved = []
    for l in range(LAYERS):
        bias_h, rate, skip_x = consts[l]
        if l > 0:
            normed, u, raw = line_project(normed, w_in1)
        edge = lax.ppermute(u[GT - 16 :], ZX, onward)
        v, pre, within, local, step, run, before, decay, sent = span_mix(
            seg_ends, u, edge, same, conv_here[l], raw, bias_h, rate, seg_col, seg_row
        )
        if l == 0:
            w_o[1] = group_gather(wait_for(out_blocks[1], v))
            z, d_q = mm(normed, w_z0), None
            back = exclusive_scan(sent, False, grad_full, z)
        else:
            z, d_q = mm(normed, w_in1[:, CA:]), mm(grad_full, w_o[1], 1, 1)
            back = exclusive_scan(sent, False, z, d_q)
        y0, other, mine, sums = span_gate(
            seg_ends, back, local, before, run, v, within, z, seg_col, skip_x, w_o[l],
            d_q,
        )
        saved.append(
            dict(
                h=h, normed=normed, u=u, edge=edge, pre=pre, v=v, z=z, raw=raw, bias_h=bias_h,
                rate=rate, skip_x=skip_x, step=step, run=run, before=before, decay=decay,
                local=local, back=back, y0=y0,
            )
        )
        if l < LAYERS - 1:
            parts = line_parts(other, mine)
            square = wait_for(to_owners(sums[0]), *parts[1:])
            h, branch, normed, r_gate = plain_call(
                advance_kernel,
                "advance",
                [struct((TOK, D)), struct((TOK, D)), struct((TOK, D), bf), struct((8, TOK))],
                (*parts, square, h),
            )
        else:
            scales = to_line(sums[:2])
            at = (line_index() // 2 * 4 + core * 2 + yl) * TOK
            square = lax.dynamic_slice_in_dim(scales, at, TOK, 1)
            square = jnp.sum(square.reshape(NG, 2, TOK)[:, 0], axis=0)
            r_last = lax.rsqrt(square / DI + EPS)[:, None]
            last_halves = other, mine

    grad = cotangent
    conv_grads, head_grads = [None] * LAYERS, [None] * LAYERS
    a_sums, z_sums, out_sums = ([None] * LAYERS for _ in range(3))
    for l in reversed(range(LAYERS)):
        s = saved[l]
        dy, dz, gr, dlocal, after, sent = span_gate_back(
            l == LAYERS - 1, seg_ends, d_q if l else grad_full, w_o[l], scales, s["v"], s["y0"], s["z"], s["run"],
            seg_col, s["skip_x"], s["decay"],
        )
        out_part = mm(gr, grad_full, 0, 0).astype(bf)
        dxs, dbc = span_mix_back(s["v"], s["step"], s["run"], seg_col, seg_row, dy)
        later = exclusive_scan(sent, True, out_part, dxs)
        if l == 0:
            both = z_out_sums(s["normed"], wait_for(dz, later), out_part)
            d_pre_first = both[1]
        else:
            d_pre_first = later
        d_pre, d_raw, head_sum = span_end(
            seg_ends, wait_for(later, d_pre_first), s["back"], s["local"], s["before"], dlocal, after, s["decay"], s["v"],
            s["pre"], s["raw"], s["bias_h"], s["rate"], s["step"], s["run"], seg_col, s["skip_x"],
            dy, dxs, dbc, s["y0"],
        )
        following = lax.ppermute(d_pre[:8], ZX, [(b, a) for a, b in onward])
        if l > 0:
            both = z_out_sums(s["normed"], wait_for(dz, following), out_part)
        both = both[0]
        z_sums[l] = both[:96]
        out_sums[l] = both[96:].reshape(4, 24, W).transpose(1, 0, 2).reshape(24, D)
        if l == LAYERS - 1:
            w_a, w_z, at = w_in1, w_in1, CA // W
        else:
            w_a, w_z, at = w_a0, w_z0, 0
        da, other, mine, taps = conv_back(
            d_pre, following, s["u"], s["edge"], same, conv_here[l], d_raw, dz, w_a, w_z, at
        )
        conv_full = jnp.zeros((CONV + 1, CH), f32)
        conv_full = lax.dynamic_update_slice_in_dim(
            conv_full, taps[: CONV + 1, :W], group * W, 1
        )
        conv_grads[l] = conv_full.at[:, DI:].set(taps[: CONV + 1, W:])
        head_full = lax.dynamic_update_slice_in_dim(
            jnp.zeros((3, H), f32), head_sum[:3, :HL], group * HL, 1
        )
        head_grads[l] = head_full.reshape(3, 2, H // 2).transpose(1, 0, 2).reshape(2, 3 * H // 2)
        if l == 0:
            out_sums = [lax.ppermute(a, AX, TO_OWNER) for a in out_sums]
            da = wait_for(da, out_sums)
        a_part = mm(s["normed"], da, 0, 0)
        if l == 0:
            a_part = a_part + small_block(conv_grads, head_grads).astype(f32)
        a_part = a_part.astype(bf)
        if l == 0:
            parts = line_parts(other, mine, a_part)
            a_sums[l] = group_reduce(a_part)
        else:
            parts = line_parts(other, mine)
            a_sums[l] = group_reduce(wait_for(a_part, parts[0]))
        if l > 0:
            grad, block = plain_call(
                functools.partial(retreat_kernel, True),
                "retreat",
                [struct((TOK, D)), struct((TOK + 16, D), bf)],
                (*parts, s["h"], grad, branch, r_gate),
            )
            early = jnp.concatenate([a_sums[1], z_sums[1]], axis=1).reshape(NG, 12, CA + W)
            grad_full, scales = line_gather_more(block, early)
            early = a2a(early, LINE)
            scales = wait_for(scales, early)
        else:
            grad = plain_call(
                functools.partial(retreat_kernel, False),
                "retreat_last",
                struct((TOK, D)),
                (*parts, s["h"], grad),
            )
            early = wait_for(early, parts[1])
            parts = line_parts(*last_halves, parts[1:])
            total = parts[0] + parts[1].astype(f32) + parts[2].astype(f32) + parts[3].astype(f32)
            output = (h + total * r_last).astype(bf)

    late = jnp.concatenate([a_sums[0], z_sums[0]], axis=1)
    late = a2a(late.reshape(NG, 12, CA + W), LINE)
    small = jnp.sum(late[:, :, SMALL:CA], axis=0)
    in_grads, gain_grads, out_grads, gate_grads = ([None] * LAYERS for _ in range(4))
    for l in range(LAYERS):
        got = (late, early)[l]
        a_piece, z_piece = got[:, :, :CA], got[:, :, CA:]
        g_in = jnp.concatenate(
            [
                heads_in(z_piece),
                heads_in(a_piece[:, :, :W]),
                jnp.sum(a_piece[:, :, W:CC], axis=0),
                heads_in(a_piece[:, :, CC : CC + HL]),
            ],
            axis=1,
        )
        in_grads[l] = g_in * norm_gain[l].astype(f32)[:, None]
        gain_grads[l] = jnp.sum(g_in * in_weight[l].astype(f32), axis=1)
        g_out = out_sums[l]
        out_grads[l] = g_out * gate_gain[l].astype(f32)[:, None]
        gate_grads[l] = jnp.sum(g_out * out_weight[l].astype(f32), axis=1)

    conv_grad = small[: LAYERS * (CONV + 1), :own_ch].reshape(LAYERS, CONV + 1, own_ch)
    head_grad = small[:LAYERS] + small[LAYERS : 2 * LAYERS]
    head_grad = head_grad[:, own_ch : own_ch + 3 * H // 2].reshape(LAYERS, 3, H // 2)
    return (
        output,
        grad,
        jnp.stack(gain_grads),
        jnp.stack(in_grads),
        conv_grad[:, :CONV],
        conv_grad[:, CONV],
        head_grad[:, 0],
        head_grad[:, 1],
        head_grad[:, 2],
        jnp.stack(gate_grads),
        jnp.stack(out_grads),
    )


def solution(mesh):
    fine = Mesh(mesh.devices.reshape(4, 4, 2, 2, 2), AX)
    tok, last, mid, heads = P(AX, None), P(None, AX), P(None, AX, None), P(None, "yl")
    conv = P(None, None, AX)
    return jax.shard_map(
        per_device,
        mesh=fine,
        in_specs=(tok, P(), last, mid, conv, last, heads, heads, heads, last, mid, tok),
        out_specs=(tok, tok, last, mid, conv, last, heads, heads, heads, last, mid),
        check_vma=False,
    )
```

```python
import functools

import jax
import jax.numpy as jnp
from jax import lax
from jax.experimental import pallas as pl
from jax.experimental.pallas import tpu as pltpu
from jax.sharding import Mesh, PartitionSpec as P

D = 1536
DI = 3072
H = 48
HP = 64
N = 128
CONV = 4
LAYERS = 2
CH = DI + 2 * N
EPS = 1e-05

AX = ("z", "x", "yh", "c", "yl")
ZX = ("z", "x")
LINE = ("yh", "c", "yl")
Y = ("yh", "yl")
NQ = 16
NG = 8
TOK = 128
GT = TOK * NG
SPAN = 256
NS = GT // SPAN
HL = H // NG
W = HL * HP
CC = W + 2 * N
CA = CC + 128

bf = jnp.bfloat16
f32 = jnp.float32
HI = lax.Precision.HIGHEST


SMEM = pl.BlockSpec(memory_space=pltpu.SMEM)
VMEM_BYTES = 60 * 1024 * 1024
SMALL_VMEM = 16 * 1024 * 1024


def struct(shape, dtype=f32):
    return jax.ShapeDtypeStruct(shape, dtype)


def mm(a, b, ca=1, cb=0):
    return lax.dot_general(a, b, (((ca,), (cb,)), ((), ())), preferred_element_type=f32)


def a2a(a, axes):
    return lax.all_to_all(a, axes, 0, 0, tiled=True)


def core_swap(a):
    return lax.ppermute(a, "c", [(0, 1), (1, 0)])


def line_index():
    return lax.axis_index("yh") * 2 + lax.axis_index("yl")


def along_line(a, distance):
    return lax.ppermute(a, Y, [(i, (i + distance) % 4) for i in range(4)])


def fill_places(pos_ref, blocks, x_ref):
    for i, block in enumerate(blocks):
        at = pl.multiple_of(pos_ref[i] * TOK, TOK)
        x_ref[pl.ds(at, TOK)] = block[:TOK]


def place_kernel(pos_ref, *refs):
    blocks, (out_ref, extra_ref, x_ref) = refs[:NG], refs[NG:]
    k = pl.program_id(0)

    @pl.when(k == 0)
    def _():
        fill_places(pos_ref, blocks, x_ref)
        for i, block in enumerate(blocks):
            extra_ref[pl.ds(pl.multiple_of(pos_ref[i] * 16, 16), 16)] = block[TOK:]

    out_ref[...] = x_ref[pl.ds(pl.multiple_of(k * SPAN, SPAN), SPAN)]


def place_project_kernel(pos_ref, *refs):
    blocks, (w_ref, out_ref, u_ref, raw_ref, x_ref) = refs[:NG], refs[NG:]
    k = pl.program_id(0)

    @pl.when(k == 0)
    def _():
        fill_places(pos_ref, blocks, x_ref)

    x = x_ref[pl.ds(pl.multiple_of(k * SPAN, SPAN), SPAN)]
    out_ref[...] = x
    project = jnp.dot(x, w_ref[...], preferred_element_type=f32).astype(bf)
    u_ref[...] = project[:, :CC]
    raw_ref[...] = project[:, CC:]


def line_blocks(own, first=None):
    y, core = line_index(), lax.axis_index("c")
    blocks, places = [], []

    def place(distance, c):
        at = (y - distance) % 4
        return (at // 2) * 4 + c * 2 + at % 2

    for d in (0, 1, 3, 2):
        got = along_line(own, d) if d else own
        if d and first is not None:
            got = wait_for(got, first)
        blocks += [got, core_swap(got)]
        places += [place(d, core), place(d, 1 - core)]
    return jnp.stack(places).astype(jnp.int32), blocks


X_SCRATCH = pltpu.VMEM((GT, D), bf)


def line_gather_more(own, first):
    places, blocks = line_blocks(own, first)
    return call(
        place_kernel,
        "place_gradient",
        [SMEM] + [whole(TOK + 16, D)] * NG,
        [tok_block(D), whole(NG * 16, D)],
        [struct((GT, D), bf), struct((NG * 16, D), bf)],
        [X_SCRATCH],
        (places, *blocks),
        4,
    )


def line_project(own, weight):
    return place_project(*line_blocks(own), weight)


def place_project(places, blocks, weight):
    return call(
        place_project_kernel,
        "place_project",
        [SMEM] + [whole(TOK, D)] * NG + [whole(D, CA)],
        [tok_block(D), tok_block(CC), tok_block(128)],
        [struct((GT, D), bf), struct((GT, CC), bf), struct((GT, 128), bf)],
        [X_SCRATCH],
        (places, *blocks, weight),
        9,
    )


def chip_kernel(y_ref, mine_ref, got_ref, own_ref, *sent_refs):
    def rows(distance):
        at = pl.multiple_of((y_ref[0] + distance) % 4 * TOK, TOK)
        return mine_ref[pl.ds(at, TOK)].astype(f32) + got_ref[pl.ds(at, TOK)].astype(f32)

    own_ref[...] = rows(0)
    for distance, ref in zip((1, 3, 2), sent_refs):
        ref[...] = rows(distance).astype(bf)


def line_parts(other, mine, first=None):
    got = core_swap(other)
    if first is not None:
        got = wait_for(got, first)
    own, *sent = pl.pallas_call(
        chip_kernel,
        out_shape=[struct((TOK, D))] + [struct((TOK, D), bf)] * 3,
        in_specs=[SMEM] + [pl.BlockSpec(memory_space=pltpu.VMEM)] * 2,
        out_specs=[pl.BlockSpec(memory_space=pltpu.VMEM)] * 4,
        compiler_params=pltpu.CompilerParams(vmem_limit_bytes=SMALL_VMEM),
        name="chip_sum",
    )(line_index().reshape(1).astype(jnp.int32), mine, got)
    return [own] + [along_line(block, d) for block, d in zip(sent, (1, 3, 2))]


def span_order():
    core = lax.axis_index("c")
    return jnp.stack([1 - core, 3 - core, core, 2 + core]).astype(jnp.int32)


def write_half(other_ref, mine_ref, value):
    i = pl.program_id(0)

    @pl.when(i < 2)
    def _():
        other_ref[...] = value

    @pl.when(i >= 2)
    def _():
        mine_ref[...] = value


def parts_sum(refs):
    total = refs[0][...].astype(f32)
    for ref in refs[1:]:
        total = total + ref[...].astype(f32)
    return total


def inverse_rms(a):
    return lax.rsqrt(jnp.mean(a * a, axis=1, keepdims=True) + EPS)


def advance_kernel(p0, p1, p2, p3, square_ref, h_ref, out_ref, branch_ref, normed_ref, scale_ref):
    square = jnp.sum(square_ref[...], axis=0, keepdims=True)
    r_gate = jnp.broadcast_to(lax.rsqrt(square / DI + EPS), (8, TOK))
    scale_ref[...] = r_gate
    branch = parts_sum((p0, p1, p2, p3)) * r_gate.T[:, 0:1]
    h = h_ref[...] + branch
    out_ref[...] = h
    branch_ref[...] = branch
    normed_ref[...] = (h * inverse_rms(h)).astype(bf)


def in_parts(row):
    hi = row.astype(bf).astype(f32)
    mid = (row - hi).astype(bf).astype(f32)
    return [hi, mid, row - hi - mid]


def retreat_kernel(extra, *refs):
    n = 4 if extra else 1
    parts, (h_ref, grad_ref, *refs) = refs[:n], refs[n:]
    h = h_ref[...]
    r_in = inverse_rms(h)
    d_norm = parts_sum(parts)
    inner = jnp.mean(h * d_norm, axis=1, keepdims=True)
    grad = grad_ref[...].astype(f32) + r_in * d_norm - h * (r_in * r_in * r_in * inner)
    if not extra:
        refs[0][...] = grad
        return
    branch_ref, scale_ref, out_ref, sent_ref = refs
    out_ref[...] = grad
    low = grad.astype(bf)
    r_gate = scale_ref[...]
    column = jnp.sum(low.astype(f32) * branch_ref[...], axis=1, keepdims=True)
    row = jnp.broadcast_to(column, (TOK, 128)).T[:8]
    kappa = r_gate * r_gate * row / DI
    rows = in_parts(r_gate) + in_parts(kappa)
    rows = jnp.concatenate(rows + [jnp.zeros((8, D - 6 * TOK), f32)], axis=1)
    sent_ref[:TOK] = low
    sent_ref[TOK:] = jnp.concatenate([rows, jnp.zeros((8, D), f32)], axis=0).astype(bf)


def plain_call(kernel, name, shapes, args):
    return pl.pallas_call(
        kernel,
        out_shape=shapes,
        compiler_params=pltpu.CompilerParams(vmem_limit_bytes=SMALL_VMEM),
        cost_estimate=pl.CostEstimate(
            flops=int(2e8), bytes_accessed=int(1e6), transcendentals=0
        ),
        name=name,
    )(*args)


def to_owners(row):
    return a2a(row.reshape(NG, TOK), LINE)


def to_line(rows):
    m = rows.shape[0]
    return a2a(jnp.broadcast_to(rows[None], (NG,) + rows.shape), LINE).reshape(NG * m, GT)


def rounded(a):
    return lax.reduce_precision(a, exponent_bits=8, mantissa_bits=7)


def group_gather(block):
    return lax.all_gather(block, ZX, axis=0, tiled=True)


def group_gather_now(block):
    r, n = block.shape
    return a2a(jnp.broadcast_to(block[None], (NQ, r, n)), ZX).reshape(NQ * r, n)


def wait_for(value, *others):
    return lax.optimization_barrier((value, others))[0]


def group_reduce(full):
    r = full.shape[0] // NQ
    return jnp.sum(a2a(full.reshape(NQ, r, full.shape[1]), ZX).astype(f32), axis=0)


def heads_out(cols, width):
    r = cols.shape[0]
    return cols.reshape(r, 2, 2, 2, width).transpose(2, 3, 1, 0, 4).reshape(NG, r, width)


def heads_in(blocks):
    _, r, width = blocks.shape
    return blocks.reshape(2, 2, 2, r, width).transpose(3, 2, 0, 1, 4).reshape(r, NG * width)


def line_of(group):
    yl, yh, c = group // 4, (group // 2) % 2, group % 2
    return yh * 4 + c * 2 + yl


TO_HEADS = [(s, (s % NQ) * NG + line_of(s // NQ)) for s in range(NQ * NG)]
TO_OWNER = [(b, a) for a, b in TO_HEADS]


def in_blocks(weight, gain, extra):
    folded = (weight.astype(f32) * gain.astype(f32)[:, None]).astype(bf)
    z = heads_out(folded[:, :DI], W)
    x = heads_out(folded[:, DI : 2 * DI], W)
    bc = jnp.broadcast_to(folded[None, :, 2 * DI : 2 * DI + 2 * N], (NG, 12, 2 * N))
    step = heads_out(folded[:, 2 * DI + 2 * N :], HL)
    extra = jnp.broadcast_to(extra[None], (NG,) + extra.shape)
    step = jnp.concatenate([step, extra], axis=2)
    step = jnp.pad(step, ((0, 0), (0, 0), (0, 128 - step.shape[2])))
    return jnp.concatenate([x, bc, step, z], axis=2)


SCAN_ROWS = HL * HP // NQ


def scan_kernel(reverse, q_ref, got_ref, out_ref):
    row = q_ref[0] * SCAN_ROWS + lax.broadcasted_iota(jnp.int32, (SCAN_ROWS, N), 0)
    lane = lax.broadcasted_iota(jnp.int32, (SCAN_ROWS, N), 1)
    head = jnp.zeros((SCAN_ROWS, N), jnp.int32)
    for k in range(1, HL):
        head = head + (row >= k * HP).astype(jnp.int32)
    chosen = (lane == head) | (lane == head + HL) | (lane == head + 2 * HL)
    carry = jnp.zeros((SCAN_ROWS, N), f32)
    pad = jnp.zeros((32 - SCAN_ROWS, N), f32)
    for j in range(NQ - 1, -1, -1) if reverse else range(NQ):
        out_ref[j] = jnp.concatenate([carry, pad], axis=0).astype(bf)
        block = got_ref[j].astype(f32)
        decay = jnp.sum(
            jnp.where(chosen, block[SCAN_ROWS : SCAN_ROWS + 1], 0.0), axis=1, keepdims=True
        )
        carry = decay * carry + block[:SCAN_ROWS]


def exclusive_scan(sent, reverse, first, second):
    q = lax.axis_index(ZX)
    got = a2a(sent, ZX)
    if first is not None:
        got = wait_for(got, first)
    outs = pl.pallas_call(
        functools.partial(scan_kernel, reverse),
        out_shape=jax.ShapeDtypeStruct((NQ, 32, N), bf),
        in_specs=[
            pl.BlockSpec(memory_space=pltpu.SMEM),
            pl.BlockSpec(memory_space=pltpu.VMEM),
        ],
        out_specs=pl.BlockSpec(memory_space=pltpu.VMEM),
        name="group_scan",
    )(q.reshape(1).astype(jnp.int32), got)
    extra = second(outs)
    return wait_for(a2a(outs, ZX), extra), extra


PAIRS = HL // 2
LAST = NS - 1


def dot(a, b, ca, cb, precision=None):
    return lax.dot_general(
        a, b, (((ca,), (cb,)), ((), ())), preferred_element_type=f32, precision=precision
    )


def by_lanes(cols):
    lane = lax.broadcasted_iota(jnp.int32, (cols.shape[0], 128), 1)
    return jnp.concatenate(
        [
            jnp.where(lane < HP, cols[:, 2 * p : 2 * p + 1], cols[:, 2 * p + 1 : 2 * p + 2])
            for p in range(PAIRS)
        ],
        axis=1,
    )


def by_rows(row, states):
    return jnp.concatenate(
        [row[:, h : h + 1] * states[h * HP : (h + 1) * HP] for h in range(HL)], axis=0
    )


def two_parts(a):
    hi = a.astype(bf)
    return hi, (a - hi.astype(f32)).astype(bf)


def head_sums(wide):
    column = lax.broadcasted_iota(jnp.int32, (W, 128), 0)
    lane = lax.broadcasted_iota(jnp.int32, (W, 128), 1)
    chosen = ((column >= lane * HP) & (column < lane * HP + HP)).astype(f32).astype(bf)
    hi, low = two_parts(wide)
    return dot(hi, chosen, 1, 0) + dot(low, chosen, 1, 0)


def token_sums(wide):
    ones = jnp.ones((8, wide.shape[1]), bf)
    hi, low = two_parts(wide)
    return dot(ones, hi, 1, 1) + dot(ones, low, 1, 1)


def running_sums(chosen, a):
    hi = a.astype(bf).astype(f32)
    mid = (a - hi).astype(bf).astype(f32)
    packed = hi + pltpu.roll(mid, 8, 1) + pltpu.roll(a - hi - mid, 16, 1)
    out = dot(chosen.astype(f32).astype(bf), packed.astype(bf), 1, 0)
    total = out + pltpu.roll(out, 128 - 8, 1) + pltpu.roll(out, 128 - 16, 1)
    lane = lax.broadcasted_iota(jnp.int32, (SPAN, 128), 1)
    return jnp.where(lane < HL, total, 0.0)


def write_states(sent_ref, states, decay):
    lane = lax.broadcasted_iota(jnp.int32, (8, 128), 1)
    decay = jnp.where(lane < HL, jnp.broadcast_to(decay, (8, 128)), 0.0)
    hi = decay.astype(bf).astype(f32)
    mid = (decay - hi).astype(bf).astype(f32)
    low = decay - hi - mid
    tail = hi + pltpu.roll(mid, HL, 1) + pltpu.roll(low, 2 * HL, 1)
    for j in range(NQ):
        block = states[j * SCAN_ROWS : (j + 1) * SCAN_ROWS]
        sent_ref[j] = jnp.concatenate([block, tail], axis=0).astype(bf)


def read_states(back_ref):
    return jnp.concatenate([back_ref[j].astype(f32)[:SCAN_ROWS] for j in range(NQ)], axis=0)


def span_masks(segc_ref, segr_ref):
    row = lax.broadcasted_iota(jnp.int32, (SPAN, SPAN), 0)
    col = lax.broadcasted_iota(jnp.int32, (SPAN, SPAN), 1)
    return (col <= row) & (segc_ref[...] == segr_ref[0])


def head_decay(mask, run, run_t, h):
    return jnp.exp(jnp.where(mask, run[:, h : h + 1] - run_t[h : h + 1], -1e30))


def end_weights(run, segc_ref, seg_end):
    return jnp.exp(run[SPAN - 1 :] - run) * (segc_ref[...] == seg_end).astype(f32)


def inflow_of(run, segc_ref, seg_before):
    return jnp.exp(run) * (segc_ref[...] == seg_before).astype(f32)


def past_rows(k, u_ref, past_ref, edge_ref):
    past = jnp.where(k == 0, edge_ref[...].astype(f32), past_ref[...].astype(f32))
    return jnp.concatenate([past, u_ref[...].astype(f32)], axis=0)


def back_by(rows, distance):
    return (pltpu.roll(rows, distance, 0) if distance else rows)[16:]


def mix_kernel(
    seg_ref, u_ref, past_ref, edge_ref, same_ref, conv_ref, raw_ref, bias_ref, rate_ref, segc_ref,
    segr_ref, v_ref, pre_ref, within_ref, local_ref, step_ref, run_ref, before_ref, decay_ref, sent_ref, acc_ref, dec_ref,
):
    k = pl.program_id(0)

    @pl.when(k == 0)
    def _():
        acc_ref[...] = jnp.zeros_like(acc_ref)
        dec_ref[...] = jnp.ones_like(dec_ref)

    rows = past_rows(k, u_ref, past_ref, edge_ref)
    pre = jnp.broadcast_to(conv_ref[CONV : CONV + 1], (SPAN, CC))
    for i in range(CONV):
        pre = pre + conv_ref[i : i + 1] * back_by(rows, i) * same_ref[:, i : i + 1]
    pre_ref[...] = pre.astype(bf)
    v_low = silu_both(pre)[0].astype(bf)
    v_ref[...] = v_low
    lane = lax.broadcasted_iota(jnp.int32, (SPAN, 128), 1)
    raw = raw_ref[...].astype(f32) + bias_ref[...]
    step = jnp.where(lane < HL, jax.nn.softplus(raw), 0.0)
    row = lax.broadcasted_iota(jnp.int32, (SPAN, SPAN), 0)
    col = lax.broadcasted_iota(jnp.int32, (SPAN, SPAN), 1)
    run = running_sums(col <= row, rate_ref[...] * step)
    step_ref[...] = step
    run_ref[...] = run
    run_t = run.T
    mask = span_masks(segc_ref, segr_ref)
    xc = v_low[:, :W].astype(f32)
    b_low = v_low[:, W : W + N]
    c_low = v_low[:, W + N :]
    gram = dot(c_low, b_low, 1, 1)
    xs = (by_lanes(step) * xc).astype(bf)
    half = lane < HP
    for p in range(PAIRS):
        cols = slice(p * 128, (p + 1) * 128)
        out = [
            dot((gram * head_decay(mask, run, run_t, h)).astype(bf), xs[:, cols], 1, 0)
            for h in (2 * p, 2 * p + 1)
        ]
        within_ref[:, cols] = jnp.where(half, out[0], out[1])
    w_end = end_weights(run, segc_ref, seg_ref[1, k])
    weighted = (by_lanes(w_end * step) * xc).astype(bf)
    own = dot(weighted, b_low, 0, 0)
    local_ref[0] = acc_ref[...]
    before_ref[0] = dec_ref[...]
    inside = (seg_ref[1, k] == seg_ref[0, k]).astype(f32)
    decay = jnp.exp(run[SPAN - 1 :]) * inside
    decay_ref[0] = decay
    acc = by_rows(decay, acc_ref[...]) + own
    acc_ref[...] = acc
    dec = dec_ref[...] * decay
    dec_ref[...] = dec

    @pl.when(k == LAST)
    def _():
        write_states(sent_ref, acc, dec)


def silu_both(v):
    s = 1.0 / (1.0 + jnp.exp(-v))
    return v * s, s * (1.0 + v * (1.0 - s))


def gate_kernel(
    last, order_ref, seg_ref, back_ref, local_ref, before_ref, run_ref, v_ref, within_ref, z_ref, segc_ref,
    skip_ref, wo_ref, *rest,
):
    if last:
        dq_ref, y0_ref, part_ref, sums_ref, carry_ref = rest
    else:
        y0_ref, other_ref, mine_ref, sums_ref, carry_ref = rest
    i = pl.program_id(0)
    k = order_ref[i]

    @pl.when(i == 0)
    def _():
        carry_ref[...] = read_states(back_ref)

    carried = (by_rows(before_ref[0], carry_ref[...]) + local_ref[0]).astype(bf)
    xc = v_ref[:, :W].astype(f32)
    c_low = v_ref[:, W + N :]
    reading = dot(c_low, carried, 1, 1)
    y0 = within_ref[...] + by_lanes(inflow_of(run_ref[...], segc_ref, seg_ref[0, k])) * reading
    y0_ref[...] = y0
    mixed = (y0 + skip_ref[...] * xc).astype(bf).astype(f32)
    gated = mixed * silu_both(z_ref[...].astype(f32))[0]
    part = dot(gated.astype(bf), wo_ref[...], 1, 0).astype(bf)
    if last:
        part_ref[...] = part
    else:
        write_half(other_ref, mine_ref, part)
    sums = token_sums(gated * gated)
    if last:
        row = lax.broadcasted_iota(jnp.int32, (8, SPAN), 0)
        sums = jnp.where(row < 1, sums, token_sums(gated * dq_ref[...]))
    sums_ref[...] = sums


def gate_back_kernel(
    last, seg_ref, grad_ref, wo_ref, scale_ref, v_ref, y0_ref, z_ref, run_ref, segc_ref, skip_ref,
    decay_ref, dy_ref, dz_ref, gr_ref, local_ref, after_ref, sent_ref, acc_ref, dec_ref,
):
    i = pl.program_id(0)
    k = LAST - i

    @pl.when(i == 0)
    def _():
        acc_ref[...] = jnp.zeros_like(acc_ref)
        dec_ref[...] = jnp.ones_like(dec_ref)

    if last:
        sums = scale_ref[...]
        odd = lax.broadcasted_iota(jnp.int32, (2 * NG, SPAN), 0) % 2 == 1
        square = jnp.sum(jnp.where(odd, 0.0, sums), axis=0, keepdims=True)
        inner = jnp.sum(jnp.where(odd, sums, 0.0), axis=0, keepdims=True)
        r_row = lax.rsqrt(square / DI + EPS)
        k_row = r_row * r_row * r_row * inner / DI
    else:
        rows = scale_ref[...].astype(f32)
        pieces = [rows[:, i * TOK : (i + 1) * TOK] for i in range(6)]
        r_two = pieces[0] + pieces[1] + pieces[2]
        k_two = pieces[3] + pieces[4] + pieces[5]
        r_row = jnp.concatenate([r_two[0:1], r_two[16:17]], axis=1)
        k_row = jnp.concatenate([k_two[0:1], k_two[16:17]], axis=1)
    r = jnp.broadcast_to(r_row, (8, SPAN)).T[:, 0:1]
    kappa = jnp.broadcast_to(k_row, (8, SPAN)).T[:, 0:1]
    d_q = grad_ref[...] if last else dot(grad_ref[...], wo_ref[...], 1, 1)
    mixed = (y0_ref[...] + skip_ref[...] * v_ref[:, :W].astype(f32)).astype(bf).astype(f32)
    silu, d_silu = silu_both(z_ref[...].astype(f32))
    gated = mixed * silu
    gr_ref[...] = (r * gated).astype(bf)
    d_gated = r * d_q - kappa * gated
    dy = (d_gated * silu).astype(bf)
    dy_ref[...] = dy
    dz_ref[...] = (d_gated * mixed * d_silu).astype(bf)
    inflow = by_lanes(inflow_of(run_ref[...], segc_ref, seg_ref[0, k]))
    scaled = (inflow * dy.astype(f32)).astype(bf)
    d_carried = dot(scaled, v_ref[:, W + N :], 0, 0)
    local_ref[0] = acc_ref[...]
    after_ref[0] = dec_ref[...]
    decay = decay_ref[0]
    acc = by_rows(decay, acc_ref[...]) + d_carried
    acc_ref[...] = acc
    dec = dec_ref[...] * decay
    dec_ref[...] = dec

    @pl.when(i == LAST)
    def _():
        write_states(sent_ref, acc, dec)


def mix_back_kernel(v_ref, step_ref, run_ref, segc_ref, segr_ref, dy_ref, dxs_ref, dbc_ref):
    lane = lax.broadcasted_iota(jnp.int32, (SPAN, 128), 1)
    half = lane < HP
    run = run_ref[...]
    run_t = run.T
    mask = span_masks(segc_ref, segr_ref)
    xs = (by_lanes(step_ref[...]) * v_ref[:, :W].astype(f32)).astype(bf)
    b_low = v_ref[:, W : W + N]
    c_low = v_ref[:, W + N :]
    gram = dot(c_low, b_low, 1, 1)
    d_gram = jnp.zeros((SPAN, SPAN), f32)
    zero = jnp.zeros((SPAN, 128), bf)
    for p in range(PAIRS):
        cols = slice(p * 128, (p + 1) * 128)
        dy = dy_ref[:, cols]
        out = []
        for i, h in enumerate((2 * p, 2 * p + 1)):
            decay = head_decay(mask, run, run_t, h)
            mixing = (gram * decay).astype(bf)
            dy_one = jnp.where(half, dy, zero) if i == 0 else jnp.where(half, zero, dy)
            d_gram = d_gram + dot(dy_one, xs[:, cols], 1, 1) * decay
            out.append(dot(mixing, dy, 0, 0))
        dxs_ref[:, cols] = jnp.where(half, out[0], out[1])
    d_gram = d_gram.astype(bf)
    dbc_ref[:, :N] = dot(d_gram, c_low, 0, 0).astype(bf)
    dbc_ref[:, N:] = dot(d_gram, b_low, 1, 0).astype(bf)


def end_kernel(
    seg_ref, later_ref, back_ref, local_ref, before_ref, dlocal_ref, after_ref, decay_ref, v_ref,
    pre_ref, raw_ref, bias_ref, rate_ref, step_ref, run_ref, segc_ref, skip_ref, dy_ref, dxs_ref,
    dbc_ref, y0_ref, dpre_ref, draw_ref, sums_ref, later_s, carry_s,
):
    k = pl.program_id(0)

    @pl.when(k == 0)
    def _():
        later_s[...] = read_states(later_ref)
        carry_s[...] = read_states(back_ref)
        sums_ref[...] = jnp.zeros_like(sums_ref)

    d_end = by_rows(after_ref[0], later_s[...]) + dlocal_ref[0]
    carried = by_rows(before_ref[0], carry_s[...]) + local_ref[0]
    d_end_low = d_end.astype(bf)
    run, step, rate = run_ref[...], step_ref[...], rate_ref[...]
    xc = v_ref[:, :W].astype(f32)
    b_low = v_ref[:, W : W + N]
    dy = dy_ref[...].astype(f32)
    dxs = dxs_ref[...]
    step_x = by_lanes(step)
    xs = (step_x * xc).astype(bf).astype(f32)
    w_end = end_weights(run, segc_ref, seg_ref[1, k])
    weights_x = by_lanes(w_end * step)
    weighted = (weights_x * xc).astype(bf)
    scaled = (by_lanes(inflow_of(run, segc_ref, seg_ref[0, k])) * dy).astype(bf)
    d_weighted = dot(b_low, d_end_low, 1, 1)
    d_b = dbc_ref[:, :N].astype(f32) + dot(weighted, d_end_low, 1, 0)
    d_c = dbc_ref[:, N:].astype(f32) + dot(scaled, carried.astype(bf), 1, 0)
    d_xc = skip_ref[...] * dy + step_x * dxs + weights_x * d_weighted
    dv = jnp.concatenate([d_xc, d_b, d_c], axis=1)
    dpre_ref[...] = (dv * silu_both(pre_ref[...].astype(f32))[1]).astype(bf)
    skip_sum = head_sums(dy * xc)
    d_run = head_sums(dy * y0_ref[...] - xs * dxs)
    d_step = head_sums(xc * dxs)
    d_w = head_sums(d_weighted * xc)
    product = d_end * carried
    lane1 = lax.broadcasted_iota(jnp.int32, (1, 128), 1)
    d_span = jnp.zeros((1, 128), f32)
    for h in range(HL):
        rows = jnp.sum(product[h * HP : (h + 1) * HP], axis=0, keepdims=True)
        d_span = d_span + jnp.where(lane1 == h, jnp.sum(rows, axis=1, keepdims=True), 0.0)
    d_step = d_step + d_w * w_end
    d_ww = d_w * w_end * step
    d_run = d_run - d_ww
    d_last = jnp.sum(d_ww, axis=0, keepdims=True) + d_span * decay_ref[0]
    row = lax.broadcasted_iota(jnp.int32, (SPAN, SPAN), 0)
    col = lax.broadcasted_iota(jnp.int32, (SPAN, SPAN), 1)
    d_a = running_sums(col >= row, d_run) + d_last
    d_step = d_step + rate * d_a
    raw = raw_ref[...].astype(f32) + bias_ref[...]
    lane = lax.broadcasted_iota(jnp.int32, (SPAN, 128), 1)
    d_raw = jnp.where(lane < HL, d_step / (1.0 + jnp.exp(-raw)), 0.0)
    draw_ref[...] = d_raw.astype(bf)
    sums = jnp.concatenate(
        [
            jnp.sum(d_raw, axis=0, keepdims=True),
            rate * jnp.sum(step * d_a, axis=0, keepdims=True),
            jnp.sum(skip_sum, axis=0, keepdims=True),
            jnp.zeros((5, 128), f32),
        ],
        axis=0,
    )
    sums_ref[...] = sums_ref[...] + sums


def conv_back_kernel(
    first, order_ref, dpre_ref, next_ref, after_ref, u_ref, past_ref, edge_ref, same_ref, conv_ref, draw_ref, dz_ref,
    wa_ref, wz_ref, da_ref, *outs,
):
    taps_ref = outs[-1]
    i = pl.program_id(0)
    k = order_ref[i]

    @pl.when(i == 0)
    def _():
        taps_ref[...] = jnp.zeros_like(taps_ref)

    d_pre = dpre_ref[...].astype(f32)
    later = jnp.where(k == LAST, after_ref[...].astype(f32), next_ref[...].astype(f32))
    d_rows = jnp.concatenate([d_pre, later], axis=0)
    rows = past_rows(k, u_ref, past_ref, edge_ref)
    du = jnp.zeros((SPAN, CC), f32)
    taps = []
    for tap in range(CONV):
        ahead = pltpu.roll(d_rows, SPAN + 16 - tap, 0) if tap else d_rows
        same = same_ref[:, CONV + tap : CONV + tap + 1]
        du = du + conv_ref[tap : tap + 1] * ahead[:SPAN] * same
        product = d_pre * back_by(rows, tap) * same_ref[:, tap : tap + 1]
        taps.append(jnp.sum(product, axis=0, keepdims=True))
    taps.append(jnp.sum(d_pre, axis=0, keepdims=True))
    taps.append(jnp.zeros((3, CC), f32))
    taps_ref[...] = taps_ref[...] + jnp.concatenate(taps, axis=0)
    da = jnp.concatenate([du.astype(bf), draw_ref[...]], axis=1)
    da_ref[...] = da
    part = dot(da, wa_ref[...], 1, 1) + dot(dz_ref[...], wz_ref[...], 1, 1)
    if first:
        outs[0][...] = part.astype(bf)
    else:
        write_half(*outs[:2], part.astype(bf))


def tok_block(n, reverse=False):
    return pl.BlockSpec((SPAN, n), lambda k: (LAST - k if reverse else k, 0))


def span_block(rows, n, reverse=False):
    return pl.BlockSpec((1, rows, n), lambda k: (LAST - k if reverse else k, 0, 0))


def whole(*shape):
    return pl.BlockSpec(shape, lambda k: (0,) * len(shape))


STATE = struct((NS, W, N))
ROW = struct((NS, 1, 128))
SENT = struct((NQ, 32, N), bf)
STATE_SCRATCH = pltpu.VMEM((W, N), f32)


def call(kernel, name, ins, outs, shapes, scratch, args, us, vmem=VMEM_BYTES):
    return pl.pallas_call(
        kernel,
        grid=(NS,),
        in_specs=ins,
        out_specs=outs,
        out_shape=shapes,
        scratch_shapes=scratch,
        compiler_params=pltpu.CompilerParams(
            dimension_semantics=("arbitrary",), vmem_limit_bytes=vmem
        ),
        cost_estimate=pl.CostEstimate(
            flops=int(us * 4e7), bytes_accessed=int(us * 2e5), transcendentals=0
        ),
        name=name,
    )(*args)


def ordered_call(kernel, name, ins, outs, shapes, scratch, args, us):
    return pl.pallas_call(
        kernel,
        grid_spec=pltpu.PrefetchScalarGridSpec(
            num_scalar_prefetch=1, grid=(NS,), in_specs=ins, out_specs=outs, scratch_shapes=scratch
        ),
        out_shape=shapes,
        compiler_params=pltpu.CompilerParams(
            dimension_semantics=("arbitrary",), vmem_limit_bytes=VMEM_BYTES
        ),
        cost_estimate=pl.CostEstimate(
            flops=int(us * 4e7), bytes_accessed=int(us * 2e5), transcendentals=0
        ),
        name=name,
    )(span_order(), *args)


def tok_at(n):
    return pl.BlockSpec((SPAN, n), lambda i, order: (order[i], 0))


def span_at(rows, n):
    return pl.BlockSpec((1, rows, n), lambda i, order: (order[i], 0, 0))


def whole_at(*shape):
    return pl.BlockSpec(shape, lambda i, order: (0,) * len(shape))


HALVES = [
    pl.BlockSpec((SPAN, D), lambda i, order: (jnp.minimum(i, 1), 0)),
    pl.BlockSpec((SPAN, D), lambda i, order: (jnp.maximum(i - 2, 0), 0)),
]
HALF_SHAPES = [struct((GT // 2, D), bf)] * 2


def past_block(n):
    return pl.BlockSpec((16, n), lambda k: (jnp.maximum(k * (SPAN // 16) - 1, 0), 0))


def span_mix(seg, u, edge, same, conv, raw, bias, rate, segc, segr):
    return call(
        mix_kernel,
        "span_mix",
        [SMEM, tok_block(CC), past_block(CC), whole(16, CC), tok_block(8), whole(8, CC),
         tok_block(128), whole(1, 128), whole(1, 128), tok_block(1), span_block(1, SPAN)],
        [tok_block(CC), tok_block(CC), tok_block(W), span_block(W, N), tok_block(128),
         tok_block(128), span_block(1, 128), span_block(1, 128), whole(NQ, 32, N)],
        [struct((GT, CC), bf), struct((GT, CC), bf), struct((GT, W)), STATE, struct((GT, 128)),
         struct((GT, 128)), ROW, ROW, SENT],
        [STATE_SCRATCH, pltpu.VMEM((1, 128), f32)],
        (seg, u, u, edge, same, conv, raw, bias, rate, segc, segr),
        10,
    )


def conv_back(first, d_pre, after, u, edge, same, conv, d_raw, dz, wa, wz, at):
    following = pl.BlockSpec(
        (16, CC), lambda i, order: (jnp.minimum((order[i] + 1) * (SPAN // 16), GT // 16 - 1), 0)
    )
    past = pl.BlockSpec(
        (16, CC), lambda i, order: (jnp.maximum(order[i] * (SPAN // 16) - 1, 0), 0)
    )
    return ordered_call(
        functools.partial(conv_back_kernel, first),
        "conv_back",
        [tok_at(CC), following, whole_at(16, CC), tok_at(CC), past, whole_at(16, CC), tok_at(8),
         whole_at(8, CC), tok_at(128), tok_at(W), whole_at(D, CA),
         pl.BlockSpec((D, W), lambda i, order: (0, at))],
        [tok_at(CA)] + ([tok_at(D)] if first else HALVES) + [whole_at(8, CC)],
        [struct((GT, CA), bf)] + ([struct((GT, D), bf)] if first else HALF_SHAPES)
        + [struct((8, CC))],
        [],
        (d_pre, d_pre, after, u, u, edge, same, conv, d_raw, dz, wa, wz),
        10,
    )


def span_gate(seg, back, local, before, run, v, within, z, segc, skip, wo, d_q):
    last = d_q is not None
    ins = [SMEM, whole_at(NQ, 32, N), span_at(W, N), span_at(1, 128), tok_at(128), tok_at(CC),
           tok_at(W), tok_at(W), tok_at(1), whole_at(1, W), whole_at(W, D)]
    args = (seg, back, local, before, run, v, within, z, segc, skip, wo)
    return ordered_call(
        functools.partial(gate_kernel, last),
        "span_gate",
        ins + [tok_at(W)] if last else ins,
        [tok_at(W)] + ([tok_at(D)] if last else HALVES)
        + [pl.BlockSpec((8, SPAN), lambda i, order: (0, order[i]))],
        [struct((GT, W))] + ([struct((GT, D), bf)] if last else HALF_SHAPES)
        + [struct((8, GT))],
        [STATE_SCRATCH],
        args + (d_q,) if last else args,
        10,
    )


def span_gate_back(last, seg, grad, wo, scales, v, y0, z, run, segc, skip, decay):
    if last:
        scale_block = pl.BlockSpec((2 * NG, SPAN), lambda k: (0, LAST - k))
    else:
        scale_block = pl.BlockSpec((32, D), lambda k: (LAST - k, 0))
    return call(
        functools.partial(gate_back_kernel, last),
        "span_gate_back",
        [SMEM, tok_block(W if last else D, True), whole(W, D), scale_block,
         tok_block(CC, True), tok_block(W, True), tok_block(W, True), tok_block(128, True),
         tok_block(1, True), whole(1, W), span_block(1, 128, True)],
        [tok_block(W, True), tok_block(W, True), tok_block(W, True), span_block(W, N, True),
         span_block(1, 128, True), whole(NQ, 32, N)],
        [struct((GT, W), bf), struct((GT, W), bf), struct((GT, W), bf), STATE, ROW, SENT],
        [STATE_SCRATCH, pltpu.VMEM((1, 128), f32)],
        (seg, grad, wo, scales, v, y0, z, run, segc, skip, decay),
        12,
    )


def span_mix_back(v, step, run, segc, segr, dy):
    return call(
        mix_back_kernel,
        "span_mix_back",
        [tok_block(CC), tok_block(128), tok_block(128), tok_block(1), span_block(1, SPAN),
         tok_block(W)],
        [tok_block(W), tok_block(2 * N)],
        [struct((GT, W)), struct((GT, 2 * N), bf)],
        [],
        (v, step, run, segc, segr, dy),
        14,
    )


def span_end(seg, later, back, local, before, dlocal, after, decay, v, pre, raw, bias, rate, step,
             run, segc, skip, dy, dxs, dbc, y0):
    return call(
        end_kernel,
        "span_end",
        [SMEM, whole(NQ, 32, N), whole(NQ, 32, N), span_block(W, N), span_block(1, 128),
         span_block(W, N), span_block(1, 128), span_block(1, 128), tok_block(CC), tok_block(CC),
         tok_block(128), whole(1, 128), whole(1, 128), tok_block(128), tok_block(128),
         tok_block(1), whole(1, W), tok_block(W), tok_block(W), tok_block(2 * N), tok_block(W)],
        [tok_block(CC), tok_block(128), whole(8, 128)],
        [struct((GT, CC), bf), struct((GT, 128), bf), struct((8, 128))],
        [STATE_SCRATCH, STATE_SCRATCH],
        (seg, later, back, local, before, dlocal, after, decay, v, pre, raw, bias, rate, step, run,
         segc, skip, dy, dxs, dbc, y0),
        16,
    )


def group_reduce_blocks(sent):
    return jnp.sum(a2a(sent, ZX).astype(f32), axis=0)


SMALL = CC + HL


def small_block(conv_grads, head_grads):
    own_ch = CH // (NQ * NG)
    conv = jnp.stack(conv_grads).reshape(LAYERS * (CONV + 1), NQ * NG, own_ch)
    conv = jnp.pad(conv.transpose(1, 0, 2), ((0, 0), (0, 12 - LAYERS * (CONV + 1)), (0, 0)))
    head = jnp.stack(head_grads, axis=1)
    high = rounded(head)
    head = jnp.concatenate([high, head - high], axis=1)
    head = jnp.tile(head, (NQ * NG // 2, 1, 1))
    head = jnp.pad(head, ((0, 0), (0, 12 - 2 * LAYERS), (0, 0)))
    block = jnp.concatenate([conv, head], axis=2).reshape(D, own_ch + 3 * H // 2)
    return jnp.pad(block.astype(bf), ((0, 0), (SMALL, CA - SMALL - block.shape[1])))


def per_device(
    tokens,
    doc_starts,
    norm_gain,
    in_weight,
    conv_weight,
    conv_bias,
    step_bias,
    decay_log,
    skip_gain,
    gate_gain,
    out_weight,
    cotangent,
):
    q = lax.axis_index(ZX)
    yh, core, yl = lax.axis_index("yh"), lax.axis_index("c"), lax.axis_index("yl")
    sub = yh * 2 + core
    group = yl * 4 + sub

    own_ch = CH // (NQ * NG)
    conv_own = jnp.concatenate([conv_weight, conv_bias[:, None]], axis=1).reshape(-1, own_ch)
    conv_own = jnp.pad(conv_own, ((0, 12 - conv_own.shape[0]), (0, 0)))
    sent = [in_blocks(in_weight[l], norm_gain[l], conv_own if l == 0 else conv_own[:, :0]) for l in range(LAYERS)]
    sent = jnp.stack(sent, axis=1)
    got = a2a(sent, LINE)
    in_0 = got[:, 0].reshape(NG * 12, CA + W)
    in_1 = got[:, 1].reshape(NG * 12, CA + W)
    own_0 = jnp.broadcast_to(in_0[None, :, :CA], (NQ, NG * 12, CA))
    w_a0 = a2a(own_0, ZX).reshape(D, CA)
    h = tokens.astype(f32)
    normed = (h * lax.rsqrt(jnp.mean(h * h, axis=-1, keepdims=True) + EPS)).astype(bf)
    pos = q * GT + jnp.arange(-(CONV - 1), GT + CONV - 1, dtype=jnp.int32)
    seg_ext = jnp.sum((doc_starts[None, :] <= pos[:, None]).astype(jnp.int32), axis=1) - 1
    seg = seg_ext[CONV - 1 : CONV - 1 + GT]
    seg_spans = seg.reshape(NS, SPAN)
    seg_before = seg_ext[CONV - 2 : CONV - 2 + GT : SPAN]
    seg_ends = jnp.stack([seg_before, seg_spans[:, -1]])
    seg_col, seg_row = seg[:, None], seg_spans[:, None, :]
    same = jnp.stack(
        [seg_ext[CONV - 1 - k : CONV - 1 - k + GT] == seg for k in range(CONV)]
        + [seg_ext[CONV - 1 + k : CONV - 1 + k + GT] == seg for k in range(CONV)],
        axis=1,
    ).astype(f32)

    def pick_heads(a):
        own = lax.dynamic_slice_in_dim(a, sub * HL, HL, 0)
        return jnp.pad(own, (0, 128 - HL))[None]

    onward = [(i, i + 1) for i in range(NQ - 1)]
    consts = []
    for l in range(LAYERS):
        rate = jnp.where(jnp.arange(128)[None] < HL, -jnp.exp(pick_heads(decay_log[l])), 0.0)
        skip_x = jnp.repeat(lax.dynamic_slice_in_dim(skip_gain[l], sub * HL, HL, 0), HP)[None]
        consts.append((pick_heads(step_bias[l]), rate, skip_x))
    prepared = own_0, consts, same, seg_ends, seg_col, seg_row, span_order()
    places, blocks = line_blocks(wait_for(normed, got), prepared)
    folded_out = (out_weight.astype(f32) * gate_gain.astype(f32)[:, :, None]).astype(bf)
    out_blocks = lax.ppermute(folded_out, AX, TO_HEADS)
    zo = jnp.concatenate([in_0[:, CA:], out_blocks.reshape(192, W)], axis=0)
    grad_full = lax.all_gather(cotangent, LINE, axis=0, tiled=True)
    w_a0 = wait_for(w_a0, zo)
    normed, u, raw = place_project(places, blocks, w_a0)
    tail = u[GT - 16 :]
    conv_all = wait_for(w_a0, tail)[:, SMALL : SMALL + own_ch].reshape(NQ * NG, 12, own_ch)
    conv_all = conv_all[:, : LAYERS * (CONV + 1)].transpose(1, 0, 2)
    conv_all = conv_all.reshape(LAYERS, CONV + 1, CH).astype(f32)
    conv_x = lax.dynamic_slice_in_dim(conv_all, group * W, W, 2)
    conv_here = jnp.concatenate([conv_x, conv_all[:, :, DI:]], axis=2)
    conv_here = jnp.pad(conv_here, ((0, 0), (0, 7 - CONV), (0, 0)))
    zo = group_gather(wait_for(zo, tail)).reshape(NQ, 288, W)
    w_z0 = zo[:, :96].reshape(D, W)
    w_o = [zo[:, 96:192].reshape(W, D), None]
    w_in1 = group_gather(wait_for(in_1, tail))
    saved = []
    for l in range(LAYERS):
        bias_h, rate, skip_x = consts[l]
        if l > 0:
            normed, u, raw = line_project(normed, w_in1)
        edge = lax.ppermute(u[GT - 16 :], ZX, onward)
        v, pre, within, local, step, run, before, decay, sent = span_mix(
            seg_ends, u, edge, same, conv_here[l], raw, bias_h, rate, seg_col, seg_row
        )
        if l == 0:
            w_o[1] = wait_for(zo, v)[:, 192:].reshape(W, D)
            d_q = None
            back, z = exclusive_scan(
                sent, False, None, lambda outs: mm(wait_for(normed, outs), w_z0).astype(bf)
            )
        else:
            z = mm(normed, w_in1[:, CA:]).astype(bf)
            back, d_q = exclusive_scan(
                sent, False, z, lambda outs: mm(wait_for(grad_full, outs), w_o[1], 1, 1)
            )
        y0, *parts, sums = span_gate(
            seg_ends, back, local, before, run, v, within, z, seg_col, skip_x, w_o[l],
            d_q,
        )
        saved.append(
            dict(
                h=h, normed=normed, u=u, edge=edge, pre=pre, v=v, z=z, raw=raw, bias_h=bias_h,
                rate=rate, skip_x=skip_x, step=step, run=run, before=before, decay=decay,
                local=local, back=back, y0=y0,
            )
        )
        if l < LAYERS - 1:
            parts = line_parts(*parts)
            square = wait_for(to_owners(sums[0]), *parts[1:])
            h, branch, normed, r_gate = plain_call(
                advance_kernel,
                "advance",
                [struct((TOK, D)), struct((TOK, D)), struct((TOK, D), bf), struct((8, TOK))],
                (*parts, square, h),
            )
        else:
            scales = to_line(sums[:2])
            at = (line_index() // 2 * 4 + core * 2 + yl) * TOK
            square = lax.dynamic_slice_in_dim(scales, at, TOK, 1)
            square = jnp.sum(square.reshape(NG, 2, TOK)[:, 0], axis=0)
            r_last = lax.rsqrt(square / DI + EPS)[:, None]
            total = lax.psum_scatter(parts[0], LINE, scatter_dimension=0, tiled=True)
            output = (h + total.astype(f32) * r_last).astype(bf)

    grad = cotangent
    conv_grads, head_grads = [None] * LAYERS, [None] * LAYERS
    a_sums, z_sums, out_sums = ([None] * LAYERS for _ in range(3))
    for l in reversed(range(LAYERS)):
        s = saved[l]
        dy, dz, gr, dlocal, after, sent = span_gate_back(
            l == LAYERS - 1, seg_ends, d_q if l else grad_full, w_o[l], scales, s["v"], s["y0"], s["z"], s["run"],
            seg_col, s["skip_x"], s["decay"],
        )
        z_part = mm(s["normed"], dz, 0, 0).astype(bf).reshape(NQ, 96, W)

        def out_blocks_of(outs):
            low = wait_for(gr, outs)
            return [
                mm(low, grad_full[:, i * W : (i + 1) * W], 0, 0).astype(bf).reshape(NQ, 24, W)
                for i in range(D // W)
            ]

        later, out_part = exclusive_scan(sent, True, z_part, out_blocks_of)
        sums = jnp.concatenate([z_part, *out_part], axis=1)
        both = group_reduce_blocks(wait_for(sums, later))
        dxs, dbc = span_mix_back(s["v"], s["step"], s["run"], seg_col, seg_row, wait_for(dy, sums))
        d_pre, d_raw, head_sum = span_end(
            seg_ends, later, s["back"], s["local"], s["before"], dlocal, after, s["decay"], s["v"],
            s["pre"], s["raw"], s["bias_h"], s["rate"], s["step"], s["run"], seg_col, s["skip_x"],
            dy, dxs, dbc, s["y0"],
        )
        following = lax.ppermute(d_pre[:16], ZX, [(b, a) for a, b in onward])
        z_sums[l] = both[:96]
        out_sums[l] = both[96:].reshape(4, 24, W).transpose(1, 0, 2).reshape(24, D)
        if l == LAYERS - 1:
            w_a, w_z, at = w_in1, w_in1, CA // W
        else:
            w_a, w_z, at = w_a0, w_z0, 0
        da, *parts, taps = conv_back(
            l == 0, d_pre, following, s["u"], s["edge"], same, conv_here[l], d_raw, dz, w_a, w_z, at
        )
        conv_full = jnp.zeros((CONV + 1, CH), f32)
        conv_full = lax.dynamic_update_slice_in_dim(
            conv_full, taps[: CONV + 1, :W], group * W, 1
        )
        conv_grads[l] = conv_full.at[:, DI:].set(taps[: CONV + 1, W:])
        head_full = lax.dynamic_update_slice_in_dim(
            jnp.zeros((3, H), f32), head_sum[:3, :HL], group * HL, 1
        )
        head_grads[l] = head_full.reshape(3, 2, H // 2).transpose(1, 0, 2).reshape(2, 3 * H // 2)
        a_part = mm(s["normed"], da, 0, 0)
        if l == 0:
            a_part = a_part + small_block(conv_grads, head_grads).astype(f32)
        a_part = a_part.astype(bf)
        if l == 0:
            parts = [lax.psum_scatter(parts[0], LINE, scatter_dimension=0, tiled=True)]
            a_sums[l] = group_reduce(a_part)
        else:
            parts = line_parts(*parts, output)
            a_sums[l] = group_reduce(wait_for(a_part, parts[0]))
        if l > 0:
            grad, block = plain_call(
                functools.partial(retreat_kernel, True),
                "retreat",
                [struct((TOK, D)), struct((TOK + 16, D), bf)],
                (*parts, s["h"], grad, branch, r_gate),
            )
            early = jnp.concatenate([a_sums[1], z_sums[1]], axis=1).reshape(NG, 12, CA + W)
            grad_full, scales = line_gather_more(block, early)
            early = a2a(early, LINE)
            scales = wait_for(scales, early)
        else:
            grad = plain_call(
                functools.partial(retreat_kernel, False),
                "retreat_last",
                struct((TOK, D)),
                (*parts, s["h"], grad),
            )

    out_sums = [
        lax.ppermute(wait_for(out_sums[l], a_part if l else a_sums[0]), AX, TO_OWNER)
        for l in range(LAYERS)
    ]
    late = jnp.concatenate([a_sums[0], z_sums[0]], axis=1)
    late = a2a(late.reshape(NG, 12, CA + W), LINE)
    small = jnp.sum(late[:, :, SMALL:CA], axis=0)
    in_grads, gain_grads, out_grads, gate_grads = ([None] * LAYERS for _ in range(4))
    for l in range(LAYERS):
        got = (late, early)[l]
        a_piece, z_piece = got[:, :, :CA], got[:, :, CA:]
        g_in = jnp.concatenate(
            [
                heads_in(z_piece),
                heads_in(a_piece[:, :, :W]),
                jnp.sum(a_piece[:, :, W:CC], axis=0),
                heads_in(a_piece[:, :, CC : CC + HL]),
            ],
            axis=1,
        )
        in_grads[l] = g_in * norm_gain[l].astype(f32)[:, None]
        gain_grads[l] = jnp.sum(g_in * in_weight[l].astype(f32), axis=1)
        g_out = out_sums[l]
        out_grads[l] = g_out * gate_gain[l].astype(f32)[:, None]
        gate_grads[l] = jnp.sum(g_out * out_weight[l].astype(f32), axis=1)

    conv_grad = small[: LAYERS * (CONV + 1), :own_ch].reshape(LAYERS, CONV + 1, own_ch)
    head_grad = small[:LAYERS] + small[LAYERS : 2 * LAYERS]
    head_grad = head_grad[:, own_ch : own_ch + 3 * H // 2].reshape(LAYERS, 3, H // 2)
    return (
        output,
        grad,
        jnp.stack(gain_grads),
        jnp.stack(in_grads),
        conv_grad[:, :CONV],
        conv_grad[:, CONV],
        head_grad[:, 0],
        head_grad[:, 1],
        head_grad[:, 2],
        jnp.stack(gate_grads),
        jnp.stack(out_grads),
    )


def solution(mesh):
    fine = Mesh(mesh.devices.reshape(4, 4, 2, 2, 2), AX)
    tok, last, mid, heads = P(AX, None), P(None, AX), P(None, AX, None), P(None, "yl")
    conv = P(None, None, AX)
    return jax.shard_map(
        per_device,
        mesh=fine,
        in_specs=(tok, P(), last, mid, conv, last, heads, heads, heads, last, mid, tok),
        out_specs=(tok, tok, last, mid, conv, last, heads, heads, heads, last, mid),
        check_vma=False,
    )
```

```python
import functools

import jax
import jax.numpy as jnp
from jax import lax
from jax.experimental import pallas as pl
from jax.experimental.pallas import tpu as pltpu
from jax.sharding import Mesh, PartitionSpec as P

D = 1536
DI = 3072
H = 48
HP = 64
N = 128
CONV = 4
LAYERS = 2
CH = DI + 2 * N
EPS = 1e-05

AX = ("z", "x", "yh", "c", "yl")
ZX = ("z", "x")
LINE = ("yh", "c", "yl")
Y = ("yh", "yl")
NQ = 16
NG = 8
TOK = 128
GT = TOK * NG
SPAN = 256
NS = GT // SPAN
HL = H // NG
W = HL * HP
CC = W + 2 * N
CA = CC + 128

bf = jnp.bfloat16
f32 = jnp.float32
HI = lax.Precision.HIGHEST


SMEM = pl.BlockSpec(memory_space=pltpu.SMEM)
VMEM_BYTES = 60 * 1024 * 1024
SMALL_VMEM = 16 * 1024 * 1024


def struct(shape, dtype=f32):
    return jax.ShapeDtypeStruct(shape, dtype)


def mm(a, b, ca=1, cb=0):
    return lax.dot_general(a, b, (((ca,), (cb,)), ((), ())), preferred_element_type=f32)


def a2a(a, axes):
    return lax.all_to_all(a, axes, 0, 0, tiled=True)


def core_swap(a):
    return lax.ppermute(a, "c", [(0, 1), (1, 0)])


def line_index():
    return lax.axis_index("yh") * 2 + lax.axis_index("yl")


def along_line(a, distance):
    return lax.ppermute(a, Y, [(i, (i + distance) % 4) for i in range(4)])


def fill_places(pos_ref, blocks, x_ref):
    for i, block in enumerate(blocks):
        at = pl.multiple_of(pos_ref[i] * TOK, TOK)
        x_ref[pl.ds(at, TOK)] = block[:TOK]


def place_kernel(pos_ref, *refs):
    blocks, (out_ref, extra_ref, x_ref) = refs[:NG], refs[NG:]
    k = pl.program_id(0)

    @pl.when(k == 0)
    def _():
        fill_places(pos_ref, blocks, x_ref)
        for i, block in enumerate(blocks):
            extra_ref[pl.ds(pl.multiple_of(pos_ref[i] * 16, 16), 16)] = block[TOK:]

    out_ref[...] = x_ref[pl.ds(pl.multiple_of(k * SPAN, SPAN), SPAN)]


def place_project_kernel(pos_ref, *refs):
    blocks, (w_ref, out_ref, u_ref, raw_ref, x_ref) = refs[:NG], refs[NG:]
    k = pl.program_id(0)

    @pl.when(k == 0)
    def _():
        fill_places(pos_ref, blocks, x_ref)

    x = x_ref[pl.ds(pl.multiple_of(k * SPAN, SPAN), SPAN)]
    out_ref[...] = x
    project = jnp.dot(x, w_ref[...], preferred_element_type=f32).astype(bf)
    u_ref[...] = project[:, :CC]
    raw_ref[...] = project[:, CC:]


def line_blocks(own, first=None):
    y, core = line_index(), lax.axis_index("c")
    blocks, places = [], []

    def place(distance, c):
        at = (y - distance) % 4
        return (at // 2) * 4 + c * 2 + at % 2

    for d in (0, 1, 3, 2):
        got = along_line(own, d) if d else own
        if d and first is not None:
            got = wait_for(got, first)
        blocks += [got, core_swap(got)]
        places += [place(d, core), place(d, 1 - core)]
    return jnp.stack(places).astype(jnp.int32), blocks


X_SCRATCH = pltpu.VMEM((GT, D), bf)


def line_gather_more(own, first):
    places, blocks = line_blocks(own, first)
    return call(
        place_kernel,
        "place_gradient",
        [SMEM] + [whole(TOK + 16, D)] * NG,
        [tok_block(D), whole(NG * 16, D)],
        [struct((GT, D), bf), struct((NG * 16, D), bf)],
        [X_SCRATCH],
        (places, *blocks),
        4,
    )


def line_project(own, weight):
    return place_project(*line_blocks(own), weight)


def place_project(places, blocks, weight):
    return call(
        place_project_kernel,
        "place_project",
        [SMEM] + [whole(TOK, D)] * NG + [whole(D, CA)],
        [tok_block(D), tok_block(CC), tok_block(128)],
        [struct((GT, D), bf), struct((GT, CC), bf), struct((GT, 128), bf)],
        [X_SCRATCH],
        (places, *blocks, weight),
        9,
    )


def chip_kernel(y_ref, mine_ref, got_ref, own_ref, *sent_refs):
    def rows(distance):
        at = pl.multiple_of((y_ref[0] + distance) % 4 * TOK, TOK)
        return mine_ref[pl.ds(at, TOK)].astype(f32) + got_ref[pl.ds(at, TOK)].astype(f32)

    own_ref[...] = rows(0)
    for distance, ref in zip((1, 3, 2), sent_refs):
        ref[...] = rows(distance).astype(bf)


def line_parts(other, mine, first=None):
    got = core_swap(other)
    if first is not None:
        got = wait_for(got, first)
    own, *sent = pl.pallas_call(
        chip_kernel,
        out_shape=[struct((TOK, D))] + [struct((TOK, D), bf)] * 3,
        in_specs=[SMEM] + [pl.BlockSpec(memory_space=pltpu.VMEM)] * 2,
        out_specs=[pl.BlockSpec(memory_space=pltpu.VMEM)] * 4,
        compiler_params=pltpu.CompilerParams(vmem_limit_bytes=SMALL_VMEM),
        name="chip_sum",
    )(line_index().reshape(1).astype(jnp.int32), mine, got)
    return [own] + [along_line(block, d) for block, d in zip(sent, (1, 3, 2))]


def span_order():
    core = lax.axis_index("c")
    return jnp.stack([1 - core, 3 - core, core, 2 + core]).astype(jnp.int32)


def write_half(other_ref, mine_ref, value):
    i = pl.program_id(0)

    @pl.when(i < 2)
    def _():
        other_ref[...] = value

    @pl.when(i >= 2)
    def _():
        mine_ref[...] = value


def parts_sum(refs):
    total = refs[0][...].astype(f32)
    for ref in refs[1:]:
        total = total + ref[...].astype(f32)
    return total


def inverse_rms(a):
    return lax.rsqrt(jnp.mean(a * a, axis=1, keepdims=True) + EPS)


def advance_kernel(p0, p1, p2, p3, square_ref, h_ref, out_ref, branch_ref, normed_ref, scale_ref):
    square = jnp.sum(square_ref[...], axis=0, keepdims=True)
    r_gate = jnp.broadcast_to(lax.rsqrt(square / DI + EPS), (8, TOK))
    scale_ref[...] = r_gate
    branch = parts_sum((p0, p1, p2, p3)) * r_gate.T[:, 0:1]
    h = h_ref[...] + branch
    out_ref[...] = h
    branch_ref[...] = branch
    normed_ref[...] = (h * inverse_rms(h)).astype(bf)


def in_parts(row):
    hi = row.astype(bf).astype(f32)
    mid = (row - hi).astype(bf).astype(f32)
    return [hi, mid, row - hi - mid]


def retreat_kernel(extra, *refs):
    n = 4 if extra else 1
    parts, (h_ref, grad_ref, *refs) = refs[:n], refs[n:]
    h = h_ref[...]
    r_in = inverse_rms(h)
    d_norm = parts_sum(parts)
    inner = jnp.mean(h * d_norm, axis=1, keepdims=True)
    grad = grad_ref[...].astype(f32) + r_in * d_norm - h * (r_in * r_in * r_in * inner)
    if not extra:
        refs[0][...] = grad
        return
    branch_ref, scale_ref, out_ref, sent_ref = refs
    out_ref[...] = grad
    low = grad.astype(bf)
    r_gate = scale_ref[...]
    column = jnp.sum(low.astype(f32) * branch_ref[...], axis=1, keepdims=True)
    row = jnp.broadcast_to(column, (TOK, 128)).T[:8]
    kappa = r_gate * r_gate * row / DI
    rows = in_parts(r_gate) + in_parts(kappa)
    rows = jnp.concatenate(rows + [jnp.zeros((8, D - 6 * TOK), f32)], axis=1)
    sent_ref[:TOK] = low
    sent_ref[TOK:] = jnp.concatenate([rows, jnp.zeros((8, D), f32)], axis=0).astype(bf)


def plain_call(kernel, name, shapes, args):
    return pl.pallas_call(
        kernel,
        out_shape=shapes,
        compiler_params=pltpu.CompilerParams(vmem_limit_bytes=SMALL_VMEM),
        cost_estimate=pl.CostEstimate(
            flops=int(2e8), bytes_accessed=int(1e6), transcendentals=0
        ),
        name=name,
    )(*args)


def to_owners(row):
    return a2a(row.reshape(NG, TOK), LINE)


def to_line(rows):
    m = rows.shape[0]
    return a2a(jnp.broadcast_to(rows[None], (NG,) + rows.shape), LINE).reshape(NG * m, GT)


def rounded(a):
    return lax.reduce_precision(a, exponent_bits=8, mantissa_bits=7)


def group_gather(block):
    return lax.all_gather(block, ZX, axis=0, tiled=True)


def group_gather_now(block):
    r, n = block.shape
    return a2a(jnp.broadcast_to(block[None], (NQ, r, n)), ZX).reshape(NQ * r, n)


def wait_for(value, *others):
    return lax.optimization_barrier((value, others))[0]


def group_reduce(full):
    r = full.shape[0] // NQ
    return jnp.sum(a2a(full.reshape(NQ, r, full.shape[1]), ZX).astype(f32), axis=0)


def heads_out(cols, width):
    r = cols.shape[0]
    return cols.reshape(r, 2, 2, 2, width).transpose(2, 3, 1, 0, 4).reshape(NG, r, width)


def heads_in(blocks):
    _, r, width = blocks.shape
    return blocks.reshape(2, 2, 2, r, width).transpose(3, 2, 0, 1, 4).reshape(r, NG * width)


def line_of(group):
    yl, yh, c = group // 4, (group // 2) % 2, group % 2
    return yh * 4 + c * 2 + yl


TO_HEADS = [(s, (s % NQ) * NG + line_of(s // NQ)) for s in range(NQ * NG)]
TO_OWNER = [(b, a) for a, b in TO_HEADS]


def in_blocks(weight, gain, extra):
    folded = (weight.astype(f32) * gain.astype(f32)[:, None]).astype(bf)
    z = heads_out(folded[:, :DI], W)
    x = heads_out(folded[:, DI : 2 * DI], W)
    bc = jnp.broadcast_to(folded[None, :, 2 * DI : 2 * DI + 2 * N], (NG, 12, 2 * N))
    step = heads_out(folded[:, 2 * DI + 2 * N :], HL)
    extra = jnp.broadcast_to(extra[None], (NG,) + extra.shape)
    step = jnp.concatenate([step, extra], axis=2)
    step = jnp.pad(step, ((0, 0), (0, 0), (0, 128 - step.shape[2])))
    return jnp.concatenate([x, bc, step, z], axis=2)


STATE_ROWS = W + 16


def line_scan_kernel(reverse, at_ref, own_ref, r1, r2, r3, sent_ref, before_ref, decay_ref):
    rank = 3 - at_ref[0] if reverse else at_ref[0]
    blocks = [read_states(ref) for ref in ((r3, r2, r1) if reverse else (r1, r2, r3))]
    own, own_decay = read_states(own_ref)
    state, decay = fold_before(rank, blocks)
    before_ref[...] = state
    decay_ref[...] = jnp.broadcast_to(decay, (8, 128))
    total = by_rows(own_decay, state) + own
    decay = decay * own_decay
    for i in (1, 2, 3):
        next_state, next_decay = blocks[3 - i]
        there = rank + i <= 3
        total = jnp.where(there, by_rows(next_decay, total) + next_state, total)
        decay = jnp.where(there, decay * next_decay, decay)
    write_states(sent_ref, total, decay)


def fold_before(rank, blocks):
    state = jnp.zeros((W, N), f32)
    decay = jnp.ones((1, 128), f32)
    for i in (3, 2, 1):
        block, block_decay = blocks[i - 1]
        there = rank >= i
        state = jnp.where(there, by_rows(block_decay, state) + block, state)
        decay = jnp.where(there, decay * block_decay, decay)
    return state, decay


def final_states(reverse, at_ref, r1, r2, r3, before_ref, decay_ref):
    rank = 3 - at_ref[0] if reverse else at_ref[0]
    blocks = [read_states(ref) for ref in ((r3, r2, r1) if reverse else (r1, r2, r3))]
    entering = fold_before(rank, blocks)[0]
    return by_rows(decay_ref[0:1], entering) + before_ref[...]


def exclusive_scan(sent, reverse, first, second):
    def around(a, axis):
        return [lax.ppermute(a, axis, [(i, (i + d) % 4) for i in range(4)]) for d in (1, 2, 3)]

    def index(axis):
        return lax.axis_index(axis).reshape(1).astype(jnp.int32)

    got = around(sent, "x")
    if first is not None:
        got[0] = wait_for(got[0], first)
    line, before, decay = pl.pallas_call(
        functools.partial(line_scan_kernel, reverse),
        out_shape=[SENT, struct((W, N)), struct((8, 128))],
        in_specs=[SMEM] + [pl.BlockSpec(memory_space=pltpu.VMEM)] * 4,
        out_specs=[pl.BlockSpec(memory_space=pltpu.VMEM)] * 3,
        name="line_scan",
    )(index("x"), sent, *got)
    got = around(line, "z")
    extra = second(line)
    got[0] = wait_for(got[0], extra)
    return (index("z"), *got, before, decay), extra


PAIRS = HL // 2
LAST = NS - 1


def dot(a, b, ca, cb, precision=None):
    return lax.dot_general(
        a, b, (((ca,), (cb,)), ((), ())), preferred_element_type=f32, precision=precision
    )


def by_lanes(cols):
    lane = lax.broadcasted_iota(jnp.int32, (cols.shape[0], 128), 1)
    return jnp.concatenate(
        [
            jnp.where(lane < HP, cols[:, 2 * p : 2 * p + 1], cols[:, 2 * p + 1 : 2 * p + 2])
            for p in range(PAIRS)
        ],
        axis=1,
    )


def by_rows(row, states):
    return jnp.concatenate(
        [row[:, h : h + 1] * states[h * HP : (h + 1) * HP] for h in range(HL)], axis=0
    )


def two_parts(a):
    hi = a.astype(bf)
    return hi, (a - hi.astype(f32)).astype(bf)


def head_sums(wide):
    column = lax.broadcasted_iota(jnp.int32, (W, 128), 0)
    lane = lax.broadcasted_iota(jnp.int32, (W, 128), 1)
    chosen = ((column >= lane * HP) & (column < lane * HP + HP)).astype(f32).astype(bf)
    hi, low = two_parts(wide)
    return dot(hi, chosen, 1, 0) + dot(low, chosen, 1, 0)


def token_sums(wide):
    ones = jnp.ones((8, wide.shape[1]), bf)
    hi, low = two_parts(wide)
    return dot(ones, hi, 1, 1) + dot(ones, low, 1, 1)


def running_sums(chosen, a):
    hi = a.astype(bf).astype(f32)
    mid = (a - hi).astype(bf).astype(f32)
    packed = hi + pltpu.roll(mid, 8, 1) + pltpu.roll(a - hi - mid, 16, 1)
    out = dot(chosen.astype(f32).astype(bf), packed.astype(bf), 1, 0)
    total = out + pltpu.roll(out, 128 - 8, 1) + pltpu.roll(out, 128 - 16, 1)
    lane = lax.broadcasted_iota(jnp.int32, (SPAN, 128), 1)
    return jnp.where(lane < HL, total, 0.0)


def write_states(sent_ref, states, decay):
    lane = lax.broadcasted_iota(jnp.int32, (8, 128), 1)
    decay = jnp.where(lane < HL, jnp.broadcast_to(decay, (8, 128)), 0.0)
    hi = decay.astype(bf).astype(f32)
    mid = (decay - hi).astype(bf).astype(f32)
    low = decay - hi - mid
    tail = hi + pltpu.roll(mid, HL, 1) + pltpu.roll(low, 2 * HL, 1)
    sent_ref[...] = jnp.concatenate([states, tail, tail], axis=0).astype(bf)


def read_states(ref):
    block = ref[...].astype(f32)
    tail = block[W : W + 8]
    decay = tail + pltpu.roll(tail, 128 - HL, 1) + pltpu.roll(tail, 128 - 2 * HL, 1)
    return block[:W], decay[:1]


def span_masks(segc_ref, segr_ref):
    row = lax.broadcasted_iota(jnp.int32, (SPAN, SPAN), 0)
    col = lax.broadcasted_iota(jnp.int32, (SPAN, SPAN), 1)
    return (col <= row) & (segc_ref[...] == segr_ref[0])


def head_decay(mask, run, run_t, h):
    return jnp.exp(jnp.where(mask, run[:, h : h + 1] - run_t[h : h + 1], -1e30))


def end_weights(run, segc_ref, seg_end):
    return jnp.exp(run[SPAN - 1 :] - run) * (segc_ref[...] == seg_end).astype(f32)


def inflow_of(run, segc_ref, seg_before):
    return jnp.exp(run) * (segc_ref[...] == seg_before).astype(f32)


def past_rows(k, u_ref, past_ref, edge_ref):
    past = jnp.where(k == 0, edge_ref[...].astype(f32), past_ref[...].astype(f32))
    return jnp.concatenate([past, u_ref[...].astype(f32)], axis=0)


def back_by(rows, distance):
    return (pltpu.roll(rows, distance, 0) if distance else rows)[16:]


def mix_kernel(
    seg_ref, u_ref, past_ref, edge_ref, same_ref, conv_ref, raw_ref, bias_ref, rate_ref, segc_ref,
    segr_ref, v_ref, pre_ref, within_ref, local_ref, step_ref, run_ref, before_ref, decay_ref, sent_ref, acc_ref, dec_ref,
):
    k = pl.program_id(0)

    @pl.when(k == 0)
    def _():
        acc_ref[...] = jnp.zeros_like(acc_ref)
        dec_ref[...] = jnp.ones_like(dec_ref)

    rows = past_rows(k, u_ref, past_ref, edge_ref)
    pre = jnp.broadcast_to(conv_ref[CONV : CONV + 1], (SPAN, CC))
    for i in range(CONV):
        pre = pre + conv_ref[i : i + 1] * back_by(rows, i) * same_ref[:, i : i + 1]
    pre_ref[...] = pre.astype(bf)
    v_low = silu_both(pre)[0].astype(bf)
    v_ref[...] = v_low
    lane = lax.broadcasted_iota(jnp.int32, (SPAN, 128), 1)
    raw = raw_ref[...].astype(f32) + bias_ref[...]
    step = jnp.where(lane < HL, jax.nn.softplus(raw), 0.0)
    row = lax.broadcasted_iota(jnp.int32, (SPAN, SPAN), 0)
    col = lax.broadcasted_iota(jnp.int32, (SPAN, SPAN), 1)
    run = running_sums(col <= row, rate_ref[...] * step)
    step_ref[...] = step
    run_ref[...] = run
    run_t = run.T
    mask = span_masks(segc_ref, segr_ref)
    xc = v_low[:, :W].astype(f32)
    b_low = v_low[:, W : W + N]
    c_low = v_low[:, W + N :]
    gram = dot(c_low, b_low, 1, 1)
    xs = (by_lanes(step) * xc).astype(bf)
    half = lane < HP
    for p in range(PAIRS):
        cols = slice(p * 128, (p + 1) * 128)
        out = [
            dot((gram * head_decay(mask, run, run_t, h)).astype(bf), xs[:, cols], 1, 0)
            for h in (2 * p, 2 * p + 1)
        ]
        within_ref[:, cols] = jnp.where(half, out[0], out[1])
    w_end = end_weights(run, segc_ref, seg_ref[1, k])
    weighted = (by_lanes(w_end * step) * xc).astype(bf)
    own = dot(weighted, b_low, 0, 0)
    local_ref[0] = acc_ref[...]
    before_ref[0] = dec_ref[...]
    inside = (seg_ref[1, k] == seg_ref[0, k]).astype(f32)
    decay = jnp.exp(run[SPAN - 1 :]) * inside
    decay_ref[0] = decay
    acc = by_rows(decay, acc_ref[...]) + own
    acc_ref[...] = acc
    dec = dec_ref[...] * decay
    dec_ref[...] = dec

    @pl.when(k == LAST)
    def _():
        write_states(sent_ref, acc, dec)


def silu_both(v):
    s = 1.0 / (1.0 + jnp.exp(-v))
    return v * s, s * (1.0 + v * (1.0 - s))


def gate_kernel(
    last, order_ref, seg_ref, at_ref, r1, r2, r3, line_ref, line_decay_ref, local_ref, before_ref, run_ref, v_ref, within_ref, z_ref, segc_ref,
    skip_ref, wo_ref, *rest,
):
    if last:
        dq_ref, y0_ref, part_ref, sums_ref, carry_ref = rest
    else:
        y0_ref, other_ref, mine_ref, sums_ref, carry_ref = rest
    i = pl.program_id(0)
    k = order_ref[i]

    @pl.when(i == 0)
    def _():
        carry_ref[...] = final_states(False, at_ref, r1, r2, r3, line_ref, line_decay_ref)

    carried = (by_rows(before_ref[0], carry_ref[...]) + local_ref[0]).astype(bf)
    xc = v_ref[:, :W].astype(f32)
    c_low = v_ref[:, W + N :]
    reading = dot(c_low, carried, 1, 1)
    y0 = within_ref[...] + by_lanes(inflow_of(run_ref[...], segc_ref, seg_ref[0, k])) * reading
    y0_ref[...] = y0
    mixed = (y0 + skip_ref[...] * xc).astype(bf).astype(f32)
    gated = mixed * silu_both(z_ref[...].astype(f32))[0]
    part = dot(gated.astype(bf), wo_ref[...], 1, 0).astype(bf)
    if last:
        part_ref[...] = part
    else:
        write_half(other_ref, mine_ref, part)
    sums = token_sums(gated * gated)
    if last:
        row = lax.broadcasted_iota(jnp.int32, (8, SPAN), 0)
        sums = jnp.where(row < 1, sums, token_sums(gated * dq_ref[...]))
    sums_ref[...] = sums


def gate_back_kernel(
    last, seg_ref, grad_ref, wo_ref, scale_ref, v_ref, y0_ref, z_ref, run_ref, segc_ref, skip_ref,
    decay_ref, dy_ref, dz_ref, gr_ref, local_ref, after_ref, sent_ref, acc_ref, dec_ref,
):
    i = pl.program_id(0)
    k = LAST - i

    @pl.when(i == 0)
    def _():
        acc_ref[...] = jnp.zeros_like(acc_ref)
        dec_ref[...] = jnp.ones_like(dec_ref)

    if last:
        sums = scale_ref[...]
        odd = lax.broadcasted_iota(jnp.int32, (2 * NG, SPAN), 0) % 2 == 1
        square = jnp.sum(jnp.where(odd, 0.0, sums), axis=0, keepdims=True)
        inner = jnp.sum(jnp.where(odd, sums, 0.0), axis=0, keepdims=True)
        r_row = lax.rsqrt(square / DI + EPS)
        k_row = r_row * r_row * r_row * inner / DI
    else:
        rows = scale_ref[...].astype(f32)
        pieces = [rows[:, i * TOK : (i + 1) * TOK] for i in range(6)]
        r_two = pieces[0] + pieces[1] + pieces[2]
        k_two = pieces[3] + pieces[4] + pieces[5]
        r_row = jnp.concatenate([r_two[0:1], r_two[16:17]], axis=1)
        k_row = jnp.concatenate([k_two[0:1], k_two[16:17]], axis=1)
    r = jnp.broadcast_to(r_row, (8, SPAN)).T[:, 0:1]
    kappa = jnp.broadcast_to(k_row, (8, SPAN)).T[:, 0:1]
    d_q = grad_ref[...] if last else dot(grad_ref[...], wo_ref[...], 1, 1)
    mixed = (y0_ref[...] + skip_ref[...] * v_ref[:, :W].astype(f32)).astype(bf).astype(f32)
    silu, d_silu = silu_both(z_ref[...].astype(f32))
    gated = mixed * silu
    gr_ref[...] = (r * gated).astype(bf)
    d_gated = r * d_q - kappa * gated
    dy = (d_gated * silu).astype(bf)
    dy_ref[...] = dy
    dz_ref[...] = (d_gated * mixed * d_silu).astype(bf)
    inflow = by_lanes(inflow_of(run_ref[...], segc_ref, seg_ref[0, k]))
    scaled = (inflow * dy.astype(f32)).astype(bf)
    d_carried = dot(scaled, v_ref[:, W + N :], 0, 0)
    local_ref[0] = acc_ref[...]
    after_ref[0] = dec_ref[...]
    decay = decay_ref[0]
    acc = by_rows(decay, acc_ref[...]) + d_carried
    acc_ref[...] = acc
    dec = dec_ref[...] * decay
    dec_ref[...] = dec

    @pl.when(i == LAST)
    def _():
        write_states(sent_ref, acc, dec)


def mix_back_kernel(v_ref, step_ref, run_ref, segc_ref, segr_ref, dy_ref, dxs_ref, dbc_ref):
    lane = lax.broadcasted_iota(jnp.int32, (SPAN, 128), 1)
    half = lane < HP
    run = run_ref[...]
    run_t = run.T
    mask = span_masks(segc_ref, segr_ref)
    xs = (by_lanes(step_ref[...]) * v_ref[:, :W].astype(f32)).astype(bf)
    b_low = v_ref[:, W : W + N]
    c_low = v_ref[:, W + N :]
    gram = dot(c_low, b_low, 1, 1)
    d_gram = jnp.zeros((SPAN, SPAN), f32)
    zero = jnp.zeros((SPAN, 128), bf)
    for p in range(PAIRS):
        cols = slice(p * 128, (p + 1) * 128)
        dy = dy_ref[:, cols]
        out = []
        for i, h in enumerate((2 * p, 2 * p + 1)):
            decay = head_decay(mask, run, run_t, h)
            mixing = (gram * decay).astype(bf)
            dy_one = jnp.where(half, dy, zero) if i == 0 else jnp.where(half, zero, dy)
            d_gram = d_gram + dot(dy_one, xs[:, cols], 1, 1) * decay
            out.append(dot(mixing, dy, 0, 0))
        dxs_ref[:, cols] = jnp.where(half, out[0], out[1])
    d_gram = d_gram.astype(bf)
    dbc_ref[:, :N] = dot(d_gram, c_low, 0, 0).astype(bf)
    dbc_ref[:, N:] = dot(d_gram, b_low, 1, 0).astype(bf)


def end_kernel(
    seg_ref, at_ref, r1, r2, r3, line_ref, line_decay_ref, carry_ref, local_ref, before_ref, dlocal_ref, after_ref, decay_ref, v_ref,
    pre_ref, raw_ref, bias_ref, rate_ref, step_ref, run_ref, segc_ref, skip_ref, dy_ref, dxs_ref,
    dbc_ref, y0_ref, dpre_ref, draw_ref, sums_ref, later_s,
):
    k = pl.program_id(0)

    @pl.when(k == 0)
    def _():
        later_s[...] = final_states(True, at_ref, r1, r2, r3, line_ref, line_decay_ref)
        sums_ref[...] = jnp.zeros_like(sums_ref)

    d_end = by_rows(after_ref[0], later_s[...]) + dlocal_ref[0]
    carried = by_rows(before_ref[0], carry_ref[...]) + local_ref[0]
    d_end_low = d_end.astype(bf)
    run, step, rate = run_ref[...], step_ref[...], rate_ref[...]
    xc = v_ref[:, :W].astype(f32)
    b_low = v_ref[:, W : W + N]
    dy = dy_ref[...].astype(f32)
    dxs = dxs_ref[...]
    step_x = by_lanes(step)
    xs = (step_x * xc).astype(bf).astype(f32)
    w_end = end_weights(run, segc_ref, seg_ref[1, k])
    weights_x = by_lanes(w_end * step)
    weighted = (weights_x * xc).astype(bf)
    scaled = (by_lanes(inflow_of(run, segc_ref, seg_ref[0, k])) * dy).astype(bf)
    d_weighted = dot(b_low, d_end_low, 1, 1)
    d_b = dbc_ref[:, :N].astype(f32) + dot(weighted, d_end_low, 1, 0)
    d_c = dbc_ref[:, N:].astype(f32) + dot(scaled, carried.astype(bf), 1, 0)
    d_xc = skip_ref[...] * dy + step_x * dxs + weights_x * d_weighted
    dv = jnp.concatenate([d_xc, d_b, d_c], axis=1)
    dpre_ref[...] = (dv * silu_both(pre_ref[...].astype(f32))[1]).astype(bf)
    skip_sum = head_sums(dy * xc)
    d_run = head_sums(dy * y0_ref[...] - xs * dxs)
    d_step = head_sums(xc * dxs)
    d_w = head_sums(d_weighted * xc)
    product = d_end * carried
    lane1 = lax.broadcasted_iota(jnp.int32, (1, 128), 1)
    d_span = jnp.zeros((1, 128), f32)
    for h in range(HL):
        rows = jnp.sum(product[h * HP : (h + 1) * HP], axis=0, keepdims=True)
        d_span = d_span + jnp.where(lane1 == h, jnp.sum(rows, axis=1, keepdims=True), 0.0)
    d_step = d_step + d_w * w_end
    d_ww = d_w * w_end * step
    d_run = d_run - d_ww
    d_last = jnp.sum(d_ww, axis=0, keepdims=True) + d_span * decay_ref[0]
    row = lax.broadcasted_iota(jnp.int32, (SPAN, SPAN), 0)
    col = lax.broadcasted_iota(jnp.int32, (SPAN, SPAN), 1)
    d_a = running_sums(col >= row, d_run) + d_last
    d_step = d_step + rate * d_a
    raw = raw_ref[...].astype(f32) + bias_ref[...]
    lane = lax.broadcasted_iota(jnp.int32, (SPAN, 128), 1)
    d_raw = jnp.where(lane < HL, d_step / (1.0 + jnp.exp(-raw)), 0.0)
    draw_ref[...] = d_raw.astype(bf)
    sums = jnp.concatenate(
        [
            jnp.sum(d_raw, axis=0, keepdims=True),
            rate * jnp.sum(step * d_a, axis=0, keepdims=True),
            jnp.sum(skip_sum, axis=0, keepdims=True),
            jnp.zeros((5, 128), f32),
        ],
        axis=0,
    )
    sums_ref[...] = sums_ref[...] + sums


def conv_back_kernel(
    first, order_ref, dpre_ref, next_ref, after_ref, u_ref, past_ref, edge_ref, same_ref, conv_ref, draw_ref, dz_ref,
    wa_ref, wz_ref, da_ref, *outs,
):
    taps_ref = outs[-1]
    i = pl.program_id(0)
    k = order_ref[i]

    @pl.when(i == 0)
    def _():
        taps_ref[...] = jnp.zeros_like(taps_ref)

    d_pre = dpre_ref[...].astype(f32)
    later = jnp.where(k == LAST, after_ref[...].astype(f32), next_ref[...].astype(f32))
    d_rows = jnp.concatenate([d_pre, later], axis=0)
    rows = past_rows(k, u_ref, past_ref, edge_ref)
    du = jnp.zeros((SPAN, CC), f32)
    taps = []
    for tap in range(CONV):
        ahead = pltpu.roll(d_rows, SPAN + 16 - tap, 0) if tap else d_rows
        same = same_ref[:, CONV + tap : CONV + tap + 1]
        du = du + conv_ref[tap : tap + 1] * ahead[:SPAN] * same
        product = d_pre * back_by(rows, tap) * same_ref[:, tap : tap + 1]
        taps.append(jnp.sum(product, axis=0, keepdims=True))
    taps.append(jnp.sum(d_pre, axis=0, keepdims=True))
    taps.append(jnp.zeros((3, CC), f32))
    taps_ref[...] = taps_ref[...] + jnp.concatenate(taps, axis=0)
    da = jnp.concatenate([du.astype(bf), draw_ref[...]], axis=1)
    da_ref[...] = da
    part = dot(da, wa_ref[...], 1, 1) + dot(dz_ref[...], wz_ref[...], 1, 1)
    if first:
        outs[0][...] = part.astype(bf)
    else:
        write_half(*outs[:2], part.astype(bf))


def tok_block(n, reverse=False):
    return pl.BlockSpec((SPAN, n), lambda k: (LAST - k if reverse else k, 0))


def span_block(rows, n, reverse=False):
    return pl.BlockSpec((1, rows, n), lambda k: (LAST - k if reverse else k, 0, 0))


def whole(*shape):
    return pl.BlockSpec(shape, lambda k: (0,) * len(shape))


STATE = struct((NS, W, N))
ROW = struct((NS, 1, 128))
SENT = struct((STATE_ROWS, N), bf)
STATE_SCRATCH = pltpu.VMEM((W, N), f32)


def call(kernel, name, ins, outs, shapes, scratch, args, us, vmem=VMEM_BYTES):
    return pl.pallas_call(
        kernel,
        grid=(NS,),
        in_specs=ins,
        out_specs=outs,
        out_shape=shapes,
        scratch_shapes=scratch,
        compiler_params=pltpu.CompilerParams(
            dimension_semantics=("arbitrary",), vmem_limit_bytes=vmem
        ),
        cost_estimate=pl.CostEstimate(
            flops=int(us * 4e7), bytes_accessed=int(us * 2e5), transcendentals=0
        ),
        name=name,
    )(*args)


def ordered_call(kernel, name, ins, outs, shapes, scratch, args, us):
    return pl.pallas_call(
        kernel,
        grid_spec=pltpu.PrefetchScalarGridSpec(
            num_scalar_prefetch=1, grid=(NS,), in_specs=ins, out_specs=outs, scratch_shapes=scratch
        ),
        out_shape=shapes,
        compiler_params=pltpu.CompilerParams(
            dimension_semantics=("arbitrary",), vmem_limit_bytes=VMEM_BYTES
        ),
        cost_estimate=pl.CostEstimate(
            flops=int(us * 4e7), bytes_accessed=int(us * 2e5), transcendentals=0
        ),
        name=name,
    )(span_order(), *args)


def tok_at(n):
    return pl.BlockSpec((SPAN, n), lambda i, order: (order[i], 0))


def span_at(rows, n):
    return pl.BlockSpec((1, rows, n), lambda i, order: (order[i], 0, 0))


def whole_at(*shape):
    return pl.BlockSpec(shape, lambda i, order: (0,) * len(shape))


HALVES = [
    pl.BlockSpec((SPAN, D), lambda i, order: (jnp.minimum(i, 1), 0)),
    pl.BlockSpec((SPAN, D), lambda i, order: (jnp.maximum(i - 2, 0), 0)),
]
HALF_SHAPES = [struct((GT // 2, D), bf)] * 2


def past_block(n):
    return pl.BlockSpec((16, n), lambda k: (jnp.maximum(k * (SPAN // 16) - 1, 0), 0))


def span_mix(seg, u, edge, same, conv, raw, bias, rate, segc, segr):
    return call(
        mix_kernel,
        "span_mix",
        [SMEM, tok_block(CC), past_block(CC), whole(16, CC), tok_block(8), whole(8, CC),
         tok_block(128), whole(1, 128), whole(1, 128), tok_block(1), span_block(1, SPAN)],
        [tok_block(CC), tok_block(CC), tok_block(W), span_block(W, N), tok_block(128),
         tok_block(128), span_block(1, 128), span_block(1, 128), whole(STATE_ROWS, N)],
        [struct((GT, CC), bf), struct((GT, CC), bf), struct((GT, W)), STATE, struct((GT, 128)),
         struct((GT, 128)), ROW, ROW, SENT],
        [STATE_SCRATCH, pltpu.VMEM((1, 128), f32)],
        (seg, u, u, edge, same, conv, raw, bias, rate, segc, segr),
        10,
    )


def conv_back(first, d_pre, after, u, edge, same, conv, d_raw, dz, wa, wz, at):
    following = pl.BlockSpec(
        (16, CC), lambda i, order: (jnp.minimum((order[i] + 1) * (SPAN // 16), GT // 16 - 1), 0)
    )
    past = pl.BlockSpec(
        (16, CC), lambda i, order: (jnp.maximum(order[i] * (SPAN // 16) - 1, 0), 0)
    )
    return ordered_call(
        functools.partial(conv_back_kernel, first),
        "conv_back",
        [tok_at(CC), following, whole_at(16, CC), tok_at(CC), past, whole_at(16, CC), tok_at(8),
         whole_at(8, CC), tok_at(128), tok_at(W), whole_at(D, CA),
         pl.BlockSpec((D, W), lambda i, order: (0, at))],
        [tok_at(CA)] + ([tok_at(D)] if first else HALVES) + [whole_at(8, CC)],
        [struct((GT, CA), bf)] + ([struct((GT, D), bf)] if first else HALF_SHAPES)
        + [struct((8, CC))],
        [],
        (d_pre, d_pre, after, u, u, edge, same, conv, d_raw, dz, wa, wz),
        10,
    )


def span_gate(seg, back, local, before, run, v, within, z, segc, skip, wo, d_q):
    last = d_q is not None
    ins = [SMEM, SMEM] + [whole_at(STATE_ROWS, N)] * 3 + [
           whole_at(W, N), whole_at(8, 128), span_at(W, N), span_at(1, 128), tok_at(128), tok_at(CC),
           tok_at(W), tok_at(W), tok_at(1), whole_at(1, W), whole_at(W, D)]
    args = (seg, *back, local, before, run, v, within, z, segc, skip, wo)
    return ordered_call(
        functools.partial(gate_kernel, last),
        "span_gate",
        ins + [tok_at(W)] if last else ins,
        [tok_at(W)] + ([tok_at(D)] if last else HALVES)
        + [pl.BlockSpec((8, SPAN), lambda i, order: (0, order[i])), whole_at(W, N)],
        [struct((GT, W))] + ([struct((GT, D), bf)] if last else HALF_SHAPES)
        + [struct((8, GT)), struct((W, N))],
        [],
        args + (d_q,) if last else args,
        10,
    )


def span_gate_back(last, seg, grad, wo, scales, v, y0, z, run, segc, skip, decay):
    if last:
        scale_block = pl.BlockSpec((2 * NG, SPAN), lambda k: (0, LAST - k))
    else:
        scale_block = pl.BlockSpec((32, D), lambda k: (LAST - k, 0))
    return call(
        functools.partial(gate_back_kernel, last),
        "span_gate_back",
        [SMEM, tok_block(W if last else D, True), whole(W, D), scale_block,
         tok_block(CC, True), tok_block(W, True), tok_block(W, True), tok_block(128, True),
         tok_block(1, True), whole(1, W), span_block(1, 128, True)],
        [tok_block(W, True), tok_block(W, True), tok_block(W, True), span_block(W, N, True),
         span_block(1, 128, True), whole(STATE_ROWS, N)],
        [struct((GT, W), bf), struct((GT, W), bf), struct((GT, W), bf), STATE, ROW, SENT],
        [STATE_SCRATCH, pltpu.VMEM((1, 128), f32)],
        (seg, grad, wo, scales, v, y0, z, run, segc, skip, decay),
        12,
    )


def span_mix_back(v, step, run, segc, segr, dy):
    return call(
        mix_back_kernel,
        "span_mix_back",
        [tok_block(CC), tok_block(128), tok_block(128), tok_block(1), span_block(1, SPAN),
         tok_block(W)],
        [tok_block(W), tok_block(2 * N)],
        [struct((GT, W)), struct((GT, 2 * N), bf)],
        [],
        (v, step, run, segc, segr, dy),
        14,
    )


def span_end(seg, later, back, local, before, dlocal, after, decay, v, pre, raw, bias, rate, step,
             run, segc, skip, dy, dxs, dbc, y0):
    return call(
        end_kernel,
        "span_end",
        [SMEM, SMEM] + [whole(STATE_ROWS, N)] * 3 + [
         whole(W, N), whole(8, 128), whole(W, N), span_block(W, N), span_block(1, 128),
         span_block(W, N), span_block(1, 128), span_block(1, 128), tok_block(CC), tok_block(CC),
         tok_block(128), whole(1, 128), whole(1, 128), tok_block(128), tok_block(128),
         tok_block(1), whole(1, W), tok_block(W), tok_block(W), tok_block(2 * N), tok_block(W)],
        [tok_block(CC), tok_block(128), whole(8, 128)],
        [struct((GT, CC), bf), struct((GT, 128), bf), struct((8, 128))],
        [STATE_SCRATCH],
        (seg, *later, back, local, before, dlocal, after, decay, v, pre, raw, bias, rate, step, run,
         segc, skip, dy, dxs, dbc, y0),
        16,
    )


def group_reduce_blocks(sent):
    return jnp.sum(a2a(sent, ZX).astype(f32), axis=0)


SMALL = CC + HL


def small_block(conv_grads, head_grads):
    own_ch = CH // (NQ * NG)
    conv = jnp.stack(conv_grads).reshape(LAYERS * (CONV + 1), NQ * NG, own_ch)
    conv = jnp.pad(conv.transpose(1, 0, 2), ((0, 0), (0, 12 - LAYERS * (CONV + 1)), (0, 0)))
    head = jnp.stack(head_grads, axis=1)
    high = rounded(head)
    head = jnp.concatenate([high, head - high], axis=1)
    head = jnp.tile(head, (NQ * NG // 2, 1, 1))
    head = jnp.pad(head, ((0, 0), (0, 12 - 2 * LAYERS), (0, 0)))
    block = jnp.concatenate([conv, head], axis=2).reshape(D, own_ch + 3 * H // 2)
    return jnp.pad(block.astype(bf), ((0, 0), (SMALL, CA - SMALL - block.shape[1])))


def per_device(
    tokens,
    doc_starts,
    norm_gain,
    in_weight,
    conv_weight,
    conv_bias,
    step_bias,
    decay_log,
    skip_gain,
    gate_gain,
    out_weight,
    cotangent,
):
    q = lax.axis_index(ZX)
    yh, core, yl = lax.axis_index("yh"), lax.axis_index("c"), lax.axis_index("yl")
    sub = yh * 2 + core
    group = yl * 4 + sub

    own_ch = CH // (NQ * NG)
    conv_own = jnp.concatenate([conv_weight, conv_bias[:, None]], axis=1).reshape(-1, own_ch)
    conv_own = jnp.pad(conv_own, ((0, 12 - conv_own.shape[0]), (0, 0)))
    sent = [in_blocks(in_weight[l], norm_gain[l], conv_own if l == 0 else conv_own[:, :0]) for l in range(LAYERS)]
    sent = jnp.stack(sent, axis=1)
    got = a2a(sent, LINE)
    in_0 = got[:, 0].reshape(NG * 12, CA + W)
    in_1 = got[:, 1].reshape(NG * 12, CA + W)
    own_0 = jnp.broadcast_to(in_0[None, :, :CA], (NQ, NG * 12, CA))
    w_a0 = a2a(own_0, ZX).reshape(D, CA)
    h = tokens.astype(f32)
    normed = (h * lax.rsqrt(jnp.mean(h * h, axis=-1, keepdims=True) + EPS)).astype(bf)
    pos = q * GT + jnp.arange(-(CONV - 1), GT + CONV - 1, dtype=jnp.int32)
    seg_ext = jnp.sum((doc_starts[None, :] <= pos[:, None]).astype(jnp.int32), axis=1) - 1
    seg = seg_ext[CONV - 1 : CONV - 1 + GT]
    seg_spans = seg.reshape(NS, SPAN)
    seg_before = seg_ext[CONV - 2 : CONV - 2 + GT : SPAN]
    seg_ends = jnp.stack([seg_before, seg_spans[:, -1]])
    seg_col, seg_row = seg[:, None], seg_spans[:, None, :]
    same = jnp.stack(
        [seg_ext[CONV - 1 - k : CONV - 1 - k + GT] == seg for k in range(CONV)]
        + [seg_ext[CONV - 1 + k : CONV - 1 + k + GT] == seg for k in range(CONV)],
        axis=1,
    ).astype(f32)

    def pick_heads(a):
        own = lax.dynamic_slice_in_dim(a, sub * HL, HL, 0)
        return jnp.pad(own, (0, 128 - HL))[None]

    onward = [(i, i + 1) for i in range(NQ - 1)]
    consts = []
    for l in range(LAYERS):
        rate = jnp.where(jnp.arange(128)[None] < HL, -jnp.exp(pick_heads(decay_log[l])), 0.0)
        skip_x = jnp.repeat(lax.dynamic_slice_in_dim(skip_gain[l], sub * HL, HL, 0), HP)[None]
        consts.append((pick_heads(step_bias[l]), rate, skip_x))
    prepared = own_0, consts, same, seg_ends, seg_col, seg_row, span_order()
    places, blocks = line_blocks(wait_for(normed, got), prepared)
    folded_out = (out_weight.astype(f32) * gate_gain.astype(f32)[:, :, None]).astype(bf)
    out_blocks = lax.ppermute(folded_out, AX, TO_HEADS)
    zo = jnp.concatenate([in_0[:, CA:], out_blocks.reshape(192, W)], axis=0)
    grad_full = lax.all_gather(cotangent, LINE, axis=0, tiled=True)
    w_a0 = wait_for(w_a0, zo)
    normed, u, raw = place_project(places, blocks, w_a0)
    tail = u[GT - 16 :]
    conv_all = wait_for(w_a0, tail)[:, SMALL : SMALL + own_ch].reshape(NQ * NG, 12, own_ch)
    conv_all = conv_all[:, : LAYERS * (CONV + 1)].transpose(1, 0, 2)
    conv_all = conv_all.reshape(LAYERS, CONV + 1, CH).astype(f32)
    conv_x = lax.dynamic_slice_in_dim(conv_all, group * W, W, 2)
    conv_here = jnp.concatenate([conv_x, conv_all[:, :, DI:]], axis=2)
    conv_here = jnp.pad(conv_here, ((0, 0), (0, 7 - CONV), (0, 0)))
    zo = group_gather(wait_for(zo, tail)).reshape(NQ, 288, W)
    w_z0 = zo[:, :96].reshape(D, W)
    w_o = [zo[:, 96:192].reshape(W, D), None]
    w_in1 = group_gather(wait_for(in_1, tail))
    saved = []
    for l in range(LAYERS):
        bias_h, rate, skip_x = consts[l]
        if l > 0:
            normed, u, raw = line_project(normed, w_in1)
        edge = lax.ppermute(u[GT - 16 :], ZX, onward)
        v, pre, within, local, step, run, before, decay, sent = span_mix(
            seg_ends, u, edge, same, conv_here[l], raw, bias_h, rate, seg_col, seg_row
        )
        if l == 0:
            w_o[1] = wait_for(zo, v)[:, 192:].reshape(W, D)
            d_q = None
            back, z = exclusive_scan(
                sent, False, None, lambda outs: mm(wait_for(normed, outs), w_z0).astype(bf)
            )
        else:
            z = mm(normed, w_in1[:, CA:]).astype(bf)
            back, d_q = exclusive_scan(
                sent, False, z, lambda outs: mm(wait_for(grad_full, outs), w_o[1], 1, 1)
            )
        y0, *parts, sums, carry = span_gate(
            seg_ends, back, local, before, run, v, within, z, seg_col, skip_x, w_o[l],
            d_q,
        )
        saved.append(
            dict(
                h=h, normed=normed, u=u, edge=edge, pre=pre, v=v, z=z, raw=raw, bias_h=bias_h,
                rate=rate, skip_x=skip_x, step=step, run=run, before=before, decay=decay,
                local=local, carry=carry, y0=y0,
            )
        )
        if l < LAYERS - 1:
            parts = line_parts(*parts)
            square = wait_for(to_owners(sums[0]), *parts[1:])
            h, branch, normed, r_gate = plain_call(
                advance_kernel,
                "advance",
                [struct((TOK, D)), struct((TOK, D)), struct((TOK, D), bf), struct((8, TOK))],
                (*parts, square, h),
            )
        else:
            scales = to_line(sums[:2])
            at = (line_index() // 2 * 4 + core * 2 + yl) * TOK
            square = lax.dynamic_slice_in_dim(scales, at, TOK, 1)
            square = jnp.sum(square.reshape(NG, 2, TOK)[:, 0], axis=0)
            r_last = lax.rsqrt(square / DI + EPS)[:, None]
            total = lax.psum_scatter(parts[0], LINE, scatter_dimension=0, tiled=True)
            output = (h + total.astype(f32) * r_last).astype(bf)

    grad = cotangent
    conv_grads, head_grads = [None] * LAYERS, [None] * LAYERS
    a_sums, z_sums, out_sums = ([None] * LAYERS for _ in range(3))
    for l in reversed(range(LAYERS)):
        s = saved[l]
        dy, dz, gr, dlocal, after, sent = span_gate_back(
            l == LAYERS - 1, seg_ends, d_q if l else grad_full, w_o[l], scales, s["v"], s["y0"], s["z"], s["run"],
            seg_col, s["skip_x"], s["decay"],
        )
        z_part = mm(s["normed"], dz, 0, 0).astype(bf).reshape(NQ, 96, W)

        def out_blocks_of(outs):
            low = wait_for(gr, outs)
            return [
                mm(low, grad_full[:, i * W : (i + 1) * W], 0, 0).astype(bf).reshape(NQ, 24, W)
                for i in range(D // W)
            ]

        later, out_part = exclusive_scan(sent, True, z_part, out_blocks_of)
        sums = jnp.concatenate([z_part, *out_part], axis=1)
        both = group_reduce_blocks(wait_for(sums, later))
        dxs, dbc = span_mix_back(s["v"], s["step"], s["run"], seg_col, seg_row, wait_for(dy, sums))
        d_pre, d_raw, head_sum = span_end(
            seg_ends, later, s["carry"], s["local"], s["before"], dlocal, after, s["decay"], s["v"],
            s["pre"], s["raw"], s["bias_h"], s["rate"], s["step"], s["run"], seg_col, s["skip_x"],
            dy, dxs, dbc, s["y0"],
        )
        following = lax.ppermute(d_pre[:16], ZX, [(b, a) for a, b in onward])
        z_sums[l] = both[:96]
        out_sums[l] = both[96:].reshape(4, 24, W).transpose(1, 0, 2).reshape(24, D)
        if l == LAYERS - 1:
            w_a, w_z, at = w_in1, w_in1, CA // W
        else:
            w_a, w_z, at = w_a0, w_z0, 0
        da, *parts, taps = conv_back(
            l == 0, d_pre, following, s["u"], s["edge"], same, conv_here[l], d_raw, dz, w_a, w_z, at
        )
        conv_full = jnp.zeros((CONV + 1, CH), f32)
        conv_full = lax.dynamic_update_slice_in_dim(
            conv_full, taps[: CONV + 1, :W], group * W, 1
        )
        conv_grads[l] = conv_full.at[:, DI:].set(taps[: CONV + 1, W:])
        head_full = lax.dynamic_update_slice_in_dim(
            jnp.zeros((3, H), f32), head_sum[:3, :HL], group * HL, 1
        )
        head_grads[l] = head_full.reshape(3, 2, H // 2).transpose(1, 0, 2).reshape(2, 3 * H // 2)
        a_part = mm(s["normed"], da, 0, 0)
        if l == 0:
            a_part = a_part + small_block(conv_grads, head_grads).astype(f32)
        a_part = a_part.astype(bf)
        if l == 0:
            parts = [lax.psum_scatter(parts[0], LINE, scatter_dimension=0, tiled=True)]
            a_sums[l] = group_reduce(a_part)
        else:
            parts = line_parts(*parts, output)
            a_sums[l] = group_reduce(wait_for(a_part, parts[0]))
        if l > 0:
            grad, block = plain_call(
                functools.partial(retreat_kernel, True),
                "retreat",
                [struct((TOK, D)), struct((TOK + 16, D), bf)],
                (*parts, s["h"], grad, branch, r_gate),
            )
            early = jnp.concatenate([a_sums[1], z_sums[1]], axis=1).reshape(NG, 12, CA + W)
            grad_full, scales = line_gather_more(block, early)
            early = a2a(early, LINE)
            scales = wait_for(scales, early)
        else:
            grad = plain_call(
                functools.partial(retreat_kernel, False),
                "retreat_last",
                struct((TOK, D)),
                (*parts, s["h"], grad),
            )

    out_sums = [
        lax.ppermute(wait_for(out_sums[l], a_part if l else a_sums[0]), AX, TO_OWNER)
        for l in range(LAYERS)
    ]
    late = jnp.concatenate([a_sums[0], z_sums[0]], axis=1)
    late = a2a(late.reshape(NG, 12, CA + W), LINE)
    small = jnp.sum(late[:, :, SMALL:CA], axis=0)
    in_grads, gain_grads, out_grads, gate_grads = ([None] * LAYERS for _ in range(4))
    for l in range(LAYERS):
        got = (late, early)[l]
        a_piece, z_piece = got[:, :, :CA], got[:, :, CA:]
        g_in = jnp.concatenate(
            [
                heads_in(z_piece),
                heads_in(a_piece[:, :, :W]),
                jnp.sum(a_piece[:, :, W:CC], axis=0),
                heads_in(a_piece[:, :, CC : CC + HL]),
            ],
            axis=1,
        )
        in_grads[l] = g_in * norm_gain[l].astype(f32)[:, None]
        gain_grads[l] = jnp.sum(g_in * in_weight[l].astype(f32), axis=1)
        g_out = out_sums[l]
        out_grads[l] = g_out * gate_gain[l].astype(f32)[:, None]
        gate_grads[l] = jnp.sum(g_out * out_weight[l].astype(f32), axis=1)

    conv_grad = small[: LAYERS * (CONV + 1), :own_ch].reshape(LAYERS, CONV + 1, own_ch)
    head_grad = small[:LAYERS] + small[LAYERS : 2 * LAYERS]
    head_grad = head_grad[:, own_ch : own_ch + 3 * H // 2].reshape(LAYERS, 3, H // 2)
    return (
        output,
        grad,
        jnp.stack(gain_grads),
        jnp.stack(in_grads),
        conv_grad[:, :CONV],
        conv_grad[:, CONV],
        head_grad[:, 0],
        head_grad[:, 1],
        head_grad[:, 2],
        jnp.stack(gate_grads),
        jnp.stack(out_grads),
    )


def solution(mesh):
    fine = Mesh(mesh.devices.reshape(4, 4, 2, 2, 2), AX)
    tok, last, mid, heads = P(AX, None), P(None, AX), P(None, AX, None), P(None, "yl")
    conv = P(None, None, AX)
    return jax.shard_map(
        per_device,
        mesh=fine,
        in_specs=(tok, P(), last, mid, conv, last, heads, heads, heads, last, mid, tok),
        out_specs=(tok, tok, last, mid, conv, last, heads, heads, heads, last, mid),
        check_vma=False,
    )
```

```python
import functools

import jax
import jax.numpy as jnp
from jax import lax
from jax.experimental import pallas as pl
from jax.experimental.pallas import tpu as pltpu
from jax.sharding import Mesh, PartitionSpec as P

D = 1536
DI = 3072
H = 48
HP = 64
N = 128
CONV = 4
LAYERS = 2
CH = DI + 2 * N
EPS = 1e-05

AX = ("z", "x", "yh", "c", "yl")
ZX = ("z", "x")
LINE = ("yh", "c", "yl")
Y = ("yh", "yl")
NQ = 16
NG = 8
TOK = 128
GT = TOK * NG
SPAN = 256
NS = GT // SPAN
HL = H // NG
W = HL * HP
CC = W + 2 * N
CA = CC + 128

bf = jnp.bfloat16
f32 = jnp.float32
HI = lax.Precision.HIGHEST


SMEM = pl.BlockSpec(memory_space=pltpu.SMEM)
VMEM_BYTES = 60 * 1024 * 1024
SMALL_VMEM = 16 * 1024 * 1024


def struct(shape, dtype=f32):
    return jax.ShapeDtypeStruct(shape, dtype)


def mm(a, b, ca=1, cb=0):
    return lax.dot_general(a, b, (((ca,), (cb,)), ((), ())), preferred_element_type=f32)


def a2a(a, axes):
    return lax.all_to_all(a, axes, 0, 0, tiled=True)


def core_swap(a):
    return lax.ppermute(a, "c", [(0, 1), (1, 0)])


def line_index():
    return lax.axis_index("yh") * 2 + lax.axis_index("yl")


def along_line(a, distance):
    return lax.ppermute(a, Y, [(i, (i + distance) % 4) for i in range(4)])


def fill_places(pos_ref, blocks, x_ref):
    for i, block in enumerate(blocks):
        at = pl.multiple_of(pos_ref[i] * TOK, TOK)
        x_ref[pl.ds(at, TOK)] = block[:TOK]


def place_kernel(pos_ref, *refs):
    blocks, (out_ref, extra_ref, x_ref) = refs[:NG], refs[NG:]
    k = pl.program_id(0)

    @pl.when(k == 0)
    def _():
        fill_places(pos_ref, blocks, x_ref)
        for i, block in enumerate(blocks):
            extra_ref[pl.ds(pl.multiple_of(pos_ref[i] * 16, 16), 16)] = block[TOK:]

    out_ref[...] = x_ref[pl.ds(pl.multiple_of(k * SPAN, SPAN), SPAN)]


def place_project_kernel(pos_ref, *refs):
    blocks, (w_ref, out_ref, u_ref, raw_ref, x_ref) = refs[:NG], refs[NG:]
    k = pl.program_id(0)

    @pl.when(k == 0)
    def _():
        fill_places(pos_ref, blocks, x_ref)

    x = x_ref[pl.ds(pl.multiple_of(k * SPAN, SPAN), SPAN)]
    out_ref[...] = x
    project = jnp.dot(x, w_ref[...], preferred_element_type=f32).astype(bf)
    u_ref[...] = project[:, :CC]
    raw_ref[...] = project[:, CC:]


def line_blocks(own, first=None):
    y, core = line_index(), lax.axis_index("c")
    blocks, places = [], []

    def place(distance, c):
        at = (y - distance) % 4
        return (at // 2) * 4 + c * 2 + at % 2

    for d in (0, 1, 3, 2):
        got = along_line(own, d) if d else own
        if d and first is not None:
            got = wait_for(got, first)
        blocks += [got, core_swap(got)]
        places += [place(d, core), place(d, 1 - core)]
    return jnp.stack(places).astype(jnp.int32), blocks


X_SCRATCH = pltpu.VMEM((GT, D), bf)


def line_gather_more(own, first):
    places, blocks = line_blocks(own, first)
    return call(
        place_kernel,
        "place_gradient",
        [SMEM] + [whole(TOK + 16, D)] * NG,
        [tok_block(D), whole(NG * 16, D)],
        [struct((GT, D), bf), struct((NG * 16, D), bf)],
        [X_SCRATCH],
        (places, *blocks),
        4,
    )


def line_project(own, weight):
    return place_project(*line_blocks(own), weight)


def place_project(places, blocks, weight):
    return call(
        place_project_kernel,
        "place_project",
        [SMEM] + [whole(TOK, D)] * NG + [whole(D, CA)],
        [tok_block(D), tok_block(CC), tok_block(128)],
        [struct((GT, D), bf), struct((GT, CC), bf), struct((GT, 128), bf)],
        [X_SCRATCH],
        (places, *blocks, weight),
        9,
    )


def chip_kernel(y_ref, mine_ref, got_ref, own_ref, *sent_refs):
    def rows(distance):
        at = pl.multiple_of((y_ref[0] + distance) % 4 * TOK, TOK)
        return mine_ref[pl.ds(at, TOK)].astype(f32) + got_ref[pl.ds(at, TOK)].astype(f32)

    own_ref[...] = rows(0)
    for distance, ref in zip((1, 3, 2), sent_refs):
        ref[...] = rows(distance).astype(bf)


def line_parts(other, mine, first=None):
    got = core_swap(other)
    if first is not None:
        got = wait_for(got, first)
    own, *sent = pl.pallas_call(
        chip_kernel,
        out_shape=[struct((TOK, D))] + [struct((TOK, D), bf)] * 3,
        in_specs=[SMEM] + [pl.BlockSpec(memory_space=pltpu.VMEM)] * 2,
        out_specs=[pl.BlockSpec(memory_space=pltpu.VMEM)] * 4,
        compiler_params=pltpu.CompilerParams(vmem_limit_bytes=SMALL_VMEM),
        name="chip_sum",
    )(line_index().reshape(1).astype(jnp.int32), mine, got)
    return [own] + [along_line(block, d) for block, d in zip(sent, (1, 3, 2))]


def span_order():
    core = lax.axis_index("c")
    return jnp.stack([1 - core, 3 - core, core, 2 + core]).astype(jnp.int32)


def write_half(other_ref, mine_ref, value):
    i = pl.program_id(0)

    @pl.when(i < 2)
    def _():
        other_ref[...] = value

    @pl.when(i >= 2)
    def _():
        mine_ref[...] = value


def parts_sum(refs):
    total = refs[0][...].astype(f32)
    for ref in refs[1:]:
        total = total + ref[...].astype(f32)
    return total


def inverse_rms(a):
    return lax.rsqrt(jnp.mean(a * a, axis=1, keepdims=True) + EPS)


def advance_kernel(p0, p1, p2, p3, square_ref, h_ref, out_ref, branch_ref, normed_ref, scale_ref):
    square = jnp.sum(square_ref[...], axis=0, keepdims=True)
    r_gate = jnp.broadcast_to(lax.rsqrt(square / DI + EPS), (8, TOK))
    scale_ref[...] = r_gate
    branch = parts_sum((p0, p1, p2, p3)) * r_gate.T[:, 0:1]
    h = h_ref[...] + branch
    out_ref[...] = h
    branch_ref[...] = branch
    normed_ref[...] = (h * inverse_rms(h)).astype(bf)


def in_parts(row):
    hi = row.astype(bf).astype(f32)
    mid = (row - hi).astype(bf).astype(f32)
    return [hi, mid, row - hi - mid]


def retreat_kernel(extra, *refs):
    n = 4 if extra else 1
    parts, (h_ref, grad_ref, *refs) = refs[:n], refs[n:]
    h = h_ref[...]
    r_in = inverse_rms(h)
    d_norm = parts_sum(parts)
    inner = jnp.mean(h * d_norm, axis=1, keepdims=True)
    grad = grad_ref[...].astype(f32) + r_in * d_norm - h * (r_in * r_in * r_in * inner)
    if not extra:
        refs[0][...] = grad
        return
    branch_ref, scale_ref, out_ref, sent_ref = refs
    out_ref[...] = grad
    low = grad.astype(bf)
    r_gate = scale_ref[...]
    column = jnp.sum(low.astype(f32) * branch_ref[...], axis=1, keepdims=True)
    row = jnp.broadcast_to(column, (TOK, 128)).T[:8]
    kappa = r_gate * r_gate * row / DI
    rows = in_parts(r_gate) + in_parts(kappa)
    rows = jnp.concatenate(rows + [jnp.zeros((8, D - 6 * TOK), f32)], axis=1)
    sent_ref[:TOK] = low
    sent_ref[TOK:] = jnp.concatenate([rows, jnp.zeros((8, D), f32)], axis=0).astype(bf)


def plain_call(kernel, name, shapes, args):
    return pl.pallas_call(
        kernel,
        out_shape=shapes,
        compiler_params=pltpu.CompilerParams(vmem_limit_bytes=SMALL_VMEM),
        cost_estimate=pl.CostEstimate(
            flops=int(2e8), bytes_accessed=int(1e6), transcendentals=0
        ),
        name=name,
    )(*args)


def to_owners(row):
    return a2a(row.reshape(NG, TOK), LINE)


def to_line(rows):
    m = rows.shape[0]
    return a2a(jnp.broadcast_to(rows[None], (NG,) + rows.shape), LINE).reshape(NG * m, GT)


def rounded(a):
    return lax.reduce_precision(a, exponent_bits=8, mantissa_bits=7)


def group_gather(block):
    return lax.all_gather(block, ZX, axis=0, tiled=True)


def group_gather_now(block):
    r, n = block.shape
    return a2a(jnp.broadcast_to(block[None], (NQ, r, n)), ZX).reshape(NQ * r, n)


def wait_for(value, *others):
    return lax.optimization_barrier((value, others))[0]


def group_reduce(full):
    r = full.shape[0] // NQ
    return jnp.sum(a2a(full.reshape(NQ, r, full.shape[1]), ZX).astype(f32), axis=0)


def heads_out(cols, width):
    r = cols.shape[0]
    return cols.reshape(r, 2, 2, 2, width).transpose(2, 3, 1, 0, 4).reshape(NG, r, width)


def heads_in(blocks):
    _, r, width = blocks.shape
    return blocks.reshape(2, 2, 2, r, width).transpose(3, 2, 0, 1, 4).reshape(r, NG * width)


def line_of(group):
    yl, yh, c = group // 4, (group // 2) % 2, group % 2
    return yh * 4 + c * 2 + yl


TO_HEADS = [(s, (s % NQ) * NG + line_of(s // NQ)) for s in range(NQ * NG)]
TO_OWNER = [(b, a) for a, b in TO_HEADS]


def in_blocks(weight, gain, extra):
    folded = (weight.astype(f32) * gain.astype(f32)[:, None]).astype(bf)
    z = heads_out(folded[:, :DI], W)
    x = heads_out(folded[:, DI : 2 * DI], W)
    bc = jnp.broadcast_to(folded[None, :, 2 * DI : 2 * DI + 2 * N], (NG, 12, 2 * N))
    step = heads_out(folded[:, 2 * DI + 2 * N :], HL)
    extra = jnp.broadcast_to(extra[None], (NG,) + extra.shape)
    step = jnp.concatenate([step, extra], axis=2)
    step = jnp.pad(step, ((0, 0), (0, 0), (0, 128 - step.shape[2])))
    return jnp.concatenate([x, bc, step, z], axis=2)


STATE_ROWS = W + 16


def line_scan_kernel(reverse, at_ref, own_ref, r1, r2, r3, sent_ref, before_ref, decay_ref):
    rank = 3 - at_ref[0] if reverse else at_ref[0]
    blocks = [read_states(ref) for ref in ((r3, r2, r1) if reverse else (r1, r2, r3))]
    own, own_decay = read_states(own_ref)
    state, decay = fold_before(rank, blocks)
    before_ref[...] = state
    decay_ref[...] = jnp.broadcast_to(decay, (8, 128))
    total = by_rows(own_decay, state) + own
    decay = decay * own_decay
    for i in (1, 2, 3):
        next_state, next_decay = blocks[3 - i]
        there = rank + i <= 3
        total = jnp.where(there, by_rows(next_decay, total) + next_state, total)
        decay = jnp.where(there, decay * next_decay, decay)
    write_states(sent_ref, total, decay)


def fold_before(rank, blocks):
    state = jnp.zeros((W, N), f32)
    decay = jnp.ones((1, 128), f32)
    for i in (3, 2, 1):
        block, block_decay = blocks[i - 1]
        there = rank >= i
        state = jnp.where(there, by_rows(block_decay, state) + block, state)
        decay = jnp.where(there, decay * block_decay, decay)
    return state, decay


def final_states(reverse, at_ref, r1, r2, r3, before_ref, decay_ref):
    rank = 3 - at_ref[0] if reverse else at_ref[0]
    blocks = [read_states(ref) for ref in ((r3, r2, r1) if reverse else (r1, r2, r3))]
    entering = fold_before(rank, blocks)[0]
    return by_rows(decay_ref[0:1], entering) + before_ref[...]


def exclusive_scan(sent, reverse, first, second):
    def around(a, axis):
        return [lax.ppermute(a, axis, [(i, (i + d) % 4) for i in range(4)]) for d in (1, 2, 3)]

    def index(axis):
        return lax.axis_index(axis).reshape(1).astype(jnp.int32)

    got = around(sent, "x")
    if first is not None:
        got[0] = wait_for(got[0], first)
    line, before, decay = pl.pallas_call(
        functools.partial(line_scan_kernel, reverse),
        out_shape=[SENT, struct((W, N)), struct((8, 128))],
        in_specs=[SMEM] + [pl.BlockSpec(memory_space=pltpu.VMEM)] * 4,
        out_specs=[pl.BlockSpec(memory_space=pltpu.VMEM)] * 3,
        name="line_scan",
    )(index("x"), sent, *got)
    got = around(line, "z")
    extra = second(line)
    got[0] = wait_for(got[0], extra)
    return (index("z"), *got, before, decay), extra


PAIRS = HL // 2
LAST = NS - 1


def dot(a, b, ca, cb, precision=None):
    return lax.dot_general(
        a, b, (((ca,), (cb,)), ((), ())), preferred_element_type=f32, precision=precision
    )


def by_lanes(cols):
    lane = lax.broadcasted_iota(jnp.int32, (cols.shape[0], 128), 1)
    return jnp.concatenate(
        [
            jnp.where(lane < HP, cols[:, 2 * p : 2 * p + 1], cols[:, 2 * p + 1 : 2 * p + 2])
            for p in range(PAIRS)
        ],
        axis=1,
    )


def by_rows(row, states):
    return jnp.concatenate(
        [row[:, h : h + 1] * states[h * HP : (h + 1) * HP] for h in range(HL)], axis=0
    )


def two_parts(a):
    hi = a.astype(bf)
    return hi, (a - hi.astype(f32)).astype(bf)


def head_sums(wide):
    column = lax.broadcasted_iota(jnp.int32, (W, 128), 0)
    lane = lax.broadcasted_iota(jnp.int32, (W, 128), 1)
    chosen = ((column >= lane * HP) & (column < lane * HP + HP)).astype(f32).astype(bf)
    hi, low = two_parts(wide)
    return dot(hi, chosen, 1, 0) + dot(low, chosen, 1, 0)


def token_sums(wide):
    ones = jnp.ones((8, wide.shape[1]), bf)
    hi, low = two_parts(wide)
    return dot(ones, hi, 1, 1) + dot(ones, low, 1, 1)


def running_sums(chosen, a):
    hi = a.astype(bf).astype(f32)
    mid = (a - hi).astype(bf).astype(f32)
    packed = hi + pltpu.roll(mid, 8, 1) + pltpu.roll(a - hi - mid, 16, 1)
    out = dot(chosen.astype(f32).astype(bf), packed.astype(bf), 1, 0)
    total = out + pltpu.roll(out, 128 - 8, 1) + pltpu.roll(out, 128 - 16, 1)
    lane = lax.broadcasted_iota(jnp.int32, (SPAN, 128), 1)
    return jnp.where(lane < HL, total, 0.0)


def write_states(sent_ref, states, decay):
    lane = lax.broadcasted_iota(jnp.int32, (8, 128), 1)
    decay = jnp.where(lane < HL, jnp.broadcast_to(decay, (8, 128)), 0.0)
    hi = decay.astype(bf).astype(f32)
    mid = (decay - hi).astype(bf).astype(f32)
    low = decay - hi - mid
    tail = hi + pltpu.roll(mid, HL, 1) + pltpu.roll(low, 2 * HL, 1)
    sent_ref[...] = jnp.concatenate([states, tail, tail], axis=0).astype(bf)


def read_states(ref):
    block = ref[...].astype(f32)
    tail = block[W : W + 8]
    decay = tail + pltpu.roll(tail, 128 - HL, 1) + pltpu.roll(tail, 128 - 2 * HL, 1)
    return block[:W], decay[:1]


def span_masks(segc_ref, segr_ref):
    row = lax.broadcasted_iota(jnp.int32, (SPAN, SPAN), 0)
    col = lax.broadcasted_iota(jnp.int32, (SPAN, SPAN), 1)
    return (col <= row) & (segc_ref[...] == segr_ref[0])


def head_decay(mask, run, run_t, h):
    return jnp.exp(jnp.where(mask, run[:, h : h + 1] - run_t[h : h + 1], -1e30))


def end_weights(run, segc_ref, seg_end):
    return jnp.exp(run[SPAN - 1 :] - run) * (segc_ref[...] == seg_end).astype(f32)


def inflow_of(run, segc_ref, seg_before):
    return jnp.exp(run) * (segc_ref[...] == seg_before).astype(f32)


def past_rows(k, u_ref, past_ref, edge_ref, rows_ref):
    rows_ref[:16] = jnp.where(k == 0, edge_ref[...].astype(f32), past_ref[...].astype(f32))
    rows_ref[16:] = u_ref[...].astype(f32)


def back_by(rows_ref, distance):
    return rows_ref[16 - distance : 16 - distance + SPAN]


def mix_kernel(
    seg_ref, u_ref, past_ref, edge_ref, same_ref, conv_ref, raw_ref, bias_ref, rate_ref, segc_ref,
    segr_ref, v_ref, pre_ref, within_ref, local_ref, step_ref, run_ref, before_ref, decay_ref, sent_ref, acc_ref, dec_ref, rows,
):
    k = pl.program_id(0)

    @pl.when(k == 0)
    def _():
        acc_ref[...] = jnp.zeros_like(acc_ref)
        dec_ref[...] = jnp.ones_like(dec_ref)

    past_rows(k, u_ref, past_ref, edge_ref, rows)
    pre = jnp.broadcast_to(conv_ref[CONV : CONV + 1], (SPAN, CC))
    for i in range(CONV):
        pre = pre + conv_ref[i : i + 1] * back_by(rows, i) * same_ref[:, i : i + 1]
    pre_ref[...] = pre.astype(bf)
    v_low = silu_both(pre)[0].astype(bf)
    v_ref[...] = v_low
    lane = lax.broadcasted_iota(jnp.int32, (SPAN, 128), 1)
    raw = raw_ref[...].astype(f32) + bias_ref[...]
    step = jnp.where(lane < HL, jax.nn.softplus(raw), 0.0)
    row = lax.broadcasted_iota(jnp.int32, (SPAN, SPAN), 0)
    col = lax.broadcasted_iota(jnp.int32, (SPAN, SPAN), 1)
    run = running_sums(col <= row, rate_ref[...] * step)
    step_ref[...] = step
    run_ref[...] = run
    run_t = run.T
    mask = span_masks(segc_ref, segr_ref)
    xc = v_low[:, :W].astype(f32)
    b_low = v_low[:, W : W + N]
    c_low = v_low[:, W + N :]
    gram = dot(c_low, b_low, 1, 1)
    xs = (by_lanes(step) * xc).astype(bf)
    half = lane < HP
    for p in range(PAIRS):
        cols = slice(p * 128, (p + 1) * 128)
        out = [
            dot((gram * head_decay(mask, run, run_t, h)).astype(bf), xs[:, cols], 1, 0)
            for h in (2 * p, 2 * p + 1)
        ]
        within_ref[:, cols] = jnp.where(half, out[0], out[1])
    w_end = end_weights(run, segc_ref, seg_ref[1, k])
    weighted = (by_lanes(w_end * step) * xc).astype(bf)
    own = dot(weighted, b_low, 0, 0)
    local_ref[0] = acc_ref[...]
    before_ref[0] = dec_ref[...]
    inside = (seg_ref[1, k] == seg_ref[0, k]).astype(f32)
    decay = jnp.exp(run[SPAN - 1 :]) * inside
    decay_ref[0] = decay
    acc = by_rows(decay, acc_ref[...]) + own
    acc_ref[...] = acc
    dec = dec_ref[...] * decay
    dec_ref[...] = dec

    @pl.when(k == LAST)
    def _():
        write_states(sent_ref, acc, dec)


def silu_both(v):
    s = 1.0 / (1.0 + jnp.exp(-v))
    return v * s, s * (1.0 + v * (1.0 - s))


def gate_kernel(
    last, order_ref, seg_ref, at_ref, r1, r2, r3, line_ref, line_decay_ref, local_ref, before_ref, run_ref, v_ref, within_ref, z_ref, segc_ref,
    skip_ref, wo_ref, *rest,
):
    if last:
        dq_ref, y0_ref, part_ref, sums_ref, carry_ref = rest
    else:
        y0_ref, other_ref, mine_ref, sums_ref, carry_ref = rest
    i = pl.program_id(0)
    k = order_ref[i]

    @pl.when(i == 0)
    def _():
        carry_ref[...] = final_states(False, at_ref, r1, r2, r3, line_ref, line_decay_ref)

    carried = (by_rows(before_ref[0], carry_ref[...]) + local_ref[0]).astype(bf)
    xc = v_ref[:, :W].astype(f32)
    c_low = v_ref[:, W + N :]
    reading = dot(c_low, carried, 1, 1)
    y0 = within_ref[...] + by_lanes(inflow_of(run_ref[...], segc_ref, seg_ref[0, k])) * reading
    y0_ref[...] = y0
    mixed = (y0 + skip_ref[...] * xc).astype(bf).astype(f32)
    gated = mixed * silu_both(z_ref[...].astype(f32))[0]
    part = dot(gated.astype(bf), wo_ref[...], 1, 0).astype(bf)
    if last:
        part_ref[...] = part
    else:
        write_half(other_ref, mine_ref, part)
    sums = token_sums(gated * gated)
    if last:
        row = lax.broadcasted_iota(jnp.int32, (8, SPAN), 0)
        sums = jnp.where(row < 1, sums, token_sums(gated * dq_ref[...]))
    sums_ref[...] = sums


def gate_back_kernel(
    last, seg_ref, grad_ref, wo_ref, scale_ref, v_ref, y0_ref, z_ref, run_ref, segc_ref, skip_ref,
    decay_ref, dy_ref, dz_ref, gr_ref, local_ref, after_ref, sent_ref, acc_ref, dec_ref,
):
    i = pl.program_id(0)
    k = LAST - i

    @pl.when(i == 0)
    def _():
        acc_ref[...] = jnp.zeros_like(acc_ref)
        dec_ref[...] = jnp.ones_like(dec_ref)

    if last:
        sums = scale_ref[...]
        odd = lax.broadcasted_iota(jnp.int32, (2 * NG, SPAN), 0) % 2 == 1
        square = jnp.sum(jnp.where(odd, 0.0, sums), axis=0, keepdims=True)
        inner = jnp.sum(jnp.where(odd, sums, 0.0), axis=0, keepdims=True)
        r_row = lax.rsqrt(square / DI + EPS)
        k_row = r_row * r_row * r_row * inner / DI
    else:
        rows = scale_ref[...].astype(f32)
        pieces = [rows[:, i * TOK : (i + 1) * TOK] for i in range(6)]
        r_two = pieces[0] + pieces[1] + pieces[2]
        k_two = pieces[3] + pieces[4] + pieces[5]
        r_row = jnp.concatenate([r_two[0:1], r_two[16:17]], axis=1)
        k_row = jnp.concatenate([k_two[0:1], k_two[16:17]], axis=1)
    r = jnp.broadcast_to(r_row, (8, SPAN)).T[:, 0:1]
    kappa = jnp.broadcast_to(k_row, (8, SPAN)).T[:, 0:1]
    d_q = grad_ref[...] if last else dot(grad_ref[...], wo_ref[...], 1, 1)
    mixed = (y0_ref[...] + skip_ref[...] * v_ref[:, :W].astype(f32)).astype(bf).astype(f32)
    silu, d_silu = silu_both(z_ref[...].astype(f32))
    gated = mixed * silu
    gr_ref[...] = (r * gated).astype(bf)
    d_gated = r * d_q - kappa * gated
    dy = (d_gated * silu).astype(bf)
    dy_ref[...] = dy
    dz_ref[...] = (d_gated * mixed * d_silu).astype(bf)
    inflow = by_lanes(inflow_of(run_ref[...], segc_ref, seg_ref[0, k]))
    scaled = (inflow * dy.astype(f32)).astype(bf)
    d_carried = dot(scaled, v_ref[:, W + N :], 0, 0)
    local_ref[0] = acc_ref[...]
    after_ref[0] = dec_ref[...]
    decay = decay_ref[0]
    acc = by_rows(decay, acc_ref[...]) + d_carried
    acc_ref[...] = acc
    dec = dec_ref[...] * decay
    dec_ref[...] = dec

    @pl.when(i == LAST)
    def _():
        write_states(sent_ref, acc, dec)


def mix_back_kernel(v_ref, step_ref, run_ref, segc_ref, segr_ref, dy_ref, dxs_ref, dbc_ref):
    lane = lax.broadcasted_iota(jnp.int32, (SPAN, 128), 1)
    half = lane < HP
    run = run_ref[...]
    run_t = run.T
    mask = span_masks(segc_ref, segr_ref)
    xs = (by_lanes(step_ref[...]) * v_ref[:, :W].astype(f32)).astype(bf)
    b_low = v_ref[:, W : W + N]
    c_low = v_ref[:, W + N :]
    gram = dot(c_low, b_low, 1, 1)
    d_gram = jnp.zeros((SPAN, SPAN), f32)
    zero = jnp.zeros((SPAN, 128), bf)
    for p in range(PAIRS):
        cols = slice(p * 128, (p + 1) * 128)
        dy = dy_ref[:, cols]
        out = []
        for i, h in enumerate((2 * p, 2 * p + 1)):
            decay = head_decay(mask, run, run_t, h)
            mixing = (gram * decay).astype(bf)
            dy_one = jnp.where(half, dy, zero) if i == 0 else jnp.where(half, zero, dy)
            d_gram = d_gram + dot(dy_one, xs[:, cols], 1, 1) * decay
            out.append(dot(mixing, dy, 0, 0))
        dxs_ref[:, cols] = jnp.where(half, out[0], out[1])
    d_gram = d_gram.astype(bf)
    dbc_ref[:, :N] = dot(d_gram, c_low, 0, 0).astype(bf)
    dbc_ref[:, N:] = dot(d_gram, b_low, 1, 0).astype(bf)


def end_kernel(
    seg_ref, at_ref, r1, r2, r3, line_ref, line_decay_ref, carry_ref, local_ref, before_ref, dlocal_ref, after_ref, decay_ref, v_ref,
    pre_ref, raw_ref, bias_ref, rate_ref, step_ref, run_ref, segc_ref, skip_ref, dy_ref, dxs_ref,
    dbc_ref, y0_ref, dpre_ref, draw_ref, sums_ref, later_s,
):
    k = pl.program_id(0)

    @pl.when(k == 0)
    def _():
        later_s[...] = final_states(True, at_ref, r1, r2, r3, line_ref, line_decay_ref)
        sums_ref[...] = jnp.zeros_like(sums_ref)

    d_end = by_rows(after_ref[0], later_s[...]) + dlocal_ref[0]
    carried = by_rows(before_ref[0], carry_ref[...]) + local_ref[0]
    d_end_low = d_end.astype(bf)
    run, step, rate = run_ref[...], step_ref[...], rate_ref[...]
    xc = v_ref[:, :W].astype(f32)
    b_low = v_ref[:, W : W + N]
    dy = dy_ref[...].astype(f32)
    dxs = dxs_ref[...]
    step_x = by_lanes(step)
    xs = (step_x * xc).astype(bf).astype(f32)
    w_end = end_weights(run, segc_ref, seg_ref[1, k])
    weights_x = by_lanes(w_end * step)
    weighted = (weights_x * xc).astype(bf)
    scaled = (by_lanes(inflow_of(run, segc_ref, seg_ref[0, k])) * dy).astype(bf)
    d_weighted = dot(b_low, d_end_low, 1, 1)
    d_b = dbc_ref[:, :N].astype(f32) + dot(weighted, d_end_low, 1, 0)
    d_c = dbc_ref[:, N:].astype(f32) + dot(scaled, carried.astype(bf), 1, 0)
    d_xc = skip_ref[...] * dy + step_x * dxs + weights_x * d_weighted
    dv = jnp.concatenate([d_xc, d_b, d_c], axis=1)
    dpre_ref[...] = (dv * silu_both(pre_ref[...].astype(f32))[1]).astype(bf)
    skip_sum = head_sums(dy * xc)
    d_run = head_sums(dy * y0_ref[...] - xs * dxs)
    d_step = head_sums(xc * dxs)
    d_w = head_sums(d_weighted * xc)
    product = d_end * carried
    lane1 = lax.broadcasted_iota(jnp.int32, (1, 128), 1)
    d_span = jnp.zeros((1, 128), f32)
    for h in range(HL):
        rows = jnp.sum(product[h * HP : (h + 1) * HP], axis=0, keepdims=True)
        d_span = d_span + jnp.where(lane1 == h, jnp.sum(rows, axis=1, keepdims=True), 0.0)
    d_step = d_step + d_w * w_end
    d_ww = d_w * w_end * step
    d_run = d_run - d_ww
    d_last = jnp.sum(d_ww, axis=0, keepdims=True) + d_span * decay_ref[0]
    row = lax.broadcasted_iota(jnp.int32, (SPAN, SPAN), 0)
    col = lax.broadcasted_iota(jnp.int32, (SPAN, SPAN), 1)
    d_a = running_sums(col >= row, d_run) + d_last
    d_step = d_step + rate * d_a
    raw = raw_ref[...].astype(f32) + bias_ref[...]
    lane = lax.broadcasted_iota(jnp.int32, (SPAN, 128), 1)
    d_raw = jnp.where(lane < HL, d_step / (1.0 + jnp.exp(-raw)), 0.0)
    draw_ref[...] = d_raw.astype(bf)
    sums = jnp.concatenate(
        [
            jnp.sum(d_raw, axis=0, keepdims=True),
            rate * jnp.sum(step * d_a, axis=0, keepdims=True),
            jnp.sum(skip_sum, axis=0, keepdims=True),
            jnp.zeros((5, 128), f32),
        ],
        axis=0,
    )
    sums_ref[...] = sums_ref[...] + sums


def conv_back_kernel(
    first, order_ref, dpre_ref, next_ref, after_ref, u_ref, past_ref, edge_ref, same_ref, conv_ref, draw_ref, dz_ref,
    wa_ref, wz_ref, da_ref, *outs,
):
    *outs, taps_ref, rows, d_rows = outs
    i = pl.program_id(0)
    k = order_ref[i]

    @pl.when(i == 0)
    def _():
        taps_ref[...] = jnp.zeros_like(taps_ref)

    d_pre = dpre_ref[...].astype(f32)
    d_rows[:SPAN] = d_pre
    d_rows[SPAN:] = jnp.where(
        k == LAST, after_ref[...].astype(f32), next_ref[...].astype(f32)
    )
    past_rows(k, u_ref, past_ref, edge_ref, rows)
    du = jnp.zeros((SPAN, CC), f32)
    taps = []
    for tap in range(CONV):
        ahead = d_rows[tap : tap + SPAN]
        same = same_ref[:, CONV + tap : CONV + tap + 1]
        du = du + conv_ref[tap : tap + 1] * ahead * same
        product = d_pre * back_by(rows, tap) * same_ref[:, tap : tap + 1]
        taps.append(jnp.sum(product, axis=0, keepdims=True))
    taps.append(jnp.sum(d_pre, axis=0, keepdims=True))
    taps.append(jnp.zeros((3, CC), f32))
    taps_ref[...] = taps_ref[...] + jnp.concatenate(taps, axis=0)
    da = jnp.concatenate([du.astype(bf), draw_ref[...]], axis=1)
    da_ref[...] = da
    part = dot(da, wa_ref[...], 1, 1) + dot(dz_ref[...], wz_ref[...], 1, 1)
    if first:
        outs[0][...] = part.astype(bf)
    else:
        write_half(*outs[:2], part.astype(bf))


def tok_block(n, reverse=False):
    return pl.BlockSpec((SPAN, n), lambda k: (LAST - k if reverse else k, 0))


def span_block(rows, n, reverse=False):
    return pl.BlockSpec((1, rows, n), lambda k: (LAST - k if reverse else k, 0, 0))


def whole(*shape):
    return pl.BlockSpec(shape, lambda k: (0,) * len(shape))


STATE = struct((NS, W, N))
ROW = struct((NS, 1, 128))
SENT = struct((STATE_ROWS, N), bf)
STATE_SCRATCH = pltpu.VMEM((W, N), f32)


def call(kernel, name, ins, outs, shapes, scratch, args, us, vmem=VMEM_BYTES):
    return pl.pallas_call(
        kernel,
        grid=(NS,),
        in_specs=ins,
        out_specs=outs,
        out_shape=shapes,
        scratch_shapes=scratch,
        compiler_params=pltpu.CompilerParams(
            dimension_semantics=("arbitrary",), vmem_limit_bytes=vmem
        ),
        cost_estimate=pl.CostEstimate(
            flops=int(us * 4e7), bytes_accessed=int(us * 2e5), transcendentals=0
        ),
        name=name,
    )(*args)


def ordered_call(kernel, name, ins, outs, shapes, scratch, args, us):
    return pl.pallas_call(
        kernel,
        grid_spec=pltpu.PrefetchScalarGridSpec(
            num_scalar_prefetch=1, grid=(NS,), in_specs=ins, out_specs=outs, scratch_shapes=scratch
        ),
        out_shape=shapes,
        compiler_params=pltpu.CompilerParams(
            dimension_semantics=("arbitrary",), vmem_limit_bytes=VMEM_BYTES
        ),
        cost_estimate=pl.CostEstimate(
            flops=int(us * 4e7), bytes_accessed=int(us * 2e5), transcendentals=0
        ),
        name=name,
    )(span_order(), *args)


def tok_at(n):
    return pl.BlockSpec((SPAN, n), lambda i, order: (order[i], 0))


def span_at(rows, n):
    return pl.BlockSpec((1, rows, n), lambda i, order: (order[i], 0, 0))


def whole_at(*shape):
    return pl.BlockSpec(shape, lambda i, order: (0,) * len(shape))


HALVES = [
    pl.BlockSpec((SPAN, D), lambda i, order: (jnp.minimum(i, 1), 0)),
    pl.BlockSpec((SPAN, D), lambda i, order: (jnp.maximum(i - 2, 0), 0)),
]
HALF_SHAPES = [struct((GT // 2, D), bf)] * 2


def past_block(n):
    return pl.BlockSpec((16, n), lambda k: (jnp.maximum(k * (SPAN // 16) - 1, 0), 0))


def span_mix(seg, u, edge, same, conv, raw, bias, rate, segc, segr):
    return call(
        mix_kernel,
        "span_mix",
        [SMEM, tok_block(CC), past_block(CC), whole(16, CC), tok_block(8), whole(8, CC),
         tok_block(128), whole(1, 128), whole(1, 128), tok_block(1), span_block(1, SPAN)],
        [tok_block(CC), tok_block(CC), tok_block(W), span_block(W, N), tok_block(128),
         tok_block(128), span_block(1, 128), span_block(1, 128), whole(STATE_ROWS, N)],
        [struct((GT, CC), bf), struct((GT, CC), bf), struct((GT, W)), STATE, struct((GT, 128)),
         struct((GT, 128)), ROW, ROW, SENT],
        [STATE_SCRATCH, pltpu.VMEM((1, 128), f32), pltpu.VMEM((SPAN + 16, CC), f32)],
        (seg, u, u, edge, same, conv, raw, bias, rate, segc, segr),
        10,
    )


def conv_back(first, d_pre, after, u, edge, same, conv, d_raw, dz, wa, wz, at):
    following = pl.BlockSpec(
        (16, CC), lambda i, order: (jnp.minimum((order[i] + 1) * (SPAN // 16), GT // 16 - 1), 0)
    )
    past = pl.BlockSpec(
        (16, CC), lambda i, order: (jnp.maximum(order[i] * (SPAN // 16) - 1, 0), 0)
    )
    return ordered_call(
        functools.partial(conv_back_kernel, first),
        "conv_back",
        [tok_at(CC), following, whole_at(16, CC), tok_at(CC), past, whole_at(16, CC), tok_at(8),
         whole_at(8, CC), tok_at(128), tok_at(W), whole_at(D, CA),
         pl.BlockSpec((D, W), lambda i, order: (0, at))],
        [tok_at(CA)] + ([tok_at(D)] if first else HALVES) + [whole_at(8, CC)],
        [struct((GT, CA), bf)] + ([struct((GT, D), bf)] if first else HALF_SHAPES)
        + [struct((8, CC))],
        [pltpu.VMEM((SPAN + 16, CC), f32)] * 2,
        (d_pre, d_pre, after, u, u, edge, same, conv, d_raw, dz, wa, wz),
        10,
    )


def span_gate(seg, back, local, before, run, v, within, z, segc, skip, wo, d_q):
    last = d_q is not None
    ins = [SMEM, SMEM] + [whole_at(STATE_ROWS, N)] * 3 + [
           whole_at(W, N), whole_at(8, 128), span_at(W, N), span_at(1, 128), tok_at(128), tok_at(CC),
           tok_at(W), tok_at(W), tok_at(1), whole_at(1, W), whole_at(W, D)]
    args = (seg, *back, local, before, run, v, within, z, segc, skip, wo)
    return ordered_call(
        functools.partial(gate_kernel, last),
        "span_gate",
        ins + [tok_at(W)] if last else ins,
        [tok_at(W)] + ([tok_at(D)] if last else HALVES)
        + [pl.BlockSpec((8, SPAN), lambda i, order: (0, order[i])), whole_at(W, N)],
        [struct((GT, W))] + ([struct((GT, D), bf)] if last else HALF_SHAPES)
        + [struct((8, GT)), struct((W, N))],
        [],
        args + (d_q,) if last else args,
        10,
    )


def span_gate_back(last, seg, grad, wo, scales, v, y0, z, run, segc, skip, decay):
    if last:
        scale_block = pl.BlockSpec((2 * NG, SPAN), lambda k: (0, LAST - k))
    else:
        scale_block = pl.BlockSpec((32, D), lambda k: (LAST - k, 0))
    return call(
        functools.partial(gate_back_kernel, last),
        "span_gate_back",
        [SMEM, tok_block(W if last else D, True), whole(W, D), scale_block,
         tok_block(CC, True), tok_block(W, True), tok_block(W, True), tok_block(128, True),
         tok_block(1, True), whole(1, W), span_block(1, 128, True)],
        [tok_block(W, True), tok_block(W, True), tok_block(W, True), span_block(W, N, True),
         span_block(1, 128, True), whole(STATE_ROWS, N)],
        [struct((GT, W), bf), struct((GT, W), bf), struct((GT, W), bf), STATE, ROW, SENT],
        [STATE_SCRATCH, pltpu.VMEM((1, 128), f32)],
        (seg, grad, wo, scales, v, y0, z, run, segc, skip, decay),
        12,
    )


def span_mix_back(v, step, run, segc, segr, dy):
    return call(
        mix_back_kernel,
        "span_mix_back",
        [tok_block(CC), tok_block(128), tok_block(128), tok_block(1), span_block(1, SPAN),
         tok_block(W)],
        [tok_block(W), tok_block(2 * N)],
        [struct((GT, W)), struct((GT, 2 * N), bf)],
        [],
        (v, step, run, segc, segr, dy),
        14,
    )


def span_end(seg, later, back, local, before, dlocal, after, decay, v, pre, raw, bias, rate, step,
             run, segc, skip, dy, dxs, dbc, y0):
    return call(
        end_kernel,
        "span_end",
        [SMEM, SMEM] + [whole(STATE_ROWS, N)] * 3 + [
         whole(W, N), whole(8, 128), whole(W, N), span_block(W, N), span_block(1, 128),
         span_block(W, N), span_block(1, 128), span_block(1, 128), tok_block(CC), tok_block(CC),
         tok_block(128), whole(1, 128), whole(1, 128), tok_block(128), tok_block(128),
         tok_block(1), whole(1, W), tok_block(W), tok_block(W), tok_block(2 * N), tok_block(W)],
        [tok_block(CC), tok_block(128), whole(8, 128)],
        [struct((GT, CC), bf), struct((GT, 128), bf), struct((8, 128))],
        [STATE_SCRATCH],
        (seg, *later, back, local, before, dlocal, after, decay, v, pre, raw, bias, rate, step, run,
         segc, skip, dy, dxs, dbc, y0),
        16,
    )


def group_reduce_blocks(sent):
    return jnp.sum(a2a(sent, ZX).astype(f32), axis=0)


SMALL = CC + HL


def small_block(conv_grads, head_grads):
    own_ch = CH // (NQ * NG)
    conv = jnp.stack(conv_grads).reshape(LAYERS * (CONV + 1), NQ * NG, own_ch)
    conv = jnp.pad(conv.transpose(1, 0, 2), ((0, 0), (0, 12 - LAYERS * (CONV + 1)), (0, 0)))
    head = jnp.stack(head_grads, axis=1)
    high = rounded(head)
    head = jnp.concatenate([high, head - high], axis=1)
    head = jnp.tile(head, (NQ * NG // 2, 1, 1))
    head = jnp.pad(head, ((0, 0), (0, 12 - 2 * LAYERS), (0, 0)))
    block = jnp.concatenate([conv, head], axis=2).reshape(D, own_ch + 3 * H // 2)
    return jnp.pad(block.astype(bf), ((0, 0), (SMALL, CA - SMALL - block.shape[1])))


def per_device(
    tokens,
    doc_starts,
    norm_gain,
    in_weight,
    conv_weight,
    conv_bias,
    step_bias,
    decay_log,
    skip_gain,
    gate_gain,
    out_weight,
    cotangent,
):
    q = lax.axis_index(ZX)
    yh, core, yl = lax.axis_index("yh"), lax.axis_index("c"), lax.axis_index("yl")
    sub = yh * 2 + core
    group = yl * 4 + sub

    own_ch = CH // (NQ * NG)
    conv_own = jnp.concatenate([conv_weight, conv_bias[:, None]], axis=1).reshape(-1, own_ch)
    conv_own = jnp.pad(conv_own, ((0, 12 - conv_own.shape[0]), (0, 0)))
    sent = [in_blocks(in_weight[l], norm_gain[l], conv_own if l == 0 else conv_own[:, :0]) for l in range(LAYERS)]
    sent = jnp.stack(sent, axis=1)
    got = a2a(sent, LINE)
    in_0 = got[:, 0].reshape(NG * 12, CA + W)
    in_1 = got[:, 1].reshape(NG * 12, CA + W)
    own_0 = jnp.broadcast_to(in_0[None, :, :CA], (NQ, NG * 12, CA))
    w_a0 = a2a(own_0, ZX).reshape(D, CA)
    h = tokens.astype(f32)
    normed = (h * lax.rsqrt(jnp.mean(h * h, axis=-1, keepdims=True) + EPS)).astype(bf)
    pos = q * GT + jnp.arange(-(CONV - 1), GT + CONV - 1, dtype=jnp.int32)
    seg_ext = jnp.sum((doc_starts[None, :] <= pos[:, None]).astype(jnp.int32), axis=1) - 1
    seg = seg_ext[CONV - 1 : CONV - 1 + GT]
    seg_spans = seg.reshape(NS, SPAN)
    seg_before = seg_ext[CONV - 2 : CONV - 2 + GT : SPAN]
    seg_ends = jnp.stack([seg_before, seg_spans[:, -1]])
    seg_col, seg_row = seg[:, None], seg_spans[:, None, :]
    same = jnp.stack(
        [seg_ext[CONV - 1 - k : CONV - 1 - k + GT] == seg for k in range(CONV)]
        + [seg_ext[CONV - 1 + k : CONV - 1 + k + GT] == seg for k in range(CONV)],
        axis=1,
    ).astype(f32)

    def pick_heads(a):
        own = lax.dynamic_slice_in_dim(a, sub * HL, HL, 0)
        return jnp.pad(own, (0, 128 - HL))[None]

    onward = [(i, i + 1) for i in range(NQ - 1)]
    consts = []
    for l in range(LAYERS):
        rate = jnp.where(jnp.arange(128)[None] < HL, -jnp.exp(pick_heads(decay_log[l])), 0.0)
        skip_x = jnp.repeat(lax.dynamic_slice_in_dim(skip_gain[l], sub * HL, HL, 0), HP)[None]
        consts.append((pick_heads(step_bias[l]), rate, skip_x))
    prepared = own_0, consts, same, seg_ends, seg_col, seg_row, span_order()
    places, blocks = line_blocks(wait_for(normed, got), prepared)
    folded_out = (out_weight.astype(f32) * gate_gain.astype(f32)[:, :, None]).astype(bf)
    out_blocks = lax.ppermute(folded_out, AX, TO_HEADS)
    zo = jnp.concatenate([in_0[:, CA:], out_blocks.reshape(192, W)], axis=0)
    grad_full = lax.all_gather(cotangent, LINE, axis=0, tiled=True)
    w_a0 = wait_for(w_a0, zo)
    normed, u, raw = place_project(places, blocks, w_a0)
    tail = u[GT - 16 :]
    conv_all = wait_for(w_a0, tail)[:, SMALL : SMALL + own_ch].reshape(NQ * NG, 12, own_ch)
    conv_all = conv_all[:, : LAYERS * (CONV + 1)].transpose(1, 0, 2)
    conv_all = conv_all.reshape(LAYERS, CONV + 1, CH).astype(f32)
    conv_x = lax.dynamic_slice_in_dim(conv_all, group * W, W, 2)
    conv_here = jnp.concatenate([conv_x, conv_all[:, :, DI:]], axis=2)
    conv_here = jnp.pad(conv_here, ((0, 0), (0, 7 - CONV), (0, 0)))
    zo = group_gather(wait_for(zo, w_a0, blocks)).reshape(NQ, 288, W)
    w_z0 = zo[:, :96].reshape(D, W)
    w_o = [zo[:, 96:192].reshape(W, D), None]
    w_in1 = group_gather(wait_for(in_1, tail))
    saved = []
    for l in range(LAYERS):
        bias_h, rate, skip_x = consts[l]
        if l > 0:
            normed, u, raw = line_project(normed, w_in1)
        edge = lax.ppermute(u[GT - 16 :], ZX, onward)
        v, pre, within, local, step, run, before, decay, sent = span_mix(
            seg_ends, u, edge, same, conv_here[l], raw, bias_h, rate, seg_col, seg_row
        )
        if l == 0:
            w_o[1] = wait_for(zo, v)[:, 192:].reshape(W, D)
            d_q = None
            back, z = exclusive_scan(
                sent, False, None, lambda outs: mm(wait_for(normed, outs), w_z0).astype(bf)
            )
        else:
            z = mm(normed, w_in1[:, CA:]).astype(bf)
            back, d_q = exclusive_scan(
                sent, False, z, lambda outs: mm(wait_for(grad_full, outs), w_o[1], 1, 1)
            )
        y0, *parts, sums, carry = span_gate(
            seg_ends, back, local, before, run, v, within, z, seg_col, skip_x, w_o[l],
            d_q,
        )
        saved.append(
            dict(
                h=h, normed=normed, u=u, edge=edge, pre=pre, v=v, z=z, raw=raw, bias_h=bias_h,
                rate=rate, skip_x=skip_x, step=step, run=run, before=before, decay=decay,
                local=local, carry=carry, y0=y0,
            )
        )
        if l < LAYERS - 1:
            parts = line_parts(*parts)
            square = wait_for(to_owners(sums[0]), *parts[1:])
            h, branch, normed, r_gate = plain_call(
                advance_kernel,
                "advance",
                [struct((TOK, D)), struct((TOK, D)), struct((TOK, D), bf), struct((8, TOK))],
                (*parts, square, h),
            )
        else:
            scales = to_line(sums[:2])
            at = (line_index() // 2 * 4 + core * 2 + yl) * TOK
            square = lax.dynamic_slice_in_dim(scales, at, TOK, 1)
            square = jnp.sum(square.reshape(NG, 2, TOK)[:, 0], axis=0)
            r_last = lax.rsqrt(square / DI + EPS)[:, None]
            total = lax.psum_scatter(parts[0], LINE, scatter_dimension=0, tiled=True)
            output = (h + total.astype(f32) * r_last).astype(bf)

    grad = cotangent
    conv_grads, head_grads = [None] * LAYERS, [None] * LAYERS
    a_sums, z_sums, out_sums = ([None] * LAYERS for _ in range(3))
    for l in reversed(range(LAYERS)):
        s = saved[l]
        dy, dz, gr, dlocal, after, sent = span_gate_back(
            l == LAYERS - 1, seg_ends, d_q if l else grad_full, w_o[l], scales, s["v"], s["y0"], s["z"], s["run"],
            seg_col, s["skip_x"], s["decay"],
        )
        z_part = mm(s["normed"], dz, 0, 0).astype(bf).reshape(NQ, 96, W)

        def out_blocks_of(outs):
            low = wait_for(gr, outs)
            return [
                mm(low, grad_full[:, i * W : (i + 1) * W], 0, 0).astype(bf).reshape(NQ, 24, W)
                for i in range(D // W)
            ]

        later, out_part = exclusive_scan(sent, True, z_part, out_blocks_of)
        sums = jnp.concatenate([z_part, *out_part], axis=1)
        both = group_reduce_blocks(wait_for(sums, later))
        dxs, dbc = span_mix_back(s["v"], s["step"], s["run"], seg_col, seg_row, wait_for(dy, sums))
        d_pre, d_raw, head_sum = span_end(
            seg_ends, later, s["carry"], s["local"], s["before"], dlocal, after, s["decay"], s["v"],
            s["pre"], s["raw"], s["bias_h"], s["rate"], s["step"], s["run"], seg_col, s["skip_x"],
            dy, dxs, dbc, s["y0"],
        )
        following = lax.ppermute(d_pre[:16], ZX, [(b, a) for a, b in onward])
        z_sums[l] = both[:96]
        out_sums[l] = both[96:].reshape(4, 24, W).transpose(1, 0, 2).reshape(24, D)
        if l == LAYERS - 1:
            w_a, w_z, at = w_in1, w_in1, CA // W
        else:
            w_a, w_z, at = w_a0, w_z0, 0
        da, *parts, taps = conv_back(
            l == 0, d_pre, following, s["u"], s["edge"], same, conv_here[l], d_raw, dz, w_a, w_z, at
        )
        conv_full = jnp.zeros((CONV + 1, CH), f32)
        conv_full = lax.dynamic_update_slice_in_dim(
            conv_full, taps[: CONV + 1, :W], group * W, 1
        )
        conv_grads[l] = conv_full.at[:, DI:].set(taps[: CONV + 1, W:])
        head_full = lax.dynamic_update_slice_in_dim(
            jnp.zeros((3, H), f32), head_sum[:3, :HL], group * HL, 1
        )
        head_grads[l] = head_full.reshape(3, 2, H // 2).transpose(1, 0, 2).reshape(2, 3 * H // 2)
        a_part = mm(s["normed"], da, 0, 0)
        if l == 0:
            a_part = a_part + small_block(conv_grads, head_grads).astype(f32)
        a_part = a_part.astype(bf)
        if l == 0:
            parts = [lax.psum_scatter(parts[0], LINE, scatter_dimension=0, tiled=True)]
            a_sums[l] = group_reduce(a_part)
        else:
            parts = line_parts(*parts, output)
            a_sums[l] = group_reduce(wait_for(a_part, parts[0]))
        if l > 0:
            grad, block = plain_call(
                functools.partial(retreat_kernel, True),
                "retreat",
                [struct((TOK, D)), struct((TOK + 16, D), bf)],
                (*parts, s["h"], grad, branch, r_gate),
            )
            early = jnp.concatenate([a_sums[1], z_sums[1]], axis=1).reshape(NG, 12, CA + W)
            grad_full, scales = line_gather_more(block, early)
            early = a2a(early, LINE)
            scales = wait_for(scales, early)
        else:
            grad = plain_call(
                functools.partial(retreat_kernel, False),
                "retreat_last",
                struct((TOK, D)),
                (*parts, s["h"], grad),
            )

    out_sums = [
        lax.ppermute(wait_for(out_sums[l], a_part if l else a_sums[0]), AX, TO_OWNER)
        for l in range(LAYERS)
    ]
    late = jnp.concatenate([a_sums[0], z_sums[0]], axis=1)
    late = a2a(late.reshape(NG, 12, CA + W).astype(bf), LINE).astype(f32)
    small = jnp.sum(late[:, :, SMALL:CA], axis=0)
    in_grads, gain_grads, out_grads, gate_grads = ([None] * LAYERS for _ in range(4))
    for l in range(LAYERS):
        got = (late, early)[l]
        a_piece, z_piece = got[:, :, :CA], got[:, :, CA:]
        g_in = jnp.concatenate(
            [
                heads_in(z_piece),
                heads_in(a_piece[:, :, :W]),
                jnp.sum(a_piece[:, :, W:CC], axis=0),
                heads_in(a_piece[:, :, CC : CC + HL]),
            ],
            axis=1,
        )
        in_grads[l] = g_in * norm_gain[l].astype(f32)[:, None]
        gain_grads[l] = jnp.sum(g_in * in_weight[l].astype(f32), axis=1)
        g_out = out_sums[l]
        out_grads[l] = g_out * gate_gain[l].astype(f32)[:, None]
        gate_grads[l] = jnp.sum(g_out * out_weight[l].astype(f32), axis=1)

    conv_grad = small[: LAYERS * (CONV + 1), :own_ch].reshape(LAYERS, CONV + 1, own_ch)
    head_grad = small[:LAYERS] + small[LAYERS : 2 * LAYERS]
    head_grad = head_grad[:, own_ch : own_ch + 3 * H // 2].reshape(LAYERS, 3, H // 2)
    return (
        output,
        grad,
        jnp.stack(gain_grads),
        jnp.stack(in_grads),
        conv_grad[:, :CONV],
        conv_grad[:, CONV],
        head_grad[:, 0],
        head_grad[:, 1],
        head_grad[:, 2],
        jnp.stack(gate_grads),
        jnp.stack(out_grads),
    )


def solution(mesh):
    fine = Mesh(mesh.devices.reshape(4, 4, 2, 2, 2), AX)
    tok, last, mid, heads = P(AX, None), P(None, AX), P(None, AX, None), P(None, "yl")
    conv = P(None, None, AX)
    return jax.shard_map(
        per_device,
        mesh=fine,
        in_specs=(tok, P(), last, mid, conv, last, heads, heads, heads, last, mid, tok),
        out_specs=(tok, tok, last, mid, conv, last, heads, heads, heads, last, mid),
        check_vma=False,
    )
```

```python
import functools

import jax
import jax.numpy as jnp
from jax import lax
from jax.experimental import pallas as pl
from jax.experimental.pallas import tpu as pltpu
from jax.sharding import Mesh, PartitionSpec as P

D = 1536
DI = 3072
H = 48
HP = 64
N = 128
CONV = 4
LAYERS = 2
CH = DI + 2 * N
EPS = 1e-05

AX = ("z", "x", "yh", "c", "yl")
ZX = ("z", "x")
LINE = ("yh", "c", "yl")
Y = ("yh", "yl")
NQ = 16
NG = 8
TOK = 128
GT = TOK * NG
SPAN = 256
NS = GT // SPAN
HL = H // NG
W = HL * HP
CC = W + 2 * N
CA = CC + 128

bf = jnp.bfloat16
f32 = jnp.float32
HI = lax.Precision.HIGHEST


SMEM = pl.BlockSpec(memory_space=pltpu.SMEM)
VMEM_BYTES = 60 * 1024 * 1024
SMALL_VMEM = 16 * 1024 * 1024


def struct(shape, dtype=f32):
    return jax.ShapeDtypeStruct(shape, dtype)


def mm(a, b, ca=1, cb=0):
    return lax.dot_general(a, b, (((ca,), (cb,)), ((), ())), preferred_element_type=f32)


def a2a(a, axes):
    return lax.all_to_all(a, axes, 0, 0, tiled=True)


def core_swap(a):
    return lax.ppermute(a, "c", [(0, 1), (1, 0)])


def line_index():
    return lax.axis_index("yh") * 2 + lax.axis_index("yl")


def along_line(a, distance):
    return lax.ppermute(a, Y, [(i, (i + distance) % 4) for i in range(4)])


def fill_places(pos_ref, blocks, x_ref):
    for i, block in enumerate(blocks):
        at = pl.multiple_of(pos_ref[i] * TOK, TOK)
        x_ref[pl.ds(at, TOK)] = block[:TOK]


def place_kernel(pos_ref, *refs):
    blocks, (out_ref, extra_ref, x_ref) = refs[:NG], refs[NG:]
    k = pl.program_id(0)

    @pl.when(k == 0)
    def _():
        fill_places(pos_ref, blocks, x_ref)
        for i, block in enumerate(blocks):
            extra_ref[pl.ds(pl.multiple_of(pos_ref[i] * 16, 16), 16)] = block[TOK:]

    out_ref[...] = x_ref[pl.ds(pl.multiple_of(k * SPAN, SPAN), SPAN)]


def place_project_kernel(pos_ref, *refs):
    blocks, (w_ref, out_ref, u_ref, raw_ref, x_ref) = refs[:NG], refs[NG:]
    k = pl.program_id(0)

    @pl.when(k == 0)
    def _():
        fill_places(pos_ref, blocks, x_ref)

    x = x_ref[pl.ds(pl.multiple_of(k * SPAN, SPAN), SPAN)]
    out_ref[...] = x
    project = jnp.dot(x, w_ref[...], preferred_element_type=f32).astype(bf)
    u_ref[...] = project[:, :CC]
    raw_ref[...] = project[:, CC:]


def line_blocks(own, first=None):
    y, core = line_index(), lax.axis_index("c")
    blocks, places = [], []

    def place(distance, c):
        at = (y - distance) % 4
        return (at // 2) * 4 + c * 2 + at % 2

    for d in (0, 1, 3, 2):
        got = along_line(own, d) if d else own
        if d and first is not None:
            got = wait_for(got, first)
        blocks += [got, core_swap(got)]
        places += [place(d, core), place(d, 1 - core)]
    return jnp.stack(places).astype(jnp.int32), blocks


X_SCRATCH = pltpu.VMEM((GT, D), bf)


def line_gather_more(own, first):
    places, blocks = line_blocks(own, first)
    return call(
        place_kernel,
        "place_gradient",
        [SMEM] + [whole(TOK + 16, D)] * NG,
        [tok_block(D), whole(NG * 16, D)],
        [struct((GT, D), bf), struct((NG * 16, D), bf)],
        [X_SCRATCH],
        (places, *blocks),
        4,
    )


def line_project(own, weight):
    return place_project(*line_blocks(own), weight)


def place_project(places, blocks, weight):
    return call(
        place_project_kernel,
        "place_project",
        [SMEM] + [whole(TOK, D)] * NG + [whole(D, CA)],
        [tok_block(D), tok_block(CC), tok_block(128)],
        [struct((GT, D), bf), struct((GT, CC), bf), struct((GT, 128), bf)],
        [X_SCRATCH],
        (places, *blocks, weight),
        9,
    )


def chip_kernel(y_ref, mine_ref, got_ref, own_ref, *sent_refs):
    def rows(distance):
        at = pl.multiple_of((y_ref[0] + distance) % 4 * TOK, TOK)
        return mine_ref[pl.ds(at, TOK)].astype(f32) + got_ref[pl.ds(at, TOK)].astype(f32)

    own_ref[...] = rows(0)
    for distance, ref in zip((1, 3, 2), sent_refs):
        ref[...] = rows(distance).astype(bf)


def line_parts(other, mine, first=None):
    got = core_swap(other)
    if first is not None:
        got = wait_for(got, first)
    own, *sent = pl.pallas_call(
        chip_kernel,
        out_shape=[struct((TOK, D))] + [struct((TOK, D), bf)] * 3,
        in_specs=[SMEM] + [pl.BlockSpec(memory_space=pltpu.VMEM)] * 2,
        out_specs=[pl.BlockSpec(memory_space=pltpu.VMEM)] * 4,
        compiler_params=pltpu.CompilerParams(vmem_limit_bytes=SMALL_VMEM),
        name="chip_sum",
    )(line_index().reshape(1).astype(jnp.int32), mine, got)
    return [own] + [along_line(block, d) for block, d in zip(sent, (1, 3, 2))]


def span_order():
    core = lax.axis_index("c")
    return jnp.stack([1 - core, 3 - core, core, 2 + core]).astype(jnp.int32)


def write_half(other_ref, mine_ref, value):
    i = pl.program_id(0)

    @pl.when(i < 2)
    def _():
        other_ref[...] = value

    @pl.when(i >= 2)
    def _():
        mine_ref[...] = value


def parts_sum(refs):
    total = refs[0][...].astype(f32)
    for ref in refs[1:]:
        total = total + ref[...].astype(f32)
    return total


def inverse_rms(a):
    return lax.rsqrt(jnp.mean(a * a, axis=1, keepdims=True) + EPS)


def advance_kernel(p0, p1, p2, p3, square_ref, h_ref, out_ref, branch_ref, normed_ref, scale_ref):
    square = jnp.sum(square_ref[...], axis=0, keepdims=True)
    r_gate = jnp.broadcast_to(lax.rsqrt(square / DI + EPS), (8, TOK))
    scale_ref[...] = r_gate
    branch = parts_sum((p0, p1, p2, p3)) * r_gate.T[:, 0:1]
    h = h_ref[...] + branch
    out_ref[...] = h
    branch_ref[...] = branch
    normed_ref[...] = (h * inverse_rms(h)).astype(bf)


def in_parts(row):
    hi = row.astype(bf).astype(f32)
    mid = (row - hi).astype(bf).astype(f32)
    return [hi, mid, row - hi - mid]


def retreat_kernel(extra, *refs):
    parts, (h_ref, grad_ref, *refs) = refs[:4], refs[4:]
    h = h_ref[...]
    r_in = inverse_rms(h)
    d_norm = parts_sum(parts)
    inner = jnp.mean(h * d_norm, axis=1, keepdims=True)
    grad = grad_ref[...].astype(f32) + r_in * d_norm - h * (r_in * r_in * r_in * inner)
    if not extra:
        refs[0][...] = grad
        return
    branch_ref, scale_ref, out_ref, sent_ref = refs
    out_ref[...] = grad
    low = grad.astype(bf)
    r_gate = scale_ref[...]
    column = jnp.sum(low.astype(f32) * branch_ref[...], axis=1, keepdims=True)
    row = jnp.broadcast_to(column, (TOK, 128)).T[:8]
    kappa = r_gate * r_gate * row / DI
    rows = in_parts(r_gate) + in_parts(kappa)
    rows = jnp.concatenate(rows + [jnp.zeros((8, D - 6 * TOK), f32)], axis=1)
    sent_ref[:TOK] = low
    sent_ref[TOK:] = jnp.concatenate([rows, jnp.zeros((8, D), f32)], axis=0).astype(bf)


def plain_call(kernel, name, shapes, args):
    return pl.pallas_call(
        kernel,
        out_shape=shapes,
        compiler_params=pltpu.CompilerParams(vmem_limit_bytes=SMALL_VMEM),
        cost_estimate=pl.CostEstimate(
            flops=int(2e8), bytes_accessed=int(1e6), transcendentals=0
        ),
        name=name,
    )(*args)


def to_owners(row):
    return a2a(row.reshape(NG, TOK), LINE)


def to_line(rows):
    m = rows.shape[0]
    return a2a(jnp.broadcast_to(rows[None], (NG,) + rows.shape), LINE).reshape(NG * m, GT)


def rounded(a):
    return lax.reduce_precision(a, exponent_bits=8, mantissa_bits=7)


def group_gather(block):
    return lax.all_gather(block, ZX, axis=0, tiled=True)


def group_gather_now(block):
    r, n = block.shape
    return a2a(jnp.broadcast_to(block[None], (NQ, r, n)), ZX).reshape(NQ * r, n)


def wait_for(value, *others):
    return lax.optimization_barrier((value, others))[0]


def group_reduce(full):
    r = full.shape[0] // NQ
    return jnp.sum(a2a(full.reshape(NQ, r, full.shape[1]), ZX).astype(f32), axis=0)


def heads_out(cols, width):
    r = cols.shape[0]
    return cols.reshape(r, 2, 2, 2, width).transpose(2, 3, 1, 0, 4).reshape(NG, r, width)


def heads_in(blocks):
    _, r, width = blocks.shape
    return blocks.reshape(2, 2, 2, r, width).transpose(3, 2, 0, 1, 4).reshape(r, NG * width)


def line_of(group):
    yl, yh, c = group // 4, (group // 2) % 2, group % 2
    return yh * 4 + c * 2 + yl


TO_HEADS = [(s, (s % NQ) * NG + line_of(s // NQ)) for s in range(NQ * NG)]
TO_OWNER = [(b, a) for a, b in TO_HEADS]


def in_blocks(weight, gain, extra):
    folded = (weight.astype(f32) * gain.astype(f32)[:, None]).astype(bf)
    z = heads_out(folded[:, :DI], W)
    x = heads_out(folded[:, DI : 2 * DI], W)
    bc = jnp.broadcast_to(folded[None, :, 2 * DI : 2 * DI + 2 * N], (NG, 12, 2 * N))
    step = heads_out(folded[:, 2 * DI + 2 * N :], HL)
    extra = jnp.broadcast_to(extra[None], (NG,) + extra.shape)
    step = jnp.concatenate([step, extra], axis=2)
    step = jnp.pad(step, ((0, 0), (0, 0), (0, 128 - step.shape[2])))
    return jnp.concatenate([x, bc, step, z], axis=2)


STATE_ROWS = W + 16


def line_scan_kernel(reverse, at_ref, own_ref, r1, r2, r3, sent_ref, before_ref, decay_ref):
    rank = 3 - at_ref[0] if reverse else at_ref[0]
    blocks = [read_states(ref) for ref in ((r3, r2, r1) if reverse else (r1, r2, r3))]
    own, own_decay = read_states(own_ref)
    state, decay = fold_before(rank, blocks)
    before_ref[...] = state
    decay_ref[...] = jnp.broadcast_to(decay, (8, 128))
    total = by_rows(own_decay, state) + own
    decay = decay * own_decay
    for i in (1, 2, 3):
        next_state, next_decay = blocks[3 - i]
        there = rank + i <= 3
        total = jnp.where(there, by_rows(next_decay, total) + next_state, total)
        decay = jnp.where(there, decay * next_decay, decay)
    write_states(sent_ref, total, decay)


def fold_before(rank, blocks):
    state = jnp.zeros((W, N), f32)
    decay = jnp.ones((1, 128), f32)
    for i in (3, 2, 1):
        block, block_decay = blocks[i - 1]
        there = rank >= i
        state = jnp.where(there, by_rows(block_decay, state) + block, state)
        decay = jnp.where(there, decay * block_decay, decay)
    return state, decay


def final_states(reverse, at_ref, r1, r2, r3, before_ref, decay_ref):
    rank = 3 - at_ref[0] if reverse else at_ref[0]
    blocks = [read_states(ref) for ref in ((r3, r2, r1) if reverse else (r1, r2, r3))]
    entering = fold_before(rank, blocks)[0]
    return by_rows(decay_ref[0:1], entering) + before_ref[...]


def exclusive_scan(sent, reverse, first, second):
    def around(a, axis):
        return [lax.ppermute(a, axis, [(i, (i + d) % 4) for i in range(4)]) for d in (1, 2, 3)]

    def index(axis):
        return lax.axis_index(axis).reshape(1).astype(jnp.int32)

    got = around(sent, "x")
    if first is not None:
        got[0] = wait_for(got[0], first)
    line, before, decay = pl.pallas_call(
        functools.partial(line_scan_kernel, reverse),
        out_shape=[SENT, struct((W, N)), struct((8, 128))],
        in_specs=[SMEM] + [pl.BlockSpec(memory_space=pltpu.VMEM)] * 4,
        out_specs=[pl.BlockSpec(memory_space=pltpu.VMEM)] * 3,
        name="line_scan",
    )(index("x"), sent, *got)
    got = around(line, "z")
    extra = second(line)
    got[0] = wait_for(got[0], extra)
    return (index("z"), *got, before, decay), extra


PAIRS = HL // 2
LAST = NS - 1


def dot(a, b, ca, cb, precision=None):
    return lax.dot_general(
        a, b, (((ca,), (cb,)), ((), ())), preferred_element_type=f32, precision=precision
    )


def by_lanes(cols):
    lane = lax.broadcasted_iota(jnp.int32, (cols.shape[0], 128), 1)
    return jnp.concatenate(
        [
            jnp.where(lane < HP, cols[:, 2 * p : 2 * p + 1], cols[:, 2 * p + 1 : 2 * p + 2])
            for p in range(PAIRS)
        ],
        axis=1,
    )


def by_rows(row, states):
    return jnp.concatenate(
        [row[:, h : h + 1] * states[h * HP : (h + 1) * HP] for h in range(HL)], axis=0
    )


def two_parts(a):
    hi = a.astype(bf)
    return hi, (a - hi.astype(f32)).astype(bf)


def head_sums(wide):
    column = lax.broadcasted_iota(jnp.int32, (W, 128), 0)
    lane = lax.broadcasted_iota(jnp.int32, (W, 128), 1)
    chosen = ((column >= lane * HP) & (column < lane * HP + HP)).astype(f32).astype(bf)
    hi, low = two_parts(wide)
    return dot(hi, chosen, 1, 0) + dot(low, chosen, 1, 0)


def token_sums(wide):
    ones = jnp.ones((8, wide.shape[1]), bf)
    hi, low = two_parts(wide)
    return dot(ones, hi, 1, 1) + dot(ones, low, 1, 1)


def running_sums(chosen, a):
    hi = a.astype(bf).astype(f32)
    mid = (a - hi).astype(bf).astype(f32)
    packed = hi + pltpu.roll(mid, 8, 1) + pltpu.roll(a - hi - mid, 16, 1)
    out = dot(chosen.astype(f32).astype(bf), packed.astype(bf), 1, 0)
    total = out + pltpu.roll(out, 128 - 8, 1) + pltpu.roll(out, 128 - 16, 1)
    lane = lax.broadcasted_iota(jnp.int32, (SPAN, 128), 1)
    return jnp.where(lane < HL, total, 0.0)


def write_states(sent_ref, states, decay):
    lane = lax.broadcasted_iota(jnp.int32, (8, 128), 1)
    decay = jnp.where(lane < HL, jnp.broadcast_to(decay, (8, 128)), 0.0)
    hi = decay.astype(bf).astype(f32)
    mid = (decay - hi).astype(bf).astype(f32)
    low = decay - hi - mid
    tail = hi + pltpu.roll(mid, HL, 1) + pltpu.roll(low, 2 * HL, 1)
    sent_ref[...] = jnp.concatenate([states, tail, tail], axis=0).astype(bf)


def read_states(ref):
    block = ref[...].astype(f32)
    tail = block[W : W + 8]
    decay = tail + pltpu.roll(tail, 128 - HL, 1) + pltpu.roll(tail, 128 - 2 * HL, 1)
    return block[:W], decay[:1]


def span_masks(segc_ref, segr_ref):
    row = lax.broadcasted_iota(jnp.int32, (SPAN, SPAN), 0)
    col = lax.broadcasted_iota(jnp.int32, (SPAN, SPAN), 1)
    return (col <= row) & (segc_ref[...] == segr_ref[0])


def head_decay(mask, run, run_t, h):
    return jnp.exp(jnp.where(mask, run[:, h : h + 1] - run_t[h : h + 1], -1e30))


def end_weights(run, segc_ref, seg_end):
    return jnp.exp(run[SPAN - 1 :] - run) * (segc_ref[...] == seg_end).astype(f32)


def inflow_of(run, segc_ref, seg_before):
    return jnp.exp(run) * (segc_ref[...] == seg_before).astype(f32)


def past_rows(k, u_ref, past_ref, edge_ref, rows_ref):
    rows_ref[:16] = jnp.where(k == 0, edge_ref[...].astype(f32), past_ref[...].astype(f32))
    rows_ref[16:] = u_ref[...].astype(f32)


def back_by(rows_ref, distance):
    return rows_ref[16 - distance : 16 - distance + SPAN]


def mix_kernel(
    seg_ref, u_ref, past_ref, edge_ref, same_ref, conv_ref, raw_ref, bias_ref, rate_ref, segc_ref,
    segr_ref, v_ref, pre_ref, within_ref, local_ref, step_ref, run_ref, before_ref, decay_ref, sent_ref, acc_ref, dec_ref, rows,
):
    k = pl.program_id(0)

    @pl.when(k == 0)
    def _():
        acc_ref[...] = jnp.zeros_like(acc_ref)
        dec_ref[...] = jnp.ones_like(dec_ref)

    past_rows(k, u_ref, past_ref, edge_ref, rows)
    pre = jnp.broadcast_to(conv_ref[CONV : CONV + 1], (SPAN, CC))
    for i in range(CONV):
        pre = pre + conv_ref[i : i + 1] * back_by(rows, i) * same_ref[:, i : i + 1]
    pre_ref[...] = pre.astype(bf)
    v_low = silu_both(pre)[0].astype(bf)
    v_ref[...] = v_low
    lane = lax.broadcasted_iota(jnp.int32, (SPAN, 128), 1)
    raw = raw_ref[...].astype(f32) + bias_ref[...]
    step = jnp.where(lane < HL, jax.nn.softplus(raw), 0.0)
    row = lax.broadcasted_iota(jnp.int32, (SPAN, SPAN), 0)
    col = lax.broadcasted_iota(jnp.int32, (SPAN, SPAN), 1)
    run = running_sums(col <= row, rate_ref[...] * step)
    step_ref[...] = step
    run_ref[...] = run
    run_t = run.T
    mask = span_masks(segc_ref, segr_ref)
    xc = v_low[:, :W].astype(f32)
    b_low = v_low[:, W : W + N]
    c_low = v_low[:, W + N :]
    gram = dot(c_low, b_low, 1, 1)
    xs = (by_lanes(step) * xc).astype(bf)
    half = lane < HP
    for p in range(PAIRS):
        cols = slice(p * 128, (p + 1) * 128)
        out = [
            dot((gram * head_decay(mask, run, run_t, h)).astype(bf), xs[:, cols], 1, 0)
            for h in (2 * p, 2 * p + 1)
        ]
        within_ref[:, cols] = jnp.where(half, out[0], out[1])
    w_end = end_weights(run, segc_ref, seg_ref[1, k])
    weighted = (by_lanes(w_end * step) * xc).astype(bf)
    own = dot(weighted, b_low, 0, 0)
    local_ref[0] = acc_ref[...]
    before_ref[0] = dec_ref[...]
    inside = (seg_ref[1, k] == seg_ref[0, k]).astype(f32)
    decay = jnp.exp(run[SPAN - 1 :]) * inside
    decay_ref[0] = decay
    acc = by_rows(decay, acc_ref[...]) + own
    acc_ref[...] = acc
    dec = dec_ref[...] * decay
    dec_ref[...] = dec

    @pl.when(k == LAST)
    def _():
        write_states(sent_ref, acc, dec)


def silu_both(v):
    s = 1.0 / (1.0 + jnp.exp(-v))
    return v * s, s * (1.0 + v * (1.0 - s))


def gate_kernel(
    last, order_ref, seg_ref, at_ref, r1, r2, r3, line_ref, line_decay_ref, local_ref, before_ref, run_ref, v_ref, within_ref, z_ref, segc_ref,
    skip_ref, wo_ref, *rest,
):
    if last:
        dq_ref, y0_ref, part_ref, sums_ref, carry_ref = rest
    else:
        y0_ref, other_ref, mine_ref, sums_ref, carry_ref = rest
    i = pl.program_id(0)
    k = order_ref[i]

    @pl.when(i == 0)
    def _():
        carry_ref[...] = final_states(False, at_ref, r1, r2, r3, line_ref, line_decay_ref)

    carried = (by_rows(before_ref[0], carry_ref[...]) + local_ref[0]).astype(bf)
    xc = v_ref[:, :W].astype(f32)
    c_low = v_ref[:, W + N :]
    reading = dot(c_low, carried, 1, 1)
    y0 = within_ref[...] + by_lanes(inflow_of(run_ref[...], segc_ref, seg_ref[0, k])) * reading
    y0_ref[...] = y0
    mixed = (y0 + skip_ref[...] * xc).astype(bf).astype(f32)
    gated = mixed * silu_both(z_ref[...].astype(f32))[0]
    part = dot(gated.astype(bf), wo_ref[...], 1, 0).astype(bf)
    if last:
        part_ref[...] = part
    else:
        write_half(other_ref, mine_ref, part)
    sums = token_sums(gated * gated)
    if last:
        row = lax.broadcasted_iota(jnp.int32, (8, SPAN), 0)
        sums = jnp.where(row < 1, sums, token_sums(gated * dq_ref[...]))
    sums_ref[...] = sums


def gate_back_kernel(
    last, seg_ref, grad_ref, wo_ref, scale_ref, v_ref, y0_ref, z_ref, run_ref, segc_ref, skip_ref,
    decay_ref, dy_ref, dz_ref, gr_ref, local_ref, after_ref, sent_ref, acc_ref, dec_ref,
):
    i = pl.program_id(0)
    k = LAST - i

    @pl.when(i == 0)
    def _():
        acc_ref[...] = jnp.zeros_like(acc_ref)
        dec_ref[...] = jnp.ones_like(dec_ref)

    if last:
        sums = scale_ref[...]
        odd = lax.broadcasted_iota(jnp.int32, (2 * NG, SPAN), 0) % 2 == 1
        square = jnp.sum(jnp.where(odd, 0.0, sums), axis=0, keepdims=True)
        inner = jnp.sum(jnp.where(odd, sums, 0.0), axis=0, keepdims=True)
        r_row = lax.rsqrt(square / DI + EPS)
        k_row = r_row * r_row * r_row * inner / DI
    else:
        rows = scale_ref[...].astype(f32)
        pieces = [rows[:, i * TOK : (i + 1) * TOK] for i in range(6)]
        r_two = pieces[0] + pieces[1] + pieces[2]
        k_two = pieces[3] + pieces[4] + pieces[5]
        r_row = jnp.concatenate([r_two[0:1], r_two[16:17]], axis=1)
        k_row = jnp.concatenate([k_two[0:1], k_two[16:17]], axis=1)
    r = jnp.broadcast_to(r_row, (8, SPAN)).T[:, 0:1]
    kappa = jnp.broadcast_to(k_row, (8, SPAN)).T[:, 0:1]
    d_q = grad_ref[...] if last else dot(grad_ref[...], wo_ref[...], 1, 1)
    mixed = (y0_ref[...] + skip_ref[...] * v_ref[:, :W].astype(f32)).astype(bf).astype(f32)
    silu, d_silu = silu_both(z_ref[...].astype(f32))
    gated = mixed * silu
    gr_ref[...] = (r * gated).astype(bf)
    d_gated = r * d_q - kappa * gated
    dy = (d_gated * silu).astype(bf)
    dy_ref[...] = dy
    dz_ref[...] = (d_gated * mixed * d_silu).astype(bf)
    inflow = by_lanes(inflow_of(run_ref[...], segc_ref, seg_ref[0, k]))
    scaled = (inflow * dy.astype(f32)).astype(bf)
    d_carried = dot(scaled, v_ref[:, W + N :], 0, 0)
    local_ref[0] = acc_ref[...]
    after_ref[0] = dec_ref[...]
    decay = decay_ref[0]
    acc = by_rows(decay, acc_ref[...]) + d_carried
    acc_ref[...] = acc
    dec = dec_ref[...] * decay
    dec_ref[...] = dec

    @pl.when(i == LAST)
    def _():
        write_states(sent_ref, acc, dec)


def mix_back_kernel(v_ref, step_ref, run_ref, segc_ref, segr_ref, dy_ref, dxs_ref, dbc_ref):
    lane = lax.broadcasted_iota(jnp.int32, (SPAN, 128), 1)
    half = lane < HP
    run = run_ref[...]
    run_t = run.T
    mask = span_masks(segc_ref, segr_ref)
    xs = (by_lanes(step_ref[...]) * v_ref[:, :W].astype(f32)).astype(bf)
    b_low = v_ref[:, W : W + N]
    c_low = v_ref[:, W + N :]
    gram = dot(c_low, b_low, 1, 1)
    d_gram = jnp.zeros((SPAN, SPAN), f32)
    zero = jnp.zeros((SPAN, 128), bf)
    for p in range(PAIRS):
        cols = slice(p * 128, (p + 1) * 128)
        dy = dy_ref[:, cols]
        out = []
        for i, h in enumerate((2 * p, 2 * p + 1)):
            decay = head_decay(mask, run, run_t, h)
            mixing = (gram * decay).astype(bf)
            dy_one = jnp.where(half, dy, zero) if i == 0 else jnp.where(half, zero, dy)
            d_gram = d_gram + dot(dy_one, xs[:, cols], 1, 1) * decay
            out.append(dot(mixing, dy, 0, 0))
        dxs_ref[:, cols] = jnp.where(half, out[0], out[1])
    d_gram = d_gram.astype(bf)
    dbc_ref[:, :N] = dot(d_gram, c_low, 0, 0).astype(bf)
    dbc_ref[:, N:] = dot(d_gram, b_low, 1, 0).astype(bf)


def end_kernel(
    seg_ref, at_ref, r1, r2, r3, line_ref, line_decay_ref, carry_ref, local_ref, before_ref, dlocal_ref, after_ref, decay_ref, v_ref,
    pre_ref, raw_ref, bias_ref, rate_ref, step_ref, run_ref, segc_ref, skip_ref, dy_ref, dxs_ref,
    dbc_ref, y0_ref, dpre_ref, draw_ref, sums_ref, later_s,
):
    k = pl.program_id(0)

    @pl.when(k == 0)
    def _():
        later_s[...] = final_states(True, at_ref, r1, r2, r3, line_ref, line_decay_ref)
        sums_ref[...] = jnp.zeros_like(sums_ref)

    d_end = by_rows(after_ref[0], later_s[...]) + dlocal_ref[0]
    carried = by_rows(before_ref[0], carry_ref[...]) + local_ref[0]
    d_end_low = d_end.astype(bf)
    run, step, rate = run_ref[...], step_ref[...], rate_ref[...]
    xc = v_ref[:, :W].astype(f32)
    b_low = v_ref[:, W : W + N]
    dy = dy_ref[...].astype(f32)
    dxs = dxs_ref[...]
    step_x = by_lanes(step)
    xs = (step_x * xc).astype(bf).astype(f32)
    w_end = end_weights(run, segc_ref, seg_ref[1, k])
    weights_x = by_lanes(w_end * step)
    weighted = (weights_x * xc).astype(bf)
    scaled = (by_lanes(inflow_of(run, segc_ref, seg_ref[0, k])) * dy).astype(bf)
    d_weighted = dot(b_low, d_end_low, 1, 1)
    d_b = dbc_ref[:, :N].astype(f32) + dot(weighted, d_end_low, 1, 0)
    d_c = dbc_ref[:, N:].astype(f32) + dot(scaled, carried.astype(bf), 1, 0)
    d_xc = skip_ref[...] * dy + step_x * dxs + weights_x * d_weighted
    dv = jnp.concatenate([d_xc, d_b, d_c], axis=1)
    dpre_ref[...] = (dv * silu_both(pre_ref[...].astype(f32))[1]).astype(bf)
    skip_sum = head_sums(dy * xc)
    d_run = head_sums(dy * y0_ref[...] - xs * dxs)
    d_step = head_sums(xc * dxs)
    d_w = head_sums(d_weighted * xc)
    product = d_end * carried
    lane1 = lax.broadcasted_iota(jnp.int32, (1, 128), 1)
    d_span = jnp.zeros((1, 128), f32)
    for h in range(HL):
        rows = jnp.sum(product[h * HP : (h + 1) * HP], axis=0, keepdims=True)
        d_span = d_span + jnp.where(lane1 == h, jnp.sum(rows, axis=1, keepdims=True), 0.0)
    d_step = d_step + d_w * w_end
    d_ww = d_w * w_end * step
    d_run = d_run - d_ww
    d_last = jnp.sum(d_ww, axis=0, keepdims=True) + d_span * decay_ref[0]
    row = lax.broadcasted_iota(jnp.int32, (SPAN, SPAN), 0)
    col = lax.broadcasted_iota(jnp.int32, (SPAN, SPAN), 1)
    d_a = running_sums(col >= row, d_run) + d_last
    d_step = d_step + rate * d_a
    raw = raw_ref[...].astype(f32) + bias_ref[...]
    lane = lax.broadcasted_iota(jnp.int32, (SPAN, 128), 1)
    d_raw = jnp.where(lane < HL, d_step / (1.0 + jnp.exp(-raw)), 0.0)
    draw_ref[...] = d_raw.astype(bf)
    sums = jnp.concatenate(
        [
            jnp.sum(d_raw, axis=0, keepdims=True),
            rate * jnp.sum(step * d_a, axis=0, keepdims=True),
            jnp.sum(skip_sum, axis=0, keepdims=True),
            jnp.zeros((5, 128), f32),
        ],
        axis=0,
    )
    sums_ref[...] = sums_ref[...] + sums


def conv_back_kernel(
    first, order_ref, dpre_ref, next_ref, after_ref, u_ref, past_ref, edge_ref, same_ref, conv_ref, draw_ref, dz_ref,
    wa_ref, wz_ref, da_ref, *outs,
):
    *outs, taps_ref, rows, d_rows = outs
    i = pl.program_id(0)
    k = order_ref[i]

    @pl.when(i == 0)
    def _():
        taps_ref[...] = jnp.zeros_like(taps_ref)

    d_pre = dpre_ref[...].astype(f32)
    d_rows[:SPAN] = d_pre
    d_rows[SPAN:] = jnp.where(
        k == LAST, after_ref[...].astype(f32), next_ref[...].astype(f32)
    )
    past_rows(k, u_ref, past_ref, edge_ref, rows)
    du = jnp.zeros((SPAN, CC), f32)
    taps = []
    for tap in range(CONV):
        ahead = d_rows[tap : tap + SPAN]
        same = same_ref[:, CONV + tap : CONV + tap + 1]
        du = du + conv_ref[tap : tap + 1] * ahead * same
        product = d_pre * back_by(rows, tap) * same_ref[:, tap : tap + 1]
        taps.append(jnp.sum(product, axis=0, keepdims=True))
    taps.append(jnp.sum(d_pre, axis=0, keepdims=True))
    taps.append(jnp.zeros((3, CC), f32))
    taps_ref[...] = taps_ref[...] + jnp.concatenate(taps, axis=0)
    da = jnp.concatenate([du.astype(bf), draw_ref[...]], axis=1)
    da_ref[...] = da
    part = dot(da, wa_ref[...], 1, 1) + dot(dz_ref[...], wz_ref[...], 1, 1)
    if first:
        outs[0][...] = part.astype(bf)
    else:
        write_half(*outs[:2], part.astype(bf))


def tok_block(n, reverse=False):
    return pl.BlockSpec((SPAN, n), lambda k: (LAST - k if reverse else k, 0))


def span_block(rows, n, reverse=False):
    return pl.BlockSpec((1, rows, n), lambda k: (LAST - k if reverse else k, 0, 0))


def whole(*shape):
    return pl.BlockSpec(shape, lambda k: (0,) * len(shape))


STATE = struct((NS, W, N))
ROW = struct((NS, 1, 128))
SENT = struct((STATE_ROWS, N), bf)
STATE_SCRATCH = pltpu.VMEM((W, N), f32)


def call(kernel, name, ins, outs, shapes, scratch, args, us, vmem=VMEM_BYTES):
    return pl.pallas_call(
        kernel,
        grid=(NS,),
        in_specs=ins,
        out_specs=outs,
        out_shape=shapes,
        scratch_shapes=scratch,
        compiler_params=pltpu.CompilerParams(
            dimension_semantics=("arbitrary",), vmem_limit_bytes=vmem
        ),
        cost_estimate=pl.CostEstimate(
            flops=int(us * 4e7), bytes_accessed=int(us * 2e5), transcendentals=0
        ),
        name=name,
    )(*args)


def ordered_call(kernel, name, ins, outs, shapes, scratch, args, us):
    return pl.pallas_call(
        kernel,
        grid_spec=pltpu.PrefetchScalarGridSpec(
            num_scalar_prefetch=1, grid=(NS,), in_specs=ins, out_specs=outs, scratch_shapes=scratch
        ),
        out_shape=shapes,
        compiler_params=pltpu.CompilerParams(
            dimension_semantics=("arbitrary",), vmem_limit_bytes=VMEM_BYTES
        ),
        cost_estimate=pl.CostEstimate(
            flops=int(us * 4e7), bytes_accessed=int(us * 2e5), transcendentals=0
        ),
        name=name,
    )(span_order(), *args)


def tok_at(n):
    return pl.BlockSpec((SPAN, n), lambda i, order: (order[i], 0))


def span_at(rows, n):
    return pl.BlockSpec((1, rows, n), lambda i, order: (order[i], 0, 0))


def whole_at(*shape):
    return pl.BlockSpec(shape, lambda i, order: (0,) * len(shape))


HALVES = [
    pl.BlockSpec((SPAN, D), lambda i, order: (jnp.minimum(i, 1), 0)),
    pl.BlockSpec((SPAN, D), lambda i, order: (jnp.maximum(i - 2, 0), 0)),
]
HALF_SHAPES = [struct((GT // 2, D), bf)] * 2


def past_block(n):
    return pl.BlockSpec((16, n), lambda k: (jnp.maximum(k * (SPAN // 16) - 1, 0), 0))


def span_mix(seg, u, edge, same, conv, raw, bias, rate, segc, segr):
    return call(
        mix_kernel,
        "span_mix",
        [SMEM, tok_block(CC), past_block(CC), whole(16, CC), tok_block(8), whole(8, CC),
         tok_block(128), whole(1, 128), whole(1, 128), tok_block(1), span_block(1, SPAN)],
        [tok_block(CC), tok_block(CC), tok_block(W), span_block(W, N), tok_block(128),
         tok_block(128), span_block(1, 128), span_block(1, 128), whole(STATE_ROWS, N)],
        [struct((GT, CC), bf), struct((GT, CC), bf), struct((GT, W)), STATE, struct((GT, 128)),
         struct((GT, 128)), ROW, ROW, SENT],
        [STATE_SCRATCH, pltpu.VMEM((1, 128), f32), pltpu.VMEM((SPAN + 16, CC), f32)],
        (seg, u, u, edge, same, conv, raw, bias, rate, segc, segr),
        10,
    )


def conv_back(first, d_pre, after, u, edge, same, conv, d_raw, dz, wa, wz, at):
    following = pl.BlockSpec(
        (16, CC), lambda i, order: (jnp.minimum((order[i] + 1) * (SPAN // 16), GT // 16 - 1), 0)
    )
    past = pl.BlockSpec(
        (16, CC), lambda i, order: (jnp.maximum(order[i] * (SPAN // 16) - 1, 0), 0)
    )
    return ordered_call(
        functools.partial(conv_back_kernel, first),
        "conv_back",
        [tok_at(CC), following, whole_at(16, CC), tok_at(CC), past, whole_at(16, CC), tok_at(8),
         whole_at(8, CC), tok_at(128), tok_at(W), whole_at(D, CA),
         pl.BlockSpec((D, W), lambda i, order: (0, at))],
        [tok_at(CA)] + ([tok_at(D)] if first else HALVES) + [whole_at(8, CC)],
        [struct((GT, CA), bf)] + ([struct((GT, D), bf)] if first else HALF_SHAPES)
        + [struct((8, CC))],
        [pltpu.VMEM((SPAN + 16, CC), f32)] * 2,
        (d_pre, d_pre, after, u, u, edge, same, conv, d_raw, dz, wa, wz),
        10,
    )


def span_gate(seg, back, local, before, run, v, within, z, segc, skip, wo, d_q):
    last = d_q is not None
    ins = [SMEM, SMEM] + [whole_at(STATE_ROWS, N)] * 3 + [
           whole_at(W, N), whole_at(8, 128), span_at(W, N), span_at(1, 128), tok_at(128), tok_at(CC),
           tok_at(W), tok_at(W), tok_at(1), whole_at(1, W), whole_at(W, D)]
    args = (seg, *back, local, before, run, v, within, z, segc, skip, wo)
    return ordered_call(
        functools.partial(gate_kernel, last),
        "span_gate",
        ins + [tok_at(W)] if last else ins,
        [tok_at(W)] + ([tok_at(D)] if last else HALVES)
        + [pl.BlockSpec((8, SPAN), lambda i, order: (0, order[i])), whole_at(W, N)],
        [struct((GT, W))] + ([struct((GT, D), bf)] if last else HALF_SHAPES)
        + [struct((8, GT)), struct((W, N))],
        [],
        args + (d_q,) if last else args,
        10,
    )


def span_gate_back(last, seg, grad, wo, scales, v, y0, z, run, segc, skip, decay):
    if last:
        scale_block = pl.BlockSpec((2 * NG, SPAN), lambda k: (0, LAST - k))
    else:
        scale_block = pl.BlockSpec((32, D), lambda k: (LAST - k, 0))
    return call(
        functools.partial(gate_back_kernel, last),
        "span_gate_back",
        [SMEM, tok_block(W if last else D, True), whole(W, D), scale_block,
         tok_block(CC, True), tok_block(W, True), tok_block(W, True), tok_block(128, True),
         tok_block(1, True), whole(1, W), span_block(1, 128, True)],
        [tok_block(W, True), tok_block(W, True), tok_block(W, True), span_block(W, N, True),
         span_block(1, 128, True), whole(STATE_ROWS, N)],
        [struct((GT, W), bf), struct((GT, W), bf), struct((GT, W), bf), STATE, ROW, SENT],
        [STATE_SCRATCH, pltpu.VMEM((1, 128), f32)],
        (seg, grad, wo, scales, v, y0, z, run, segc, skip, decay),
        12,
    )


def span_mix_back(v, step, run, segc, segr, dy):
    return call(
        mix_back_kernel,
        "span_mix_back",
        [tok_block(CC), tok_block(128), tok_block(128), tok_block(1), span_block(1, SPAN),
         tok_block(W)],
        [tok_block(W), tok_block(2 * N)],
        [struct((GT, W)), struct((GT, 2 * N), bf)],
        [],
        (v, step, run, segc, segr, dy),
        14,
    )


def span_end(seg, later, back, local, before, dlocal, after, decay, v, pre, raw, bias, rate, step,
             run, segc, skip, dy, dxs, dbc, y0):
    return call(
        end_kernel,
        "span_end",
        [SMEM, SMEM] + [whole(STATE_ROWS, N)] * 3 + [
         whole(W, N), whole(8, 128), whole(W, N), span_block(W, N), span_block(1, 128),
         span_block(W, N), span_block(1, 128), span_block(1, 128), tok_block(CC), tok_block(CC),
         tok_block(128), whole(1, 128), whole(1, 128), tok_block(128), tok_block(128),
         tok_block(1), whole(1, W), tok_block(W), tok_block(W), tok_block(2 * N), tok_block(W)],
        [tok_block(CC), tok_block(128), whole(8, 128)],
        [struct((GT, CC), bf), struct((GT, 128), bf), struct((8, 128))],
        [STATE_SCRATCH],
        (seg, *later, back, local, before, dlocal, after, decay, v, pre, raw, bias, rate, step, run,
         segc, skip, dy, dxs, dbc, y0),
        16,
    )


def group_reduce_blocks(sent):
    return jnp.sum(a2a(sent, ZX).astype(f32), axis=0)


SMALL = CC + HL


def small_block(conv_grads, head_grads):
    own_ch = CH // (NQ * NG)
    conv = jnp.stack(conv_grads).reshape(LAYERS * (CONV + 1), NQ * NG, own_ch)
    conv = jnp.pad(conv.transpose(1, 0, 2), ((0, 0), (0, 12 - LAYERS * (CONV + 1)), (0, 0)))
    head = jnp.stack(head_grads, axis=1)
    high = rounded(head)
    head = jnp.concatenate([high, head - high], axis=1)
    head = jnp.tile(head, (NQ * NG // 2, 1, 1))
    head = jnp.pad(head, ((0, 0), (0, 12 - 2 * LAYERS), (0, 0)))
    block = jnp.concatenate([conv, head], axis=2).reshape(D, own_ch + 3 * H // 2)
    return jnp.pad(block.astype(bf), ((0, 0), (SMALL, CA - SMALL - block.shape[1])))


def per_device(
    tokens,
    doc_starts,
    norm_gain,
    in_weight,
    conv_weight,
    conv_bias,
    step_bias,
    decay_log,
    skip_gain,
    gate_gain,
    out_weight,
    cotangent,
):
    q = lax.axis_index(ZX)
    yh, core, yl = lax.axis_index("yh"), lax.axis_index("c"), lax.axis_index("yl")
    sub = yh * 2 + core
    group = yl * 4 + sub

    own_ch = CH // (NQ * NG)
    conv_own = jnp.concatenate([conv_weight, conv_bias[:, None]], axis=1).reshape(-1, own_ch)
    conv_own = jnp.pad(conv_own, ((0, 12 - conv_own.shape[0]), (0, 0)))
    sent = [in_blocks(in_weight[l], norm_gain[l], conv_own if l == 0 else conv_own[:, :0]) for l in range(LAYERS)]
    sent = jnp.stack(sent, axis=1)
    got = a2a(sent, LINE)
    in_0 = got[:, 0].reshape(NG * 12, CA + W)
    in_1 = got[:, 1].reshape(NG * 12, CA + W)
    own_0 = jnp.broadcast_to(in_0[None, :, :CA], (NQ, NG * 12, CA))
    w_a0 = a2a(own_0, ZX).reshape(D, CA)
    h = tokens.astype(f32)
    normed = (h * lax.rsqrt(jnp.mean(h * h, axis=-1, keepdims=True) + EPS)).astype(bf)
    pos = q * GT + jnp.arange(-(CONV - 1), GT + CONV - 1, dtype=jnp.int32)
    seg_ext = jnp.sum((doc_starts[None, :] <= pos[:, None]).astype(jnp.int32), axis=1) - 1
    seg = seg_ext[CONV - 1 : CONV - 1 + GT]
    seg_spans = seg.reshape(NS, SPAN)
    seg_before = seg_ext[CONV - 2 : CONV - 2 + GT : SPAN]
    seg_ends = jnp.stack([seg_before, seg_spans[:, -1]])
    seg_col, seg_row = seg[:, None], seg_spans[:, None, :]
    same = jnp.stack(
        [seg_ext[CONV - 1 - k : CONV - 1 - k + GT] == seg for k in range(CONV)]
        + [seg_ext[CONV - 1 + k : CONV - 1 + k + GT] == seg for k in range(CONV)],
        axis=1,
    ).astype(f32)

    def pick_heads(a):
        own = lax.dynamic_slice_in_dim(a, sub * HL, HL, 0)
        return jnp.pad(own, (0, 128 - HL))[None]

    onward = [(i, i + 1) for i in range(NQ - 1)]
    consts = []
    for l in range(LAYERS):
        rate = jnp.where(jnp.arange(128)[None] < HL, -jnp.exp(pick_heads(decay_log[l])), 0.0)
        skip_x = jnp.repeat(lax.dynamic_slice_in_dim(skip_gain[l], sub * HL, HL, 0), HP)[None]
        consts.append((pick_heads(step_bias[l]), rate, skip_x))
    prepared = own_0, consts, same, seg_ends, seg_col, seg_row, span_order()
    places, blocks = line_blocks(wait_for(normed, got), prepared)
    folded_out = (out_weight.astype(f32) * gate_gain.astype(f32)[:, :, None]).astype(bf)
    out_blocks = lax.ppermute(folded_out, AX, TO_HEADS)
    zo = jnp.concatenate([in_0[:, CA:], out_blocks.reshape(192, W)], axis=0)
    grad_full = lax.all_gather(cotangent, LINE, axis=0, tiled=True)
    w_a0 = wait_for(w_a0, zo)
    normed, u, raw = place_project(places, blocks, w_a0)
    tail = u[GT - 16 :]
    conv_all = wait_for(w_a0, tail)[:, SMALL : SMALL + own_ch].reshape(NQ * NG, 12, own_ch)
    conv_all = conv_all[:, : LAYERS * (CONV + 1)].transpose(1, 0, 2)
    conv_all = conv_all.reshape(LAYERS, CONV + 1, CH).astype(f32)
    conv_x = lax.dynamic_slice_in_dim(conv_all, group * W, W, 2)
    conv_here = jnp.concatenate([conv_x, conv_all[:, :, DI:]], axis=2)
    conv_here = jnp.pad(conv_here, ((0, 0), (0, 7 - CONV), (0, 0)))
    zo = group_gather(wait_for(zo, w_a0, blocks)).reshape(NQ, 288, W)
    w_z0 = zo[:, :96].reshape(D, W)
    w_o = [zo[:, 96:192].reshape(W, D), None]
    w_in1 = group_gather(wait_for(in_1, tail))
    saved = []
    for l in range(LAYERS):
        bias_h, rate, skip_x = consts[l]
        if l > 0:
            normed, u, raw = line_project(normed, w_in1)
        edge = lax.ppermute(u[GT - 16 :], ZX, onward)
        v, pre, within, local, step, run, before, decay, sent = span_mix(
            seg_ends, u, edge, same, conv_here[l], raw, bias_h, rate, seg_col, seg_row
        )
        if l == 0:
            w_o[1] = wait_for(zo, v)[:, 192:].reshape(W, D)
            d_q = None
            back, z = exclusive_scan(
                sent, False, None, lambda outs: mm(wait_for(normed, outs), w_z0).astype(bf)
            )
        else:
            z = mm(normed, w_in1[:, CA:]).astype(bf)
            back, d_q = exclusive_scan(
                sent, False, z, lambda outs: mm(wait_for(grad_full, outs), w_o[1], 1, 1)
            )
        y0, *parts, sums, carry = span_gate(
            seg_ends, back, local, before, run, v, within, z, seg_col, skip_x, w_o[l],
            d_q,
        )
        saved.append(
            dict(
                h=h, normed=normed, u=u, edge=edge, pre=pre, v=v, z=z, raw=raw, bias_h=bias_h,
                rate=rate, skip_x=skip_x, step=step, run=run, before=before, decay=decay,
                local=local, carry=carry, y0=y0,
            )
        )
        if l < LAYERS - 1:
            parts = line_parts(*parts)
            square = wait_for(to_owners(sums[0]), *parts[1:])
            h, branch, normed, r_gate = plain_call(
                advance_kernel,
                "advance",
                [struct((TOK, D)), struct((TOK, D)), struct((TOK, D), bf), struct((8, TOK))],
                (*parts, square, h),
            )
        else:
            scales = to_line(sums[:2])
            at = (line_index() // 2 * 4 + core * 2 + yl) * TOK
            square = lax.dynamic_slice_in_dim(scales, at, TOK, 1)
            square = jnp.sum(square.reshape(NG, 2, TOK)[:, 0], axis=0)
            r_last = lax.rsqrt(square / DI + EPS)[:, None]
            total = lax.psum_scatter(parts[0], LINE, scatter_dimension=0, tiled=True)
            output = (h + total.astype(f32) * r_last).astype(bf)

    grad = cotangent
    conv_grads, head_grads = [None] * LAYERS, [None] * LAYERS
    a_sums, z_sums, out_sums = ([None] * LAYERS for _ in range(3))
    for l in reversed(range(LAYERS)):
        s = saved[l]
        dy, dz, gr, dlocal, after, sent = span_gate_back(
            l == LAYERS - 1, seg_ends, d_q if l else grad_full, w_o[l], scales, s["v"], s["y0"], s["z"], s["run"],
            seg_col, s["skip_x"], s["decay"],
        )
        z_part = mm(s["normed"], dz, 0, 0).astype(bf).reshape(NQ, 96, W)

        def out_blocks_of(outs):
            low = wait_for(gr, outs)
            return [
                mm(low, grad_full[:, i * W : (i + 1) * W], 0, 0).astype(bf).reshape(NQ, 24, W)
                for i in range(D // W)
            ]

        later, out_part = exclusive_scan(sent, True, z_part, out_blocks_of)
        sums = jnp.concatenate([z_part, *out_part], axis=1)
        both = group_reduce_blocks(wait_for(sums, later))
        dxs, dbc = span_mix_back(s["v"], s["step"], s["run"], seg_col, seg_row, wait_for(dy, sums))
        d_pre, d_raw, head_sum = span_end(
            seg_ends, later, s["carry"], s["local"], s["before"], dlocal, after, s["decay"], s["v"],
            s["pre"], s["raw"], s["bias_h"], s["rate"], s["step"], s["run"], seg_col, s["skip_x"],
            dy, dxs, dbc, s["y0"],
        )
        following = lax.ppermute(d_pre[:16], ZX, [(b, a) for a, b in onward])
        z_sums[l] = both[:96]
        out_sums[l] = both[96:].reshape(4, 24, W).transpose(1, 0, 2).reshape(24, D)
        if l == LAYERS - 1:
            w_a, w_z, at = w_in1, w_in1, CA // W
        else:
            w_a, w_z, at = w_a0, w_z0, 0
        da, *parts, taps = conv_back(
            False, d_pre, following, s["u"], s["edge"], same, conv_here[l], d_raw, dz, w_a, w_z, at
        )
        conv_full = jnp.zeros((CONV + 1, CH), f32)
        conv_full = lax.dynamic_update_slice_in_dim(
            conv_full, taps[: CONV + 1, :W], group * W, 1
        )
        conv_grads[l] = conv_full.at[:, DI:].set(taps[: CONV + 1, W:])
        head_full = lax.dynamic_update_slice_in_dim(
            jnp.zeros((3, H), f32), head_sum[:3, :HL], group * HL, 1
        )
        head_grads[l] = head_full.reshape(3, 2, H // 2).transpose(1, 0, 2).reshape(2, 3 * H // 2)
        a_part = mm(s["normed"], da, 0, 0)
        if l == 0:
            a_part = a_part + small_block(conv_grads, head_grads).astype(f32)
        a_part = a_part.astype(bf)
        if l == 0:
            parts = line_parts(*parts, a_part)
            a_sums[l] = group_reduce(a_part)
        else:
            parts = line_parts(*parts, output)
            a_sums[l] = group_reduce(wait_for(a_part, parts[0]))
        if l > 0:
            grad, block = plain_call(
                functools.partial(retreat_kernel, True),
                "retreat",
                [struct((TOK, D)), struct((TOK + 16, D), bf)],
                (*parts, s["h"], grad, branch, r_gate),
            )
            early = jnp.concatenate([a_sums[1], z_sums[1]], axis=1).reshape(NG, 12, CA + W)
            grad_full, scales = line_gather_more(block, early)
            early = a2a(early, LINE)
            scales = wait_for(scales, early)
        else:
            grad = plain_call(
                functools.partial(retreat_kernel, False),
                "retreat_last",
                struct((TOK, D)),
                (*parts, s["h"], grad),
            )

    out_sums = [
        lax.ppermute(wait_for(out_sums[l], a_part if l else a_sums[0]), AX, TO_OWNER)
        for l in range(LAYERS)
    ]
    late = jnp.concatenate([a_sums[0], z_sums[0]], axis=1)
    late = a2a(late.reshape(NG, 12, CA + W).astype(bf), LINE).astype(f32)
    small = jnp.sum(late[:, :, SMALL:CA], axis=0)
    in_grads, gain_grads, out_grads, gate_grads = ([None] * LAYERS for _ in range(4))
    for l in range(LAYERS):
        got = (late, early)[l]
        a_piece, z_piece = got[:, :, :CA], got[:, :, CA:]
        g_in = jnp.concatenate(
            [
                heads_in(z_piece),
                heads_in(a_piece[:, :, :W]),
                jnp.sum(a_piece[:, :, W:CC], axis=0),
                heads_in(a_piece[:, :, CC : CC + HL]),
            ],
            axis=1,
        )
        in_grads[l] = g_in * norm_gain[l].astype(f32)[:, None]
        gain_grads[l] = jnp.sum(g_in * in_weight[l].astype(f32), axis=1)
        g_out = out_sums[l]
        out_grads[l] = g_out * gate_gain[l].astype(f32)[:, None]
        gate_grads[l] = jnp.sum(g_out * out_weight[l].astype(f32), axis=1)

    conv_grad = small[: LAYERS * (CONV + 1), :own_ch].reshape(LAYERS, CONV + 1, own_ch)
    head_grad = small[:LAYERS] + small[LAYERS : 2 * LAYERS]
    head_grad = head_grad[:, own_ch : own_ch + 3 * H // 2].reshape(LAYERS, 3, H // 2)
    return (
        output,
        grad,
        jnp.stack(gain_grads),
        jnp.stack(in_grads),
        conv_grad[:, :CONV],
        conv_grad[:, CONV],
        head_grad[:, 0],
        head_grad[:, 1],
        head_grad[:, 2],
        jnp.stack(gate_grads),
        jnp.stack(out_grads),
    )


def solution(mesh):
    fine = Mesh(mesh.devices.reshape(4, 4, 2, 2, 2), AX)
    tok, last, mid, heads = P(AX, None), P(None, AX), P(None, AX, None), P(None, "yl")
    conv = P(None, None, AX)
    return jax.shard_map(
        per_device,
        mesh=fine,
        in_specs=(tok, P(), last, mid, conv, last, heads, heads, heads, last, mid, tok),
        out_specs=(tok, tok, last, mid, conv, last, heads, heads, heads, last, mid),
        check_vma=False,
    )
```
